32 devices in a mesh: dp: 32 (over z, y, x, core).
Axes of the slice: x: 2, y: 2, z: 4, core: 2. Of those that a mesh axis runs over, the one named last changes fastest.
Arguments:
- embeds: bfloat16 [8192, 8, 512], P('dp'), may hold values from -6 to 6
- piece_counts: int32 [8192], P('dp'), may hold values from 1 to 8
- group_ids: int32 [8192], P('dp'), may hold values from 0 to 7
- group_table: bfloat16 [8, 512], P(None, 'dp'), may hold values from -3 to 3
- gain_attn: bfloat16 [512], P('dp'), may hold values from 0.5 to 1.5
- shift_attn: bfloat16 [512], P('dp'), may hold values from -2 to 2
- w_qkv: bfloat16 [512, 1536], P('dp'), may hold values from -0.25 to 0.25
- w_out: bfloat16 [512, 512], P('dp'), may hold values from -0.375 to 0.375
- gain_ffn: bfloat16 [512], P('dp'), may hold values from 0.5 to 1.5
- shift_ffn: bfloat16 [512], P('dp'), may hold values from -2 to 2
- w_up: bfloat16 [512, 2048], P('dp'), may hold values from -0.25 to 0.25
- bias_up: bfloat16 [2048], P('dp'), may hold values from -2 to 2
- w_down: bfloat16 [2048, 512], P('dp'), may hold values from -0.1875 to 0.1875
- bias_down: bfloat16 [512], P('dp'), may hold values from -2 to 2
- w_proj: bfloat16 [512, 2048], P('dp'), may hold values from -0.25 to 0.25
- cotangent: bfloat16 [8192, 2048], P('dp'), may hold values from -6 to 6
Outputs:
- output: bfloat16 [8192, 2048], P('dp')
- grad_embeds: bfloat16 [8192, 8, 512], P('dp')
- grad_table: float32 [8, 512], P(None, 'dp')
- grad_gain_attn: float32 [512], P('dp')
- grad_shift_attn: float32 [512], P('dp')
- grad_qkv: float32 [512, 1536], P('dp')
- grad_out: float32 [512, 512], P('dp')
- grad_gain_ffn: float32 [512], P('dp')
- grad_shift_ffn: float32 [512], P('dp')
- grad_up: float32 [512, 2048], P('dp')
- grad_bias_up: float32 [2048], P('dp')
- grad_down: float32 [2048, 512], P('dp')
- grad_bias_down: float32 [512], P('dp')
- grad_proj: float32 [512, 2048], P('dp')
The draws below stay inside these ranges and needn't reach their ends.
Inputs may be any that keep to these rules, and one draw needn't show every extreme that they name: An entry's slots from piece_counts on are padding.
All inputs are finite; a program needn't handle non-finite values.
Results may differ from the reference program's by a relative error of at most 0.013.
Values may be sent and summed in bfloat16 or wider, within the bound.
No kernel may reach another device: no remote copies, remote signals or barrier semaphores. Data moves between devices by JAX's collectives and lax.ppermute only.
A program may use at most 128 MiB of HBM per device.

```python
import math
import jax
import jax.numpy as jnp
from jax import lax

D = 512
HEADS = 8
HEAD_DIM = 64
FF = 2048
OUT = 2048
SLOTS = 8
GROUPS = 8
ENTRIES = 8192


def place_ends(values, rng, smallest, high):
    longest = values.shape.index(max(values.shape))
    spots = []
    for shift in (0, 1):
        where = [jax.random.randint(jax.random.fold_in(rng, axis), (), 0, length) for axis, length in enumerate(values.shape)]
        where[longest] = (where[longest] + shift) % values.shape[longest]
        spots.append(tuple(where))
    return values.at[spots[0]].set(smallest).at[spots[1]].set(high)


def block_scale(rng, extent, shards, smallest, largest):
    def one(position, shards_of):
        heights = jax.random.uniform(jax.random.fold_in(jax.random.fold_in(rng, 6), position), (shards_of,), jnp.float32, smallest / len(shards), largest / len(shards))
        return jnp.repeat(jnp.exp(heights), extent[position] // shards_of).reshape((-1,) + (1,) * (len(extent) - position - 1))

    level = one(*shards[0])
    for cut in shards[1:]:
        level = level * one(*cut)
    return level


def gaussian(rng, shape, scale, most, shards=(), held_as=jnp.bfloat16):
    values = jax.random.normal(rng, shape, jnp.float32) * scale
    if len(shards) > 0:
        values = block_scale(rng, shape, shards, -0.22, 0.18) * values
    return jnp.clip(values, min=-most, max=most).astype(held_as)


def setup_inputs(seed: int = 0) -> dict:
    key_of = jax.random.split(jax.random.key(seed), 17)
    return {
        "embeds": gaussian(key_of[0], (ENTRIES, SLOTS, D), 1.0, 6.0, ((0, 32),)),
        "piece_counts": place_ends(jax.random.randint(key_of[1], (ENTRIES,), 1, SLOTS + 1), jax.random.fold_in(key_of[1], 1), 1, SLOTS).astype(jnp.int32),
        "group_ids": place_ends(jax.random.randint(key_of[2], (ENTRIES,), 0, GROUPS), jax.random.fold_in(key_of[2], 1), 0, GROUPS - 1).astype(jnp.int32),
        "group_table": gaussian(key_of[3], (GROUPS, D), 0.5, 3.0, ((1, 32),)),
        "gain_attn": jnp.clip(1.0 + 0.1 * jax.random.normal(key_of[4], (D,), jnp.float32), 0.5, 1.5).astype(jnp.bfloat16),
        "shift_attn": gaussian(key_of[5], (D,), 0.3, 2.0, ((0, 32),)),
        "w_qkv": gaussian(key_of[6], (D, 3 * D), D ** -0.5, 0.25, ((0, 32),)),
        "w_out": gaussian(key_of[7], (D, D), (D // 2) ** -0.5, 0.375, ((0, 32),)),
        "gain_ffn": jnp.clip(1.0 + 0.1 * jax.random.normal(key_of[8], (D,), jnp.float32), 0.5, 1.5).astype(jnp.bfloat16),
        "shift_ffn": gaussian(key_of[9], (D,), 0.3, 2.0, ((0, 32),)),
        "w_up": gaussian(key_of[10], (D, FF), D ** -0.5, 0.25, ((0, 32),)),
        "bias_up": gaussian(key_of[11], (FF,), 0.3, 2.0, ((0, 32),)),
        "w_down": gaussian(key_of[12], (FF, D), (FF // 2) ** -0.5, 0.1875, ((0, 32),)),
        "bias_down": gaussian(key_of[13], (D,), 0.3, 2.0, ((0, 32),)),
        "w_proj": gaussian(key_of[14], (D, OUT), D ** -0.5, 0.25, ((0, 32),)),
        "cotangent": gaussian(key_of[15], (ENTRIES, OUT), 1.0, 6.0, ((0, 32),)),
    }


@jax.custom_vjp
def low(v):
    return lax.optimization_barrier(v.astype(jnp.bfloat16)).astype(jnp.float32)

@jax.custom_vjp
def low_back(v):
    return v

def low_keep(v):
    return (low(v), None)

def low_pass(kept, grad):
    return (grad,)

def back_keep(v):
    return (v, None)

def back_low(kept, grad):
    return (low(grad),)
low.defvjp(low_keep, low_pass)
low_back.defvjp(back_keep, back_low)

def layer_norm(values, gain, shift):
    center = values - lax.optimization_barrier(jnp.mean(values, axis=-1, keepdims=True))
    spread = lax.optimization_barrier(jnp.mean(center * center, axis=-1, keepdims=True))
    return center * lax.rsqrt(spread + 1e-05) * gain + shift

def product(left, right):
    return jnp.dot(left, right, precision=lax.Precision.HIGHEST)

def matrix_apply(left, right):
    return jnp.einsum('esd,df->esf', left, right, precision=lax.Precision.HIGHEST)

def forward(weights, embeds, counts, groups):
    group_table, gain_attn, shift_attn, w_qkv, w_out, gain_ffn, shift_ffn, w_up, bias_up, w_down, bias_down, w_proj = weights
    entries = embeds.shape[0]
    onehot = (groups[:, None] == jnp.arange(GROUPS, dtype=jnp.int32)[None, :]).astype(jnp.float32)
    base = embeds + product(onehot, group_table)[:, None, :]
    normed = low(layer_norm(base, gain_attn, shift_attn))
    projected = low(low_back(matrix_apply(normed, w_qkv)))
    reshaped = projected.reshape(entries, SLOTS, 3, HEADS, HEAD_DIM)
    queries = reshaped[:, :, 0]
    keys = reshaped[:, :, 1]
    values = reshaped[:, :, 2]
    scores = low_back(jnp.einsum('eqhd,ekhd->ehqk', queries, keys, precision=lax.Precision.HIGHEST) * HEAD_DIM ** (-0.5))
    live = (jnp.arange(SLOTS, dtype=jnp.int32)[None, :] < counts[:, None])[:, None, None, :]
    probs = low(jax.nn.softmax(jnp.where(live, scores, -1000000000.0), axis=-1))
    mixed = jnp.einsum('ehqk,ekhd->eqhd', probs, values, precision=lax.Precision.HIGHEST)
    mixed = low(low_back(mixed.reshape(entries, SLOTS, D)))
    first = base + low_back(matrix_apply(mixed, w_out))
    normed_ffn = low(layer_norm(first, gain_ffn, shift_ffn))
    hidden = low(jax.nn.gelu(low_back(matrix_apply(normed_ffn, w_up)) + bias_up, approximate=False))
    second = first + low_back(matrix_apply(hidden, w_down)) + bias_down
    pooled = low(second[:, 0, :])
    return product(pooled, w_proj)

def reference(embeds, piece_counts, group_ids, group_table, gain_attn, shift_attn, w_qkv, w_out, gain_ffn, shift_ffn, w_up, bias_up, w_down, bias_down, w_proj, cotangent):
    weights = tuple((member.astype(jnp.float32) for member in (group_table, gain_attn, shift_attn, w_qkv, w_out, gain_ffn, shift_ffn, w_up, bias_up, w_down, bias_down, w_proj)))
    block = math.gcd(ENTRIES, 512)
    blocks = ENTRIES // block
    inputs = (embeds.astype(jnp.float32).reshape(blocks, block, SLOTS, D), piece_counts.reshape(blocks, block), group_ids.reshape(blocks, block), cotangent.astype(jnp.float32).reshape(blocks, block, OUT))

    def step(totals, item):
        block_embeds, block_counts, block_groups, block_cot = item
        result, backward = jax.vjp(lambda params, emb: forward(params, emb, block_counts, block_groups), weights, block_embeds)
        grad_params, grad_emb = backward(block_cot)
        return (tuple((left + right for left, right in zip(totals, grad_params))), (result, grad_emb))
    start = tuple((jnp.zeros_like(member) for member in weights))
    totals, (results, grads) = lax.scan(step, start, inputs)
    return (results.reshape(ENTRIES, OUT).astype(jnp.bfloat16), grads.reshape(ENTRIES, SLOTS, D).astype(jnp.bfloat16), totals[0], totals[1], totals[2], totals[3], totals[4], totals[5], totals[6], totals[7], totals[8], totals[9], totals[10], totals[11])
```

```python
import jax
import jax.numpy as jnp
from jax import lax
from jax.experimental import pallas as pl
from jax.experimental.pallas import tpu as pltpu
from jax.sharding import PartitionSpec as P

HEADS = 8
GROUPS = 8
BLOCK = 16


def pairs(n, partner):
    return [(i, partner(i)) for i in range(n)]


def core_pairs(n):
    return pairs(n, lambda i: i ^ 1)


def near_pairs(n):
    return pairs(n, lambda i: i ^ (2 if i % 2 == 0 else 4))


def far_pairs(n):
    return pairs(n, lambda i: i ^ (4 if i % 2 == 0 else 2))


def layer_pairs(n, p):
    return pairs(n, lambda i: i ^ (p << 3))


def shard_order():
    me = lax.axis_index("dp").astype(jnp.int32)
    near = jnp.where(me % 2 == 0, 2, 4).astype(jnp.int32)
    far = 6 - near
    quads = jnp.stack([0 * near, near, far, 0 * near + 6, 0 * near + 1, far + 1, near + 1, 0 * near + 7])
    layers = jnp.arange(4, dtype=jnp.int32) * 8
    return me ^ (quads[:, None] ^ layers[None, :]).reshape(32)


def gather(shard):
    n = 32
    parts = [shard] + [lax.ppermute(shard, "dp", layer_pairs(n, p)) for p in (1, 2, 3)]
    own = jnp.stack(parts)
    near = lax.ppermute(own, "dp", near_pairs(n))
    far = lax.ppermute(own, "dp", far_pairs(n))
    both = lax.ppermute(near, "dp", far_pairs(n))
    mine = [own, near, far, both]
    return mine + [lax.ppermute(part, "dp", core_pairs(n)) for part in mine]


def scatter(own, other):
    n = 32
    f32, low = jnp.float32, jnp.bfloat16
    core = lax.ppermute(other, "dp", core_pairs(n))
    first = lax.ppermute((own[8:] + core[8:].astype(f32)).astype(low), "dp", far_pairs(n))
    total = own[:8] + core[:8].astype(f32) + first.astype(f32)
    second = lax.ppermute(total[4:].astype(low), "dp", near_pairs(n))
    total = total[:4] + second.astype(f32)
    last = [lax.ppermute(total[p].astype(low), "dp", layer_pairs(n, p)) for p in (1, 2, 3)]
    return total[0] + last[0].astype(f32) + last[1].astype(f32) + last[2].astype(f32)


def place_kernel(order, *refs):
    out = refs[8]
    for i in range(8):
        for p in range(4):
            out[order[4 * i + p]] = refs[i][p]


def place(order, parts):
    vmem = pl.BlockSpec(memory_space=pltpu.VMEM)
    return pl.pallas_call(
        place_kernel,
        out_shape=jax.ShapeDtypeStruct((32,) + parts[0].shape[1:], parts[0].dtype),
        in_specs=[pl.BlockSpec(memory_space=pltpu.SMEM)] + [vmem] * 8,
        out_specs=vmem,
        compiler_params=pltpu.CompilerParams(vmem_limit_bytes=40 * 2**20),
    )(order, *parts)


def pack_kernel(order, grad, own, other):
    for i in range(16):
        own[i] = grad[order[i]]
        other[i] = grad[order[16 + i]].astype(jnp.bfloat16)


def pack(order, grad):
    vmem = pl.BlockSpec(memory_space=pltpu.VMEM)
    half = (16,) + grad.shape[1:]
    return pl.pallas_call(
        pack_kernel,
        out_shape=(jax.ShapeDtypeStruct(half, jnp.float32), jax.ShapeDtypeStruct(half, jnp.bfloat16)),
        in_specs=[pl.BlockSpec(memory_space=pltpu.SMEM), vmem],
        out_specs=(vmem, vmem),
        compiler_params=pltpu.CompilerParams(vmem_limit_bytes=40 * 2**20),
    )(order, grad)


def layer_norm(values, gain, shift):
    center = values - jnp.mean(values, axis=-1, keepdims=True)
    spread = jnp.mean(center * center, axis=-1, keepdims=True)
    return center * lax.rsqrt(spread + 1e-05) * gain + shift


def gelu_exact(values):
    return jax.nn.gelu(values, approximate=False)


def softmax_last(values):
    return jax.nn.softmax(values, axis=-1)


def on_device(
    embeds,
    piece_counts,
    group_ids,
    group_table,
    gain_attn,
    shift_attn,
    w_qkv,
    w_out,
    gain_ffn,
    shift_ffn,
    w_up,
    bias_up,
    w_down,
    bias_down,
    w_proj,
    cotangent,
):
    tuned = lax.axis_size("dp") == 32
    if tuned:
        order = shard_order()
        rows = jnp.concatenate(
            [group_table, jnp.stack([gain_attn, shift_attn, gain_ffn, shift_ffn, bias_down])]
        )
        small = jnp.concatenate(
            [
                jnp.tile(rows, (1, 8)),
                jnp.tile(bias_up[None, :], (1, 2)),
                jnp.zeros((2, 128), jnp.bfloat16),
            ]
        )
        first_all = place(order, gather(jnp.concatenate([w_qkv, w_out, small], axis=1)))
        pair_all = place(order, gather(jnp.concatenate([w_proj, w_up])))
        down_all = place(order, gather(w_down)).reshape(2048, 512)
        qkv_all = first_all[:, :, :1536].reshape(512, 1536)
        out_all = first_all[:, :, 1536:2048].reshape(512, 512)
        vectors = jnp.transpose(first_all[:, :13, 2048:2064], (1, 0, 2)).reshape(13, 512)
        table_all = vectors[:8]
        gain_one, shift_one, gain_two, shift_two, downbias_all = [vectors[8 + i] for i in range(5)]
        upbias_all = first_all[:, 13, 2048:2112].reshape(2048)
        proj_all = pair_all[:, :16].reshape(512, 2048)
        up_all = pair_all[:, 16:].reshape(512, 2048)
    else:
        (
            table_all,
            gain_one,
            shift_one,
            qkv_all,
            out_all,
            gain_two,
            shift_two,
            up_all,
            upbias_all,
            down_all,
            downbias_all,
            proj_all,
        ) = (
            lax.all_gather(group_table, "dp", axis=1, tiled=True),
            lax.all_gather(gain_attn, "dp", axis=0, tiled=True),
            lax.all_gather(shift_attn, "dp", axis=0, tiled=True),
            lax.all_gather(w_qkv, "dp", axis=0, tiled=True),
            lax.all_gather(w_out, "dp", axis=0, tiled=True),
            lax.all_gather(gain_ffn, "dp", axis=0, tiled=True),
            lax.all_gather(shift_ffn, "dp", axis=0, tiled=True),
            lax.all_gather(w_up, "dp", axis=0, tiled=True),
            lax.all_gather(bias_up, "dp", axis=0, tiled=True),
            lax.all_gather(w_down, "dp", axis=0, tiled=True),
            lax.all_gather(bias_down, "dp", axis=0, tiled=True),
            lax.all_gather(w_proj, "dp", axis=0, tiled=True),
        )
    entries, slots, width = embeds.shape
    head_dim = width // HEADS
    scale = head_dim ** (-0.5)
    onehot = (
        group_ids[:, None] == jnp.arange(table_all.shape[0], dtype=jnp.int32)[None, :]
    ).astype(jnp.bfloat16)
    group_rows = jnp.dot(onehot, table_all, preferred_element_type=jnp.float32)
    base = embeds.astype(jnp.float32) + group_rows[:, None, :]
    normed, norm_back = jax.vjp(
        layer_norm, base, gain_one.astype(jnp.float32), shift_one.astype(jnp.float32)
    )
    normed_low = normed.astype(jnp.bfloat16)
    normed_flat = normed_low.reshape(entries * slots, width)
    query = (
        jnp.dot(normed_low[:, 0, :], qkv_all[:, :width], preferred_element_type=jnp.float32)
        .astype(jnp.bfloat16)
        .reshape(entries, HEADS, head_dim)
    )
    keyval = (
        jnp.dot(normed_flat, qkv_all[:, width:], preferred_element_type=jnp.float32)
        .astype(jnp.bfloat16)
        .reshape(entries, slots, 2, HEADS, head_dim)
    )
    keys = keyval[:, :, 0]
    values = keyval[:, :, 1]
    scores = jnp.einsum("ehd,eshd->ehs", query, keys, preferred_element_type=jnp.float32) * scale
    live = (jnp.arange(slots, dtype=jnp.int32)[None, :] < piece_counts[:, None])[:, None, :]
    probs, soft_back = jax.vjp(softmax_last, jnp.where(live, scores, -1000000000.0))
    probs_low = probs.astype(jnp.bfloat16)
    mixed = (
        jnp.einsum("ehs,eshd->ehd", probs_low, values, preferred_element_type=jnp.float32)
        .reshape(entries, width)
        .astype(jnp.bfloat16)
    )
    first = base[:, 0, :] + jnp.dot(mixed, out_all, preferred_element_type=jnp.float32)
    normed_ffn, ffn_back = jax.vjp(
        layer_norm, first, gain_two.astype(jnp.float32), shift_two.astype(jnp.float32)
    )
    ffn_low = normed_ffn.astype(jnp.bfloat16)
    hidden, gelu_back = jax.vjp(
        gelu_exact,
        jnp.dot(ffn_low, up_all, preferred_element_type=jnp.float32)
        + upbias_all.astype(jnp.float32),
    )
    hidden_low = hidden.astype(jnp.bfloat16)
    second = (
        first
        + jnp.dot(hidden_low, down_all, preferred_element_type=jnp.float32)
        + downbias_all.astype(jnp.float32)
    )
    pooled_low = second.astype(jnp.bfloat16)
    output = jnp.dot(pooled_low, proj_all, preferred_element_type=jnp.float32).astype(jnp.bfloat16)
    grad_proj = jnp.einsum("ed,eo->do", pooled_low, cotangent, preferred_element_type=jnp.float32)
    grad_pool = jnp.einsum("eo,do->ed", cotangent, proj_all, preferred_element_type=jnp.float32)
    grad_downbias = jnp.sum(grad_pool, axis=0)
    pool_low = grad_pool.astype(jnp.bfloat16)
    grad_down = jnp.einsum("ef,ed->fd", hidden_low, pool_low, preferred_element_type=jnp.float32)
    grad_hidden = jnp.einsum("ed,fd->ef", pool_low, down_all, preferred_element_type=jnp.float32)
    grad_pre = gelu_back(grad_hidden)[0]
    grad_upbias = jnp.sum(grad_pre, axis=0)
    pre_low = grad_pre.astype(jnp.bfloat16)
    grad_up = jnp.einsum("ed,ef->df", ffn_low, pre_low, preferred_element_type=jnp.float32)
    grad_normffn = jnp.einsum("ef,df->ed", pre_low, up_all, preferred_element_type=jnp.float32)
    grad_first, grad_gaintwo, grad_shifttwo = ffn_back(grad_normffn)
    grad_first = grad_first + grad_pool
    branch_low = grad_first.astype(jnp.bfloat16)
    grad_out = jnp.einsum("ed,ef->df", mixed, branch_low, preferred_element_type=jnp.float32)
    grad_mixed = (
        jnp.einsum("ef,df->ed", branch_low, out_all, preferred_element_type=jnp.float32)
        .astype(jnp.bfloat16)
        .reshape(entries, HEADS, head_dim)
    )
    grad_probs = jnp.einsum("ehd,eshd->ehs", grad_mixed, values, preferred_element_type=jnp.float32)
    grad_values = jnp.einsum(
        "ehs,ehd->eshd", probs_low, grad_mixed, preferred_element_type=jnp.float32
    )
    scores_low = jnp.where(live, soft_back(grad_probs)[0], 0.0).astype(jnp.bfloat16)
    grad_query = (
        (jnp.einsum("ehs,eshd->ehd", scores_low, keys, preferred_element_type=jnp.float32) * scale)
        .astype(jnp.bfloat16)
        .reshape(entries, width)
    )
    grad_keys = (
        jnp.einsum("ehs,ehd->eshd", scores_low, query, preferred_element_type=jnp.float32) * scale
    )
    grad_keyval = (
        jnp.stack([grad_keys, grad_values], axis=2)
        .astype(jnp.bfloat16)
        .reshape(entries * slots, 2 * width)
    )
    grad_qkv = jnp.concatenate(
        [
            jnp.einsum(
                "ed,ef->df", normed_low[:, 0, :], grad_query, preferred_element_type=jnp.float32
            ),
            jnp.einsum("nd,nf->df", normed_flat, grad_keyval, preferred_element_type=jnp.float32),
        ],
        axis=1,
    )
    grad_normed = jnp.einsum(
        "nf,df->nd", grad_keyval, qkv_all[:, width:], preferred_element_type=jnp.float32
    ).reshape(entries, slots, width)
    grad_normed = grad_normed.at[:, 0, :].add(
        jnp.einsum("ef,df->ed", grad_query, qkv_all[:, :width], preferred_element_type=jnp.float32)
    )
    grad_base, grad_gainone, grad_shiftone = norm_back(grad_normed)
    grad_base = grad_base.at[:, 0, :].add(grad_first)
    grad_groups = jnp.dot(
        onehot.astype(jnp.float32).T, jnp.sum(grad_base, axis=1), precision=lax.Precision.HIGHEST
    )
    if tuned:
        vectors = jnp.concatenate(
            [grad_groups, jnp.stack([grad_gainone, grad_shiftone, grad_gaintwo, grad_shifttwo, grad_downbias])]
        ).reshape(13, 32, 16)
        small = jnp.concatenate(
            [
                jnp.pad(jnp.transpose(vectors, (1, 0, 2)), ((0, 0), (0, 0), (0, 112))),
                jnp.pad(grad_upbias.reshape(32, 1, 64), ((0, 0), (0, 2), (0, 64))),
            ],
            axis=1,
        )
        sum_down = scatter(*pack(order, grad_down.reshape(32, 64, 512)))
        pair = scatter(
            *pack(order, jnp.concatenate([grad_proj.reshape(32, 16, 2048), grad_up.reshape(32, 16, 2048)], axis=1))
        )
        last = scatter(
            *pack(
                order,
                jnp.concatenate([grad_qkv.reshape(32, 16, 1536), grad_out.reshape(32, 16, 512), small], axis=2),
            )
        )
        sum_proj, sum_up = pair[:16], pair[16:]
        sum_qkv, sum_out = last[:, :1536], last[:, 1536:2048]
        sum_groups = last[:8, 2048:2064]
        sum_gainone, sum_shiftone, sum_gaintwo, sum_shifttwo, sum_downbias = [
            last[8 + i, 2048:2064] for i in range(5)
        ]
        sum_upbias = last[13, 2048:2112]
    else:
        (
            sum_groups,
            sum_gainone,
            sum_shiftone,
            sum_qkv,
            sum_out,
            sum_gaintwo,
            sum_shifttwo,
            sum_up,
            sum_upbias,
            sum_down,
            sum_downbias,
            sum_proj,
        ) = (
            lax.psum_scatter(grad_groups, "dp", scatter_dimension=1, tiled=True),
            lax.psum_scatter(grad_gainone, "dp", scatter_dimension=0, tiled=True),
            lax.psum_scatter(grad_shiftone, "dp", scatter_dimension=0, tiled=True),
            lax.psum_scatter(grad_qkv, "dp", scatter_dimension=0, tiled=True),
            lax.psum_scatter(grad_out, "dp", scatter_dimension=0, tiled=True),
            lax.psum_scatter(grad_gaintwo, "dp", scatter_dimension=0, tiled=True),
            lax.psum_scatter(grad_shifttwo, "dp", scatter_dimension=0, tiled=True),
            lax.psum_scatter(grad_up, "dp", scatter_dimension=0, tiled=True),
            lax.psum_scatter(grad_upbias, "dp", scatter_dimension=0, tiled=True),
            lax.psum_scatter(grad_down, "dp", scatter_dimension=0, tiled=True),
            lax.psum_scatter(grad_downbias, "dp", scatter_dimension=0, tiled=True),
            lax.psum_scatter(grad_proj, "dp", scatter_dimension=0, tiled=True),
        )
    return (
        output,
        grad_base.astype(jnp.bfloat16),
        sum_groups,
        sum_gainone,
        sum_shiftone,
        sum_qkv,
        sum_out,
        sum_gaintwo,
        sum_shifttwo,
        sum_up,
        sum_upbias,
        sum_down,
        sum_downbias,
        sum_proj,
    )


def solution(mesh):
    placed = (
        P("dp", None, None),
        P("dp"),
        P("dp"),
        P(None, "dp"),
        P("dp"),
        P("dp"),
        P("dp", None),
        P("dp", None),
        P("dp"),
        P("dp"),
        P("dp", None),
        P("dp"),
        P("dp", None),
        P("dp"),
        P("dp", None),
        P("dp", None),
    )
    return jax.shard_map(
        on_device,
        mesh=mesh,
        in_specs=placed,
        out_specs=(
            P("dp", None),
            P("dp", None, None),
            P(None, "dp"),
            P("dp"),
            P("dp"),
            P("dp", None),
            P("dp", None),
            P("dp"),
            P("dp"),
            P("dp", None),
            P("dp"),
            P("dp", None),
            P("dp"),
            P("dp", None),
        ),
        check_vma=False,
    )
```

```python
import jax
import jax.numpy as jnp
from jax import lax
from jax.experimental import pallas as pl
from jax.experimental.pallas import tpu as pltpu
from jax.sharding import PartitionSpec as P

HEADS = 8
HEAD_DIM = 64
SLOTS = 8
SHARDS = 32
EB = 32
RB = EB * SLOTS
CH = 64
SCALE = HEAD_DIM ** (-0.5)
F32 = jnp.float32
LOW = jnp.bfloat16
VMEM_LIMIT = 48 * 2**20


def pairs(partner):
    return [(i, partner(i)) for i in range(32)]


CORE = pairs(lambda i: i ^ 1)
NEAR = pairs(lambda i: i ^ (2 if i % 2 == 0 else 4))
FAR = pairs(lambda i: i ^ (4 if i % 2 == 0 else 2))
LAYER = {p: pairs(lambda i: i ^ (p << 3)) for p in (1, 2, 3)}


def send(value, to):
    return lax.ppermute(value, "dp", to)


def shard_order():
    me = lax.axis_index("dp").astype(jnp.int32)
    near = jnp.where(me % 2 == 0, 2, 4).astype(jnp.int32)
    far = 6 - near
    none = 0 * near
    quads = jnp.stack([none, near, far, none + 6, none + 1, far + 1, near + 1, none + 7])
    layers = jnp.arange(4, dtype=jnp.int32) * 8
    return me ^ (quads[:, None] ^ layers[None, :]).reshape(32)


def gather(shard):
    own = jnp.stack([shard] + [send(shard, LAYER[p]) for p in (1, 2, 3)])
    near = send(own, NEAR)
    far = send(own, FAR)
    both = send(near, FAR)
    mine = [own, near, far, both]
    return mine + [send(part, CORE) for part in mine]


def scatter(own, other):
    core = send(other, CORE)
    first = send((own[8:] + core[8:].astype(F32)).astype(LOW), FAR)
    total = own[:8] + core[:8].astype(F32) + first.astype(F32)
    second = send(total[4:].astype(LOW), NEAR)
    total = total[:4] + second.astype(F32)
    last = [send(total[p].astype(LOW), LAYER[p]) for p in (1, 2, 3)]
    return total[0] + last[0].astype(F32) + last[1].astype(F32) + last[2].astype(F32)


def dot(left, right):
    return jnp.dot(left, right, preferred_element_type=F32)


def dot_nt(left, right):
    return lax.dot_general(left, right, (((1,), (1,)), ((), ())), preferred_element_type=F32)


def dot_tn(left, right):
    return lax.dot_general(left, right, (((0,), (0,)), ((), ())), preferred_element_type=F32)


def iota(shape, axis):
    return lax.broadcasted_iota(jnp.int32, shape, axis)


def norm_parts(values):
    center = values - jnp.mean(values, axis=-1, keepdims=True)
    rate = lax.rsqrt(jnp.mean(center * center, axis=-1, keepdims=True) + 1e-05)
    return center * rate, rate


def norm_back(grad, unit, rate, gain):
    scaled = grad * gain
    return rate * (
        scaled
        - jnp.mean(scaled, axis=-1, keepdims=True)
        - unit * jnp.mean(scaled * unit, axis=-1, keepdims=True)
    )


def fold(values):
    rows, width = values.shape
    return jnp.sum(values.reshape(rows // 8, 8, width), axis=0)


def spread_heads(rows):
    tiled = jnp.concatenate([rows] * HEADS, axis=0)
    shape = (HEADS * EB, HEADS * HEAD_DIM)
    return jnp.where(iota(shape, 0) // EB == iota(shape, 1) // HEAD_DIM, tiled, jnp.zeros_like(tiled))


def pick_heads(full):
    parts = []
    for k in range(HEADS // 2):
        lanes = slice(128 * k, 128 * k + 128)
        even = full[2 * k * EB : (2 * k + 1) * EB, lanes]
        odd = full[(2 * k + 1) * EB : (2 * k + 2) * EB, lanes]
        parts.append(jnp.where(iota(even.shape, 1) < HEAD_DIM, even, odd))
    return jnp.concatenate(parts, axis=1)


def slots_first(ref, out, at):
    for k in range(4):
        out[at, 128 * k : 128 * k + 128] = ref[pl.ds(k * RB, EB, stride=SLOTS), :]


def put_first(ref, values):
    for k in range(4):
        ref[pl.ds(k * RB, EB, stride=SLOTS), :] = values[:, 128 * k : 128 * k + 128]


def put_tall(ref, start, values):
    for k in range(4):
        ref[pl.ds(k * RB + start, values.shape[0]), :] = values[:, 128 * k : 128 * k + 128]


def get_tall(ref, start, rows):
    return jnp.concatenate([ref[pl.ds(k * RB + start, rows), :] for k in range(4)], axis=1)


def block(i, rows):
    return pl.ds(pl.multiple_of(i * rows, rows), rows)


def attend_kernel(order, p0, p1, p2, p3, p4, p5, p6, p7, embeds, marks,
                  w_qkv, w_out, vec, bias_up, normed, normed0, query, keyval, probs, mixed, first, norm_ffn,
                  small, table, rows, tall, rows0, base0, norm0):
    for i, piece in enumerate((p0, p1, p2, p3, p4, p5, p6, p7)):
        for p in range(4):
            r = order[4 * i + p]
            at = block(r, 16)
            w_qkv[at, :] = piece[p, :, :1536]
            w_out[at, :] = piece[p, :, 1536:2048]
            small[r] = piece[p, :, 2048:2176].astype(F32)
    lane = iota((16, 128), 1)
    for k in range(4):
        tile = jnp.zeros((16, 128), F32)
        for t in range(8):
            tile = jnp.where(lane // 16 == t, small[8 * k + t], tile)
        vec[:, 128 * k : 128 * k + 128] = tile
    lane = iota((1, 128), 1)
    for k in range(16):
        tile = jnp.where(lane < 64, small[2 * k, 13:14, :], small[2 * k + 1, 13:14, :])
        bias_up[:, 128 * k : 128 * k + 128] = jnp.broadcast_to(tile, (8, 128))
    table[...] = jnp.zeros_like(table)
    table[0:8, :] = vec[0:8, :]

    gain, shift = vec[8:9, :], vec[9:10, :]
    blocks = embeds.shape[0] // RB

    def norm_block(b, _):
        rows[...] = dot(marks[block(b, RB), :], table[...].astype(LOW))
        for c in range(RB // CH):
            at = pl.ds(c * CH, CH)
            here = pl.ds(pl.multiple_of(b * RB + c * CH, CH), CH)
            base = embeds[here, :].astype(F32) + rows[at, :]
            put_tall(tall, c * CH, base)
            unit, _rate = norm_parts(base)
            value = unit * gain + shift
            put_tall(rows0, c * CH, value)
            normed[here, :] = value.astype(LOW)
        out = block(b, EB)
        slots_first(tall, base0, out)
        slots_first(rows0, norm0, out)
        keyval[block(b, RB), :] = dot(normed[block(b, RB), :], w_qkv[:, 512:]).astype(LOW)
        return 0

    lax.fori_loop(0, blocks, norm_block, 0)
    normed0[...] = norm0[...].astype(LOW)
    query[...] = dot(normed0[...], w_qkv[:, :512]).astype(LOW)

    shape = (RB, HEADS * EB)
    match = iota(shape, 0) // SLOTS == iota(shape, 1) % EB
    liver = jnp.where(iota((128, HEADS * EB), 0) == 8, 1.0, 0.0).astype(LOW)

    def attend_block(b, _):
        at, out = block(b, RB), block(b, EB)
        scores = dot_nt(keyval[at, :512], spread_heads(query[out, :])) * SCALE
        live = dot(marks[at, :], liver) > 0.5
        scores = jnp.where(live, scores, -1000000000.0).reshape(EB, SLOTS, HEADS * EB)
        top = jnp.max(scores, axis=1, keepdims=True)
        power = jnp.exp(scores - top)
        part = (power / jnp.sum(power, axis=1, keepdims=True)).reshape(shape)
        low = jnp.where(match, part, 0.0).astype(LOW)
        probs[at, :] = low
        mixed[out, :] = pick_heads(dot_tn(low, keyval[at, 512:])).astype(LOW)
        return 0

    lax.fori_loop(0, blocks, attend_block, 0)

    def ffn_block(b, _):
        at = block(b, CH)
        value = base0[at, :] + dot(mixed[at, :], w_out[...])
        first[at, :] = value
        unit, _rate = norm_parts(value)
        norm_ffn[at, :] = (unit * vec[10:11, :] + vec[11:12, :]).astype(LOW)
        return 0

    lax.fori_loop(0, first.shape[0] // CH, ffn_block, 0)


def hidden_kernel(order, p0, p1, p2, p3, p4, p5, p6, p7, norm_ffn, bias_up, cotangent,
                  w_proj, w_up, dpool, hidden, slope, own, other, sum_pool, total):
    for i, piece in enumerate((p0, p1, p2, p3, p4, p5, p6, p7)):
        for p in range(4):
            at = block(order[4 * i + p], 16)
            w_proj[at, :] = piece[p, :16, :]
            w_up[at, :] = piece[p, 16:, :]
    grad = dot_nt(cotangent[...], w_proj[...])
    dpool[...] = grad
    sum_pool[...] = fold(grad)
    low = grad.astype(LOW)
    for k in range(8):
        lanes = slice(256 * k, 256 * k + 256)
        pre = dot(norm_ffn[...], w_up[:, lanes])
        rows = pre.shape[0] // 4
        for c in range(4):
            at = slice(rows * c, rows * c + rows)
            value = pre[at] + bias_up[0:1, lanes]
            below = 0.5 * (1.0 + lax.erf(value * (0.5**0.5)))
            hidden[at, lanes] = (value * below).astype(LOW)
            slope[at, lanes] = below + value * (jnp.exp(-0.5 * value * value) * 0.3989422804014327)
        total[256 * k : 256 * k + 256, :] = dot_tn(hidden[:, lanes], low)
    for i in range(16):
        own[i] = total[block(order[i], 64), :]
        other[i] = total[block(order[16 + i], 64), :].astype(LOW)


def ffn_back_kernel(order, p0, p1, p2, p3, p4, p5, p6, p7, dpool, hidden, slope, w_up, w_out, w_proj, vec, first,
                    norm_ffn, mixed, cotangent,
                    output, dfirst, dmixed, grad_out, own, other, sum_up, sum_gain, sum_shift,
                    w_down, pre_low, grad_proj, grad_up):
    for i, piece in enumerate((p0, p1, p2, p3, p4, p5, p6, p7)):
        for p in range(4):
            w_down[block(order[4 * i + p], 64), :] = piece[p]
    low = dpool[...].astype(LOW)
    for k in range(8):
        lanes = slice(256 * k, 256 * k + 256)
        dpre = slope[:, lanes] * dot_nt(low, w_down[lanes, :])
        sum_up[:, lanes] = fold(dpre)
        pre_low[:, lanes] = dpre.astype(LOW)
    dfirst[...] = dot_nt(pre_low[...], w_up[...])
    gains = jnp.zeros((8, 512), F32)
    shifts = jnp.zeros((8, 512), F32)
    for c in range(first.shape[0] // CH):
        at = slice(CH * c, CH * c + CH)
        grad = dfirst[at, :]
        unit, rate = norm_parts(first[at, :])
        gains += fold(grad * unit)
        shifts += fold(grad)
        dfirst[at, :] = norm_back(grad, unit, rate, vec[10:11, :]) + dpool[at, :]
    sum_gain[...] = gains
    sum_shift[...] = shifts
    first_low = dfirst[...].astype(LOW)
    dmixed[...] = dot_nt(first_low, w_out[...]).astype(LOW)
    grad_out[...] = dot_tn(mixed[...], first_low)
    pooled = (first[...] + dot(hidden[...], w_down[...]) + vec[12:13, :]).astype(LOW)
    for k in range(8):
        lanes = slice(256 * k, 256 * k + 256)
        output[:, lanes] = dot(pooled, w_proj[:, lanes]).astype(LOW)
        grad_proj[:, lanes] = dot_tn(pooled, cotangent[:, lanes])
        grad_up[:, lanes] = dot_tn(norm_ffn[...], pre_low[:, lanes])
    for i in range(16):
        at, there = block(order[i], 16), block(order[16 + i], 16)
        own[i, :16, :] = grad_proj[at, :]
        own[i, 16:, :] = grad_up[at, :]
        other[i, :16, :] = grad_proj[there, :].astype(LOW)
        other[i, 16:, :] = grad_up[there, :].astype(LOW)


def attend_back_kernel(order, embeds, marks, w_qkv, vec, normed, normed0, query, keyval, probs, dmixed, dfirst,
                       grad_out, sum_gain_ffn, sum_shift_ffn, sum_pool, sum_up,
                       grad_embeds, own, other,
                       table, rows, work, spread_query, spread_first, dquery, dkeyval, query_part, grad_qkv, small, sums):
    blocks = embeds.shape[0] // RB
    table[...] = jnp.zeros_like(table)
    table[0:8, :] = vec[0:8, :].astype(LOW)

    def attend_block(b, _):
        at, out = block(b, RB), block(b, EB)
        low = probs[at, :]
        part = low.astype(F32)
        dmix = spread_heads(dmixed[out, :])
        grad = dot_nt(keyval[at, 512:], dmix)
        shape = (EB, SLOTS, HEADS * EB)
        whole = jnp.sum((part * grad).reshape(shape), axis=1, keepdims=True)
        dscores = (part.reshape(shape) * (grad.reshape(shape) - whole)).reshape(RB, HEADS * EB).astype(LOW)
        dkeyval[at, 512:] = dot(low, dmix).astype(LOW)
        dkeyval[at, :512] = (dot(dscores, spread_heads(query[out, :])) * SCALE).astype(LOW)
        dquery[out, :] = (pick_heads(dot_tn(dscores, keyval[at, :512])) * SCALE).astype(LOW)
        return 0

    lax.fori_loop(0, blocks, attend_block, 0)
    grad_qkv[:, :512] = dot_tn(normed0[...], dquery[...])
    for k in range(4):
        lanes = slice(256 * k, 256 * k + 256)
        grad_qkv[:, 512 + 256 * k : 768 + 256 * k] = dot_tn(normed[...], dkeyval[:, lanes])
    query_part[...] = dot_nt(dquery[...], w_qkv[:, :512])
    sums[...] = jnp.zeros_like(sums)
    spread_query[...] = jnp.zeros_like(spread_query)
    spread_first[...] = jnp.zeros_like(spread_first)
    gain = vec[8:9, :]

    def norm_block(b, _):
        at, out = block(b, RB), block(b, EB)
        put_first(spread_query, query_part[out, :])
        put_first(spread_first, dfirst[out, :])
        rows[...] = dot(marks[at, :], table[...])
        work[...] = dot_nt(dkeyval[at, :], w_qkv[:, 512:])
        for c in range(RB // CH):
            local = pl.ds(c * CH, CH)
            here = pl.ds(pl.multiple_of(b * RB + c * CH, CH), CH)
            grad = work[local, :] + get_tall(spread_query, c * CH, CH)
            unit, rate = norm_parts(embeds[here, :].astype(F32) + rows[local, :])
            sums[0:8, :] += fold(grad * unit)
            sums[8:16, :] += fold(grad)
            work[local, :] = norm_back(grad, unit, rate, gain) + get_tall(spread_first, c * CH, CH)
        value = work[...]
        high = value.astype(LOW)
        rest = (value - high.astype(F32)).astype(LOW)
        grad_embeds[at, :] = high
        sums[16:144, :] += dot_tn(marks[at, :], high) + dot_tn(marks[at, :], rest)
        return 0

    lax.fori_loop(0, blocks, norm_block, 0)
    small[...] = jnp.zeros_like(small)
    small[0:8, :] = sums[16:24, :]
    for i, value in enumerate((sums[0:8, :], sums[8:16, :], sum_gain_ffn[...], sum_shift_ffn[...], sum_pool[...])):
        small[8 + i : 9 + i, :] = jnp.sum(value, axis=0, keepdims=True)
    up = jnp.sum(sum_up[...], axis=0, keepdims=True)
    row = iota((16, 128), 0)
    for r in range(SHARDS):
        tile = small[:, 128 * (r // 8) : 128 * (r // 8) + 128]
        tile = jnp.where(row == 13, up[:, 128 * (r // 2) : 128 * (r // 2) + 128], tile)
        rows[8 * r : 8 * r + 8, 0:128] = tile[0:8]
        rows[8 * r : 8 * r + 8, 128:256] = tile[8:16]
    for i in range(16):
        for k, half in ((i, own), (16 + i, other)):
            r = order[k]
            at = block(r, 16)
            near = block(r, 8)
            half[i, :, :1536] = grad_qkv[at, :].astype(half.dtype)
            half[i, :, 1536:2048] = grad_out[at, :].astype(half.dtype)
            half[i, :, 2048:2176] = jnp.concatenate([rows[near, 0:128], rows[near, 128:256]]).astype(half.dtype)


def call(kernel, args, outs, scratch=(), flops=10**9):
    vmem = pl.BlockSpec(memory_space=pltpu.VMEM)
    size = sum(a.size * a.dtype.itemsize for a in args) + sum(
        jnp.dtype(t).itemsize * jnp.prod(jnp.array(s)).item() if False else 0 for s, t in outs
    )
    return pl.pallas_call(
        kernel,
        out_shape=[jax.ShapeDtypeStruct(s, t) for s, t in outs],
        in_specs=[pl.BlockSpec(memory_space=pltpu.SMEM)] + [vmem] * (len(args) - 1),
        out_specs=[vmem] * len(outs),
        scratch_shapes=[pltpu.VMEM(s, t) for s, t in scratch],
        compiler_params=pltpu.CompilerParams(vmem_limit_bytes=VMEM_LIMIT),
        cost_estimate=pl.CostEstimate(flops=flops, bytes_accessed=size, transcendentals=0),
    )(*args)


def on_device(
    embeds,
    piece_counts,
    group_ids,
    group_table,
    gain_attn,
    shift_attn,
    w_qkv,
    w_out,
    gain_ffn,
    shift_ffn,
    w_up,
    bias_up,
    w_down,
    bias_down,
    w_proj,
    cotangent,
):
    tuned = lax.axis_size("dp") == 32
    entries = embeds.shape[0]
    rows = entries * SLOTS
    flat = embeds.reshape(rows, 512)
    lane = jnp.arange(128, dtype=jnp.int32)
    slot = jnp.arange(SLOTS, dtype=jnp.int32)
    marks = jnp.where(
        lane[None, None, :] < 8,
        group_ids[:, None, None] == lane[None, None, :],
        slot[None, :, None] < piece_counts[:, None, None],
    )
    marks = marks.astype(LOW).reshape(rows, 128)
    vectors = jnp.concatenate([group_table, jnp.stack([gain_attn, shift_attn, gain_ffn, shift_ffn, bias_down])])
    if tuned:
        order = shard_order()
        small = jnp.concatenate(
            [jnp.tile(vectors, (1, 8)), jnp.tile(bias_up[None, :], (1, 2)), jnp.zeros((2, 128), LOW)]
        )
        pieces = [
            gather(jnp.concatenate([w_qkv, w_out, small], axis=1)),
            gather(jnp.concatenate([w_proj, w_up])),
            gather(w_down),
        ]
    else:
        order = jnp.arange(32, dtype=jnp.int32)

        def whole(shard, axis=0):
            return lax.all_gather(shard, "dp", axis=axis, tiled=True)

        def cut(full):
            return [full[4 * i : 4 * i + 4] for i in range(8)]

        spread = jnp.transpose(whole(vectors, 1).reshape(13, SHARDS, 16), (1, 0, 2))
        small = jnp.concatenate(
            [
                jnp.tile(spread, (1, 1, 8)),
                jnp.tile(whole(bias_up).reshape(SHARDS, 1, 64), (1, 1, 2)),
                jnp.zeros((SHARDS, 2, 128), LOW),
            ],
            axis=1,
        )
        pieces = [
            cut(
                jnp.concatenate(
                    [whole(w_qkv).reshape(SHARDS, 16, 1536), whole(w_out).reshape(SHARDS, 16, 512), small], axis=2
                )
            ),
            cut(
                jnp.concatenate(
                    [whole(w_proj).reshape(SHARDS, 16, 2048), whole(w_up).reshape(SHARDS, 16, 2048)], axis=1
                )
            ),
            cut(whole(w_down).reshape(SHARDS, 64, 512)),
        ]
    (qkv_all, out_all, vec, upbias, normed, normed0, query, keyval, probs, mixed, first, norm_ffn) = call(
        attend_kernel,
        [order, *pieces[0], flat, marks],
        [
            ((512, 1536), LOW), ((512, 512), LOW), ((16, 512), F32), ((8, 2048), F32), ((rows, 512), LOW),
            ((entries, 512), LOW), ((entries, 512), LOW), ((rows, 1024), LOW), ((rows, HEADS * EB), LOW),
            ((entries, 512), LOW), ((entries, 512), F32), ((entries, 512), LOW),
        ],
        [
            ((32, 16, 128), F32), ((128, 512), F32), ((RB, 512), F32), ((4 * RB, 128), F32), ((4 * RB, 128), F32), ((entries, 512), F32),
            ((entries, 512), F32),
        ],
        flops=4 * 10**9,
    )
    (proj_all, up_all, dpool, hidden, slope, own_down, other_down, sum_pool) = call(
        hidden_kernel,
        [order, *pieces[1], norm_ffn, upbias, cotangent],
        [
            ((512, 2048), LOW), ((512, 2048), LOW), ((entries, 512), F32), ((entries, 2048), LOW),
            ((entries, 2048), F32), ((16, 64, 512), F32), ((16, 64, 512), LOW), ((8, 512), F32),
        ],
        [((2048, 512), F32)],
        flops=2 * 10**9,
    )
    (output, dfirst, dmixed, grad_out, own_pair, other_pair, sum_up, sum_gain, sum_shift) = call(
        ffn_back_kernel,
        [order, *pieces[2], dpool, hidden, slope, up_all, out_all, proj_all, vec, first, norm_ffn, mixed, cotangent],
        [
            ((entries, 2048), LOW), ((entries, 512), F32), ((entries, 512), LOW), ((512, 512), F32),
            ((16, 32, 2048), F32), ((16, 32, 2048), LOW), ((8, 2048), F32), ((8, 512), F32), ((8, 512), F32),
        ],
        [((2048, 512), LOW), ((entries, 2048), LOW), ((512, 2048), F32), ((512, 2048), F32)],
        flops=4 * 10**9,
    )
    (grad_embeds, own_last, other_last) = call(
        attend_back_kernel,
        [order, flat, marks, qkv_all, vec, normed, normed0, query, keyval, probs, dmixed, dfirst, grad_out, sum_gain,
         sum_shift, sum_pool, sum_up],
        [((rows, 512), LOW), ((16, 16, 2176), F32), ((16, 16, 2176), LOW)],
        [
            ((128, 512), LOW), ((RB, 512), F32), ((RB, 512), F32), ((4 * RB, 128), F32), ((4 * RB, 128), F32), ((entries, 512), LOW), ((rows, 1024), LOW),
            ((entries, 512), F32), ((512, 1536), F32), ((16, 512), F32), ((144, 512), F32),
        ],
        flops=8 * 10**9,
    )
    if tuned:
        sum_down = scatter(own_down, other_down)
        pair = scatter(own_pair, other_pair)
        last = scatter(own_last, other_last)
        sum_proj, sum_up = pair[:16], pair[16:]
        sum_qkv, sum_out = last[:, :1536], last[:, 1536:2048]
        me = lax.axis_index("dp")
        sums = lax.dynamic_slice(last, (0, 2048 + 16 * (me % 8)), (13, 16))
        sum_upbias = lax.dynamic_slice(last, (13, 2048 + 64 * (me % 2)), (1, 64))[0]
    else:

        def share(own, other, axis=0):
            full = jnp.concatenate([own, other.astype(F32)])
            return lax.psum_scatter(full.reshape(-1, full.shape[-1]), "dp", scatter_dimension=0, tiled=True)

        sum_down = share(own_down, other_down)
        sum_proj = share(own_pair[:, :16], other_pair[:, :16])
        sum_up = share(own_pair[:, 16:], other_pair[:, 16:])
        sum_qkv = share(own_last[:, :, :1536], other_last[:, :, :1536])
        sum_out = share(own_last[:, :, 1536:2048], other_last[:, :, 1536:2048])
        small = jnp.concatenate([own_last[:, :, 2048:], other_last[:, :, 2048:].astype(F32)])
        vectors = jnp.concatenate([small[8 * k, :13] for k in range(4)], axis=1)
        sums = lax.psum_scatter(vectors, "dp", scatter_dimension=1, tiled=True)
        upbias = jnp.concatenate([small[2 * k, 13] for k in range(16)])
        sum_upbias = lax.psum_scatter(upbias, "dp", scatter_dimension=0, tiled=True)
    return (
        output,
        grad_embeds.reshape(entries, SLOTS, 512),
        sums[:8],
        sums[8],
        sums[9],
        sum_qkv,
        sum_out,
        sums[10],
        sums[11],
        sum_up,
        sum_upbias,
        sum_down,
        sums[12],
        sum_proj,
    )


def solution(mesh):
    placed = (
        P("dp", None, None),
        P("dp"),
        P("dp"),
        P(None, "dp"),
        P("dp"),
        P("dp"),
        P("dp", None),
        P("dp", None),
        P("dp"),
        P("dp"),
        P("dp", None),
        P("dp"),
        P("dp", None),
        P("dp"),
        P("dp", None),
        P("dp", None),
    )
    return jax.shard_map(
        on_device,
        mesh=mesh,
        in_specs=placed,
        out_specs=(
            P("dp", None),
            P("dp", None, None),
            P(None, "dp"),
            P("dp"),
            P("dp"),
            P("dp", None),
            P("dp", None),
            P("dp"),
            P("dp"),
            P("dp", None),
            P("dp"),
            P("dp", None),
            P("dp"),
            P("dp", None),
        ),
        check_vma=False,
    )
```

```python
import jax
import jax.numpy as jnp
from jax import lax
from jax.experimental import pallas as pl
from jax.experimental.pallas import tpu as pltpu
from jax.sharding import PartitionSpec as P

HEADS = 8
HEAD_DIM = 64
SLOTS = 8
SHARDS = 32
EB = 32
RB = EB * SLOTS
CH = 64
VMEM_LIMIT = 58 * 2**20
SCALE = HEAD_DIM ** (-0.5)
F32 = jnp.float32
LOW = jnp.bfloat16


def pairs(partner):
    return [(i, partner(i)) for i in range(32)]


CORE = pairs(lambda i: i ^ 1)
NEAR = pairs(lambda i: i ^ (2 if i % 2 == 0 else 4))
FAR = pairs(lambda i: i ^ (4 if i % 2 == 0 else 2))
ACROSS = pairs(lambda i: i ^ 6)
LAYER = {p: pairs(lambda i: i ^ (p << 3)) for p in (1, 2, 3)}


def send(value, to):
    return lax.ppermute(value, "dp", to)


def spread(value, *ways):
    return [send(value, way) for way in ways]


def tie(value, *after, every=False):
    tied = lax.optimization_barrier((value, *after))
    return tied if every else tied[0]


def side_by_side(parts, shape):
    total = None
    for row, column, part in parts:
        edges = [(row, shape[0] - row - part.shape[0], 0), (column, shape[1] - column - part.shape[1], 0)]
        padded = lax.pad(part, jnp.zeros((), part.dtype), edges)
        total = padded if total is None else total + padded
    return total


def side_by_side_lanes(parts):
    return jnp.concatenate(parts, axis=-1)


def widen(*values):
    total = values[0].astype(F32)
    for value in values[1:]:
        total = total + value.astype(F32)
    return total


class Sum:
    def __init__(self, own, other):
        self.own = own
        self.core = send(other, CORE)

    def first(self):
        part = widen(self.own[8:], self.core[8:]).astype(LOW)
        self.far = send(part, FAR)
        return part

    def second(self):
        part = widen(self.own[4:8], self.core[4:8], self.far[4:]).astype(LOW)
        self.near = send(part, NEAR)
        return part

    def total(self, at):
        return widen(self.own[at], self.core[at], self.far[at], self.near[at])

    def third(self):
        part = self.total(slice(1, 4, 2)).astype(LOW)
        self.beside = send(part, LAYER[1])
        return part

    def fourth(self):
        part = widen(self.total(2), self.beside[1]).astype(LOW)
        self.beyond = send(part, LAYER[2])
        return part

    def done(self):
        return widen(self.total(0), self.beside[0], self.beyond)


def shard_at(me, k, turned=False):
    if me is None:
        return k
    near = 2 + 2 * (me & 1)
    quads = [0, near, 6 - near, 6, 1, 7 - near, near + 1, 7]
    core, row, column = k // 16, k // 4 % 4, k % 4
    quad, layer = (4 * core + column, row) if turned else (4 * core + row, column)
    return me ^ quads[quad] ^ (layer << 3)


def dot(left, right):
    return jnp.dot(left, right, preferred_element_type=F32)


def dot_nt(left, right):
    return lax.dot_general(left, right, (((1,), (1,)), ((), ())), preferred_element_type=F32)


def dot_tn(left, right):
    return lax.dot_general(left, right, (((0,), (0,)), ((), ())), preferred_element_type=F32)


def iota(shape, axis):
    return lax.broadcasted_iota(jnp.int32, shape, axis)


def norm_parts(values):
    center = values - jnp.mean(values, axis=-1, keepdims=True)
    rate = lax.rsqrt(jnp.mean(center * center, axis=-1, keepdims=True) + 1e-05)
    return center * rate, rate


def norm_back(grad, unit, rate, gain):
    scaled = grad * gain
    return rate * (
        scaled
        - jnp.mean(scaled, axis=-1, keepdims=True)
        - unit * jnp.mean(scaled * unit, axis=-1, keepdims=True)
    )


def fold(values):
    rows, width = values.shape
    return jnp.sum(values.reshape(rows // 8, 8, width), axis=0)


def spread_heads(rows):
    tiled = jnp.concatenate([rows] * HEADS, axis=0)
    shape = (HEADS * EB, HEADS * HEAD_DIM)
    return jnp.where(iota(shape, 0) // EB == iota(shape, 1) // HEAD_DIM, tiled, jnp.zeros_like(tiled))


def pick_heads(full):
    parts = []
    for k in range(HEADS // 2):
        lanes = slice(128 * k, 128 * k + 128)
        even = full[2 * k * EB : (2 * k + 1) * EB, lanes]
        odd = full[(2 * k + 1) * EB : (2 * k + 2) * EB, lanes]
        parts.append(jnp.where(iota(even.shape, 1) < HEAD_DIM, even, odd))
    return jnp.concatenate(parts, axis=1)


def slots_first(ref, out, at):
    for k in range(4):
        out[at, 128 * k : 128 * k + 128] = ref[pl.ds(k * RB, EB, stride=SLOTS), :]


def put_first(ref, values):
    for k in range(4):
        ref[pl.ds(k * RB, EB, stride=SLOTS), :] = values[:, 128 * k : 128 * k + 128]


def put_tall(ref, start, values):
    for k in range(4):
        ref[pl.ds(k * RB + start, values.shape[0]), :] = values[:, 128 * k : 128 * k + 128]


def get_tall(ref, start, rows):
    return jnp.concatenate([ref[pl.ds(k * RB + start, rows), :] for k in range(4)], axis=1)


def block(i, rows):
    return pl.ds(pl.multiple_of(i * rows, rows), rows)


class Load:
    def __init__(self, source, buffer, sems, first, parts, box):
        self.buffer, self.parts, self.box = buffer, parts, box
        self.source, self.sems, self.first = source, sems, first
        for i in range(parts):
            self.copy(i).start()

    def copy(self, i):
        rows = self.buffer.shape[0] // self.parts
        at = block(i, rows) if self.parts > 1 else pl.ds(0, rows)
        if self.box is None:
            source = self.source.at[at]
        else:
            row, _rows, column, columns = self.box
            start = row + i * rows
            if not isinstance(start, int):
                start = pl.multiple_of(start, rows)
            source = self.source.at[pl.ds(start, rows), pl.ds(column, columns)]
        return pltpu.make_async_copy(source, self.buffer.at[at], self.sems.at[self.first + i])

    def part(self, i):
        self.copy(i).wait()

    def whole(self):
        for i in range(self.parts):
            self.copy(i).wait()
        return self.buffer


class Store:
    def __init__(self, target, buffer, sems, first, parts, row=0):
        self.buffer, self.parts, self.row = buffer, parts, row
        self.target, self.sems, self.first = target, sems, first

    def copy(self, i):
        rows = self.buffer.shape[0] // self.parts
        at = block(i, rows) if self.parts > 1 else pl.ds(0, rows)
        if self.row == 0:
            target = self.target.at[at]
        else:
            start = self.row + i * rows
            target = self.target.at[pl.ds(start if isinstance(start, int) else pl.multiple_of(start, rows), rows)]
        return pltpu.make_async_copy(self.buffer.at[at], target, self.sems.at[self.first + i])

    def part(self, i):
        self.copy(i).start()

    def send(self):
        for i in range(self.parts):
            self.copy(i).start()


def call(body, micros, me, near, loads, stores, scratch=(), after=(), into=None):
    far = pl.BlockSpec(memory_space=pltpu.HBM)
    given = [] if into is None or isinstance(into[0], tuple) else [into[0]]
    counts = [len(near), len(loads), len(after) + len(given), len(stores), len(loads), len(stores), len(scratch)]
    shapes = [shape for shape, _type, _parts in stores]
    if into is not None:
        shapes[0] = into[0] if not given else into[0].shape

    def kernel(me_ref, *refs):
        groups, at = [], 0
        for count in counts:
            groups.append(refs[at : at + count])
            at += count
        near_refs, sources, _unused, targets, in_buffers, out_buffers, rest = groups
        in_sems, out_sems, near_sem = refs[at:]
        first, reads = 0, []
        for (_array, parts, box), source, buffer in zip(loads, sources, in_buffers):
            reads.append(Load(source, buffer, in_sems, first, parts, box))
            first += parts
        first, writes = 0, []
        for (_shape, _type, parts), target, buffer in zip(stores, targets, out_buffers):
            row = target.shape[0] - buffer.shape[0] if given and not writes else 0
            writes.append(Store(target, buffer, out_sems, first, parts, row))
            first += parts
        body(None if me is None else me_ref[0], (near_refs, near_sem), reads, writes, rest)
        for write in writes:
            for i in range(write.parts):
                write.copy(i).wait()

    buffers = [(a.shape if box is None else (box[1], box[3]), a.dtype) for a, _parts, box in loads]
    buffers += [(s, t) for s, t, _parts in stores]
    return pl.pallas_call(
        kernel,
        out_shape=[jax.ShapeDtypeStruct(s, t) for s, (_shape, t, _parts) in zip(shapes, stores)],
        in_specs=[pl.BlockSpec(memory_space=pltpu.SMEM)]
        + [far] * (len(near) + len(loads))
        + [pl.BlockSpec(memory_space=pl.ANY)] * len(after)
        + [far] * len(given),
        out_specs=[far] * len(stores),
        scratch_shapes=[pltpu.VMEM(s, t) for s, t in buffers + list(scratch)]
        + [
            pltpu.SemaphoreType.DMA((max(1, sum(parts for _array, parts, _box in loads)),)),
            pltpu.SemaphoreType.DMA((max(1, sum(parts for _shape, _type, parts in stores)),)),
            pltpu.SemaphoreType.DMA((4,)),
        ],
        input_output_aliases={1 + len(near) + len(loads) + len(after): 0} if given else {},
        compiler_params=pltpu.CompilerParams(vmem_limit_bytes=VMEM_LIMIT),
        cost_estimate=pl.CostEstimate(flops=int(micros * 1.1e9), bytes_accessed=1000, transcendentals=0),
    )(jnp.zeros((1,), jnp.int32) if me is None else me, *near, *[a for a, _parts, _box in loads], *after, *given)


class Place:
    def __init__(self, me, pieces, target, sem, cut, turned=False):
        self.copies = []
        rows = target.shape[0] // SHARDS
        for i, piece in enumerate(pieces):
            for p in range(4):
                at = block(shard_at(me, 4 * i + p, turned), rows)
                copy = pltpu.make_async_copy(cut(piece.at[p]), target.at[at], sem)
                copy.start()
                self.copies.append(copy)

    def wait(self):
        for copy in self.copies:
            copy.wait()


def attend_kernel(me, near, reads, writes, scratch):
    marks, embeds = reads
    weights, vec, bias_up, base0, normed, normed0, query, keyval, probs, mixed = writes
    small, table, rows, tall, rows0, norm0 = scratch
    pieces, sem = near
    Place(me, pieces, weights.buffer, sem.at[0], lambda piece: piece).wait()
    small[...] = weights.buffer[:, 1536:].astype(F32).reshape(SHARDS, 16, 128)
    lane = iota((16, 128), 1)
    for k in range(4):
        tile = small[8 * k]
        for t in range(1, 8):
            tile = jnp.where(lane // 16 == t, pltpu.roll(small[8 * k + t], 16 * t, 1), tile)
        vec.buffer[:, 128 * k : 128 * k + 128] = tile
    lane = iota((16, 128), 1)
    for k in range(16):
        tile = jnp.where(lane < 64, small[2 * k], pltpu.roll(small[2 * k + 1], 64, 1))
        bias_up.buffer[:, 128 * k : 128 * k + 128] = jnp.broadcast_to(tile[13:14], (8, 128))
    for write in (weights, vec, bias_up):
        write.send()
    table[...] = jnp.zeros_like(table)
    table[0:8, :] = vec.buffer[0:8, :]
    gain, shift = vec.buffer[8:9, :], vec.buffer[9:10, :]
    marks.whole()
    blocks = embeds.buffer.shape[0] // RB

    def norm_pair(pair, _):
        embeds.part(pair)
        for half in range(2):
            b = 2 * pair + half
            rows[half] = dot(marks.buffer[block(b, RB), :], table[...].astype(LOW))
            for c in range(RB // CH):
                at = pl.ds(c * CH, CH)
                here = pl.ds(pl.multiple_of(b * RB + c * CH, CH), CH)
                base = embeds.buffer[here, :].astype(F32) + rows[half, at, :]
                put_tall(tall.at[half], c * CH, base)
                unit, _rate = norm_parts(base)
                value = unit * gain + shift
                put_tall(rows0.at[half], c * CH, value)
                normed.buffer[here, :] = value.astype(LOW)
            out = block(b, EB)
            slots_first(tall.at[half], base0.buffer, out)
            slots_first(rows0.at[half], norm0, out)
            keyval.buffer[block(b, RB), :] = dot(normed.buffer[block(b, RB), :], weights.buffer[:, 512:1536]).astype(LOW)
        normed.part(pair)
        keyval.part(pair)
        return 0

    lax.fori_loop(0, blocks // 2, norm_pair, 0)
    normed0.buffer[...] = norm0[...].astype(LOW)
    query.buffer[...] = dot(normed0.buffer[...], weights.buffer[:, :512]).astype(LOW)
    normed0.send()
    query.send()
    base0.send()
    shape = (RB, HEADS * EB)
    match = iota(shape, 0) // SLOTS == iota(shape, 1) % EB
    liver = jnp.where(iota((128, HEADS * EB), 0) == 8, 1.0, 0.0).astype(LOW)

    def attend_pair(pair, _):
        for half in range(2):
            b = 2 * pair + half
            at, out = block(b, RB), block(b, EB)
            scores = dot_nt(keyval.buffer[at, :512], spread_heads(query.buffer[out, :])) * SCALE
            live = dot(marks.buffer[at, :], liver) > 0.5
            scores = jnp.where(live, scores, -1000000000.0).reshape(EB, SLOTS, HEADS * EB)
            top = jnp.max(scores, axis=1, keepdims=True)
            power = jnp.exp(scores - top)
            part = (power / jnp.sum(power, axis=1, keepdims=True)).reshape(shape)
            low = jnp.where(match, part, 0.0).astype(LOW)
            probs.buffer[at, :] = low
            mixed.buffer[out, :] = pick_heads(dot_tn(low, keyval.buffer[at, 512:])).astype(LOW)
        probs.part(pair)
        return 0

    lax.fori_loop(0, blocks // 2, attend_pair, 0)
    mixed.send()


def ffn_kernel(me, near, reads, writes, scratch):
    cotangent, base0, mixed, vec, bias_up = reads
    output, dfirst, dmixed, sum_up, sum_gain, sum_shift, sum_pool, own_down, other_down, own, other = writes
    w_proj, w_up, w_down, w_out, first, norm_ffn, dpool, hidden, slope, pre_low, total = scratch
    pieces, sem = near
    out = Place(me, pieces[8:], w_out, sem.at[3], lambda piece: piece.at[pl.ds(64, 16)], turned=True)
    proj = Place(me, pieces[:8], w_proj, sem.at[0], lambda piece: piece.at[pl.ds(0, 16)])
    up = Place(me, pieces[:8], w_up, sem.at[1], lambda piece: piece.at[pl.ds(16, 16)])
    down = Place(me, pieces[8:], w_down, sem.at[2], lambda piece: piece.at[pl.ds(0, 64)], turned=True)

    def share(mine, theirs, row, rows, lanes, base=0):
        for k in range(SHARDS):
            half = mine if k < 16 else theirs
            half.buffer[k % 16, row : row + rows, lanes] = total[block(base + shard_at(me, k), rows), :].astype(LOW)

    for read in (base0, mixed, vec):
        read.whole()
    out.wait()
    first[...] = base0.buffer[...] + dot(mixed.buffer[...], w_out[...])
    for c in range(first.shape[0] // CH):
        at = pl.ds(c * CH, CH)
        unit, _rate = norm_parts(first[at, :])
        norm_ffn[at, :] = (unit * vec.buffer[10:11, :] + vec.buffer[11:12, :]).astype(LOW)
    cotangent.whole()
    proj.wait()
    grad = dot_nt(cotangent.buffer[...], w_proj[...])
    dpool[...] = grad
    sum_pool.buffer[...] = fold(grad)
    low = grad.astype(LOW)
    bias_up.whole()
    up.wait()
    for k in range(8):
        lanes = slice(256 * k, 256 * k + 256)
        pre = dot(norm_ffn[...], w_up[:, lanes])
        rows = pre.shape[0] // 4
        for c in range(4):
            at = slice(rows * c, rows * c + rows)
            value = pre[at] + bias_up.buffer[0:1, lanes]
            below = 0.5 * (1.0 + lax.erf(value * (0.5**0.5)))
            hidden[at, lanes] = (value * below).astype(LOW)
            slope[at, lanes] = below + value * (jnp.exp(-0.5 * value * value) * 0.3989422804014327)
        total[256 * k : 256 * k + 256, :] = dot_tn(hidden[:, lanes], low)
    share(own_down, other_down, 0, 64, slice(0, 512))
    other_down.send()
    own_down.send()
    down.wait()
    for k in range(8):
        lanes = slice(256 * k, 256 * k + 256)
        dpre = slope[:, lanes] * dot_nt(low, w_down[lanes, :])
        sum_up.buffer[:, lanes] = fold(dpre)
        pre_low[:, lanes] = dpre.astype(LOW)
    dfirst.buffer[...] = dot_nt(pre_low[...], w_up[...])
    gains = jnp.zeros((8, 512), F32)
    shifts = jnp.zeros((8, 512), F32)
    for c in range(first.shape[0] // CH):
        at = slice(CH * c, CH * c + CH)
        grad = dfirst.buffer[at, :]
        unit, rate = norm_parts(first[at, :])
        gains += fold(grad * unit)
        shifts += fold(grad)
        dfirst.buffer[at, :] = norm_back(grad, unit, rate, vec.buffer[10:11, :]) + dpool[at, :]
    sum_gain.buffer[...] = gains
    sum_shift.buffer[...] = shifts
    dmixed.buffer[...] = dot_nt(dfirst.buffer[...].astype(LOW), w_out[...]).astype(LOW)
    for write in (dfirst, dmixed, sum_up, sum_gain, sum_shift, sum_pool):
        write.send()
    pooled = (first[...] + dot(hidden[...], w_down[...]) + vec.buffer[12:13, :]).astype(LOW)
    for k in range(4):
        lanes = slice(512 * k, 512 * k + 512)
        total[:512, :] = dot_tn(pooled, cotangent.buffer[:, lanes])
        share(own, other, 0, 16, lanes)
        total[512:1024, :] = dot_tn(norm_ffn[...], pre_low[:, lanes])
        share(own, other, 16, 16, lanes, SHARDS)
        output.buffer[:, lanes] = dot(pooled, w_proj[:, lanes]).astype(LOW)
    other.send()
    own.send()
    output.send()


def attend_back_kernel(me, _near, reads, writes, scratch):
    dmixed, query, probs, keyval, weights = reads
    dkeyval, dquery, query_part = writes
    dmixed.whole()
    query.whole()

    def attend_pair(pair, _):
        probs.part(pair)
        keyval.part(pair)
        for half in range(2):
            b = 2 * pair + half
            at, out = block(b, RB), block(b, EB)
            low = probs.buffer[at, :]
            part = low.astype(F32)
            dmix = spread_heads(dmixed.buffer[out, :])
            grad = dot_nt(keyval.buffer[at, 512:], dmix)
            shape = (EB, SLOTS, HEADS * EB)
            whole = jnp.sum((part * grad).reshape(shape), axis=1, keepdims=True)
            dscores = (part.reshape(shape) * (grad.reshape(shape) - whole)).reshape(RB, HEADS * EB).astype(LOW)
            dkeyval.buffer[at, 512:] = dot(low, dmix).astype(LOW)
            dkeyval.buffer[at, :512] = (dot(dscores, spread_heads(query.buffer[out, :])) * SCALE).astype(LOW)
            dquery.buffer[out, :] = (pick_heads(dot_tn(dscores, keyval.buffer[at, :512])) * SCALE).astype(LOW)
        dkeyval.part(pair)
        return 0

    lax.fori_loop(0, keyval.buffer.shape[0] // RB // 2, attend_pair, 0)
    dquery.send()
    query_part.buffer[...] = dot_nt(dquery.buffer[...], weights.whole()[...])
    query_part.send()


def grad_qkv_kernel(me, _near, reads, writes, scratch):
    mixed, dfirst, normed0, dquery, normed, dkeyval = reads
    own, other = writes
    grad_qkv, grad_out = scratch
    grad_out[...] = dot_tn(mixed.whole()[...], dfirst.whole()[...].astype(LOW))
    grad_qkv[:, :512] = dot_tn(normed0.whole()[...], dquery.whole()[...])
    normed.whole()
    dkeyval.whole()
    for k in range(4):
        lanes = slice(256 * k, 256 * k + 256)
        grad_qkv[:, 512 + 256 * k : 768 + 256 * k] = dot_tn(normed.buffer[...], dkeyval.buffer[:, lanes])
    for i in range(16):
        for k, half in ((i, own.buffer), (16 + i, other.buffer)):
            at = block(shard_at(me, k), 16)
            half[i, :, :1536] = grad_qkv[at, :].astype(half.dtype)
            half[i, :, 1536:2048] = grad_out[at, :].astype(half.dtype)
    other.send()
    own.send()


def norm_back_kernel(me, _near, reads, writes, scratch):
    vec, query_part, dfirst, marks, weights, dkeyval, embeds, *more = reads
    grad_embeds, *results = writes
    table, rows, work, lower, spread_query, spread_first, small, sums = scratch
    for read in (weights, query_part, dfirst, vec, marks):
        read.whole()
    table[...] = jnp.zeros_like(table)
    table[0:8, :] = vec.buffer[0:8, :].astype(LOW)
    sums[...] = jnp.zeros_like(sums)
    spread_query[...] = jnp.zeros_like(spread_query)
    spread_first[...] = jnp.zeros_like(spread_first)
    gain = vec.buffer[8:9, :]

    def norm_pair(pair, _):
        dkeyval.part(pair)
        embeds.part(pair)
        for half in range(2):
            b = 2 * pair + half
            at, out = block(b, RB), block(b, EB)
            put_first(spread_query.at[half], query_part.buffer[out, :])
            put_first(spread_first.at[half], dfirst.buffer[out, :])
            rows[half] = dot(marks.buffer[at, :], table[...])
            work[half] = dot_nt(dkeyval.buffer[at, :], weights.buffer[...])
            gains, shifts = jnp.zeros((8, 512), F32), jnp.zeros((8, 512), F32)
            for c in range(RB // CH):
                local = pl.ds(c * CH, CH)
                here = pl.ds(pl.multiple_of(b * RB + c * CH, CH), CH)
                grad = work[half, local, :] + get_tall(spread_query.at[half], c * CH, CH)
                unit, rate = norm_parts(embeds.buffer[here, :].astype(F32) + rows[half, local, :])
                gains += fold(grad * unit)
                shifts += fold(grad)
                value = norm_back(grad, unit, rate, gain) + get_tall(spread_first.at[half], c * CH, CH)
                high = value.astype(LOW)
                grad_embeds.buffer[here, :] = high
                lower[half, local, :] = (value - high.astype(F32)).astype(LOW)
            sums[half, 0:8, :] += gains
            sums[half, 8:16, :] += shifts
            mark = marks.buffer[at, :]
            sums[half, 16:144, :] += dot_tn(mark, grad_embeds.buffer[at, :]) + dot_tn(mark, lower[half])
        grad_embeds.part(pair)
        return 0

    lax.fori_loop(0, embeds.buffer.shape[0] // RB // 2, norm_pair, 0)
    if not more:
        results[0].buffer[...] = sums[0] + sums[1]
        results[0].send()
        return
    before, gain_ffn, shift_ffn, pool, up = more
    own, other = results
    sums[0] = sums[0] + sums[1] + before.whole()[...]
    small[...] = jnp.zeros_like(small)
    small[0:8, :] = sums[0, 16:24, :]
    folded = (sums[0, 0:8, :], sums[0, 8:16, :], gain_ffn.whole()[...], shift_ffn.whole()[...], pool.whole()[...])
    for i, value in enumerate(folded):
        small[8 + i : 9 + i, :] = jnp.sum(value, axis=0, keepdims=True)
    up_row = jnp.sum(up.whole()[...], axis=0, keepdims=True)
    row = iota((16, 128), 0)
    for r in range(SHARDS):
        tile = small[:, 128 * (r // 8) : 128 * (r // 8) + 128]
        tile = jnp.where(row == 13, up_row[:, 128 * (r // 2) : 128 * (r // 2) + 128], tile)
        rows[0, 8 * r : 8 * r + 8, 0:128] = tile[0:8]
        rows[0, 8 * r : 8 * r + 8, 128:256] = tile[8:16]
    for i in range(16):
        for k, half in ((i, own.buffer), (16 + i, other.buffer)):
            at = block(shard_at(me, k), 8)
            half[i] = jnp.concatenate([rows[0, at, 0:128], rows[0, at, 128:256]]).astype(half.dtype)
    other.send()
    own.send()


def on_device(
    embeds,
    piece_counts,
    group_ids,
    group_table,
    gain_attn,
    shift_attn,
    w_qkv,
    w_out,
    gain_ffn,
    shift_ffn,
    w_up,
    bias_up,
    w_down,
    bias_down,
    w_proj,
    cotangent,
):
    tuned = lax.axis_size("dp") == 32
    entries = embeds.shape[0]
    rows = entries * SLOTS
    flat = embeds.reshape(rows, 512)
    lane = jnp.arange(128, dtype=jnp.int32)
    slot = jnp.arange(SLOTS, dtype=jnp.int32)
    vectors = [gain_attn, shift_attn, gain_ffn, shift_ffn, bias_down]
    later = [embeds]
    if tuned:
        me = lax.axis_index("dp").astype(jnp.int32).reshape(1)
        parts = [(0, 0, w_qkv), (0, 1536, group_table), (13, 1536, bias_up[None, :])]
        parts += [(8 + i, 1536, vector[None, :]) for i, vector in enumerate(vectors)]
        shard = side_by_side(parts, (16, 1664))
        own = jnp.stack([shard, *spread(shard, LAYER[1], LAYER[2], LAYER[3])])
        third = side_by_side([(0, 0, w_down), (64, 0, w_out)], (80, 512))
        quad = [third, *spread(third, NEAR, FAR, ACROSS)]
        mine = [own, *spread(own, NEAR, FAR, ACROSS)]
        pieces = [mine + [send(part, CORE) for part in mine]]
        shard = side_by_side([(0, 0, w_proj), (16, 0, w_up)], (32, 2048))
        upper, lower = spread(shard, LAYER[2], LAYER[1])
        quad = jnp.stack([tie(third, own), *quad[1:]])
        own2 = jnp.stack([tie(shard, quad), lower, upper, send(tie(upper, own), LAYER[1])])
        pieces.append([own2, *spread(own2, NEAR, FAR, ACROSS)])
        pieces.append([quad, *spread(quad, LAYER[1], LAYER[2], LAYER[3])])
        later = [tie(own2, quad)]
        group_ids, piece_counts = tie(group_ids, piece_counts, own, every=True)[:2]
    else:
        me = None

        def whole(shard, axis=0):
            return lax.all_gather(shard, "dp", axis=axis, tiled=True)

        def cut(full):
            return [full[4 * i : 4 * i + 4] for i in range(8)]

        gathered = whole(jnp.concatenate([group_table, jnp.stack(vectors)]), 1)
        gathered = jnp.transpose(gathered.reshape(13, SHARDS, 16), (1, 0, 2))
        small = jnp.concatenate(
            [
                jnp.pad(gathered, ((0, 0), (0, 0), (0, 112))),
                jnp.pad(whole(bias_up).reshape(SHARDS, 1, 64), ((0, 0), (0, 2), (0, 64))),
            ],
            axis=1,
        )
        pieces = [
            cut(
                jnp.concatenate(
                    [whole(w_qkv).reshape(SHARDS, 16, 1536), small], axis=2
                )
            ),
            cut(
                jnp.concatenate(
                    [whole(w_proj).reshape(SHARDS, 16, 2048), whole(w_up).reshape(SHARDS, 16, 2048)], axis=1
                )
            ),
            cut(
                jnp.concatenate([whole(w_down).reshape(SHARDS, 64, 512), whole(w_out).reshape(SHARDS, 16, 512)], axis=1)
            ),
        ]
    marks = jnp.where(
        lane[None, None, :] < 8,
        group_ids[:, None, None] == lane[None, None, :],
        slot[None, :, None] < piece_counts[:, None, None],
    )
    marks = marks.astype(LOW).reshape(rows, 128)
    steps = rows // RB // 2
    low, wide = LOW, F32
    (qkv_all, vec, upbias, base0, normed, normed0, query, keyval, probs, mixed) = call(
        attend_kernel, 15,
        me,
        pieces[0],
        [(marks, 1, None), (flat, steps, None)],
        [
            ((512, 1664), low, 1), ((16, 512), wide, 1), ((8, 2048), wide, 1), ((entries, 512), wide, 1),
            ((rows, 512), low, steps), ((entries, 512), low, 1), ((entries, 512), low, 1), ((rows, 1024), low, steps),
            ((rows, HEADS * EB), low, steps), ((entries, 512), low, 1),
        ],
        scratch=[
            ((32, 16, 128), wide), ((128, 512), wide), ((2, RB, 512), wide), ((2, 4 * RB, 128), wide),
            ((2, 4 * RB, 128), wide), ((entries, 512), wide),
        ],
        after=later,
    )
    if tuned:
        mixed, *came = tie(mixed, *pieces[1], *pieces[2], every=True)
        came += [send(part, CORE) for part in came]
        pieces[1:] = [came[0:4] + came[8:12], came[4:8] + came[12:16]]
    (
        output, dfirst, dmixed, sum_up, sum_gain, sum_shift, sum_pool, own_down, other_down, own_pair, other_pair
    ) = call(
        ffn_kernel, 14,
        me,
        [*pieces[1], *pieces[2]],
        [
            (cotangent, 1, None), (base0, 1, None), (mixed, 1, None), (vec, 1, None), (upbias, 1, None),
        ],
        [
            ((entries, 2048), low, 1), ((entries, 512), wide, 1), ((entries, 512), low, 1), ((8, 2048), wide, 1),
            ((8, 512), wide, 1), ((8, 512), wide, 1), ((8, 512), wide, 1), ((16, 64, 512), low, 1),
            ((16, 64, 512), low, 1), ((16, 32, 2048), low, 1), ((16, 32, 2048), low, 1),
        ],
        [
            ((512, 2048), low), ((512, 2048), low), ((2048, 512), low), ((512, 512), low), ((entries, 512), wide),
            ((entries, 512), low), ((entries, 512), wide), ((entries, 2048), low),
            ((entries, 2048), wide), ((entries, 2048), low), ((2048, 512), wide),
        ],
    )
    if tuned:
        down = Sum(own_down, other_down)
        pair = Sum(own_pair, other_pair)
    (dkeyval, dquery, query_part) = call(
        attend_back_kernel, 8,
        me,
        [],
        [
            (dmixed, 1, None), (query, 1, None), (probs, steps, None), (keyval, steps, None),
            (qkv_all, 1, (0, 512, 0, 512)),
        ],
        [((rows, 1024), low, steps), ((entries, 512), low, 1), ((entries, 512), wide, 1)],
    )
    part = own_pair
    if tuned:
        query_part, down.core, pair.core = tie(query_part, down.core, pair.core, every=True)
        part = down.first()
        pair.core = tie(pair.core, part)
        part = pair.first()
    (own_last, other_last) = call(
        grad_qkv_kernel, 7,
        me,
        [],
        [
            (mixed, 1, None), (dfirst, 1, None), (normed0, 1, None), (dquery, 1, None), (normed, 1, None),
            (dkeyval, steps, None),
        ],
        [((16, 16, 2048), low, 1), ((16, 16, 2048), low, 1)],
        [((512, 1536), wide), ((512, 512), wide)],
        after=[part],
    )
    if tuned:
        last = Sum(own_last, other_last)

    def norm_back(start, count, more, stores, after, into):
        return call(
            norm_back_kernel, 6.6,
            me,
            [],
            [
                (vec, 1, None), (query_part, 1, (start // 8, count // 8, 0, 512)),
                (dfirst, 1, (start // 8, count // 8, 0, 512)), (marks, 1, (start, count, 0, 128)),
                (qkv_all, 1, (0, 512, 512, 1024)), (dkeyval, steps // 2, (start, count, 0, 1024)),
                (flat, steps // 2, (start, count, 0, 512)), *[(array, 1, None) for array in more],
            ],
            [((count, 512), low, steps // 2), *stores],
            [
                ((128, 512), low), ((2, RB, 512), wide), ((2, RB, 512), wide), ((2, RB, 512), low),
                ((2, 4 * RB, 128), wide), ((2, 4 * RB, 128), wide), ((16, 512), wide), ((2, 144, 512), wide),
            ],
            after=after,
            into=into,
        )

    half = rows // 2
    (grad_embeds, half_sums) = norm_back(0, half, [], [((144, 512), wide, 1)], [other_last], ((rows, 512), half))
    part = half_sums
    if tuned:
        half_sums, down.far, last.core = tie(half_sums, down.far, last.core, every=True)
        part = last.first()
        down.far = tie(down.far, part)
        part = down.second()
    (grad_embeds, own_small, other_small) = norm_back(
        half,
        half,
        [half_sums, sum_gain, sum_shift, sum_pool, sum_up],
        [((16, 16, 128), low, 1), ((16, 16, 128), low, 1)],
        [part],
        (grad_embeds, half),
    )
    if tuned:
        other_small, pair.far, down.near = tie(other_small, pair.far, down.near, every=True)
        little = Sum(own_small, other_small)
        part = pair.second()
        down.near = tie(down.near, part)
        part = down.third()
        little.core = tie(little.core, part)
        part = little.first()
        last.far, little.far = tie(last.far, little.far, part, every=True)[:2]
        near = [widen(sums.own[4:8], sums.core[4:8], sums.far[4:]).astype(LOW) for sums in (last, little)]
        near = side_by_side_lanes(near)
        came = send(near, NEAR)
        pair.near = tie(pair.near, near)
        part = pair.third()
        down.beside = tie(down.beside, part)
        part = down.fourth()
        came = tie(came, part)
        last.near, little.near = came[:, :, :2048], came[:, :, 2048:]
        near = side_by_side_lanes([sums.total(slice(1, 4, 2)).astype(LOW) for sums in (last, little)])
        came = send(near, LAYER[1])
        pair.beside = tie(pair.beside, near)
        part = pair.fourth()
        came = tie(came, part)
        last.beside, little.beside = came[:, :, :2048], came[:, :, 2048:]
        near = side_by_side_lanes([widen(sums.total(2), sums.beside[1]).astype(LOW) for sums in (last, little)])
        came = send(near, LAYER[2])
        down.beyond, pair.beyond = tie(down.beyond, pair.beyond, near, every=True)[:2]
        sum_down, pair = down.done(), pair.done()
        came = tie(came, sum_down, pair)
        last.beyond, little.beyond = came[:, :2048], came[:, 2048:]
        last_small = little.done()
        sum_proj, sum_up = pair[:16], pair[16:]
        sum_qkv, sum_out = [
            widen(last.total(0)[:, at], last.beside[0][:, at], last.beyond[:, at])
            for at in (slice(0, 1536), slice(1536, 2048))
        ]
        me = lax.axis_index("dp")
        sums = lax.dynamic_slice(last_small, (0, 16 * (me % 8)), (13, 16))
        sum_upbias = lax.dynamic_slice(last_small, (13, 64 * (me % 2)), (1, 64))[0]
    else:

        def share(own, other, axis=0):
            full = jnp.concatenate([own, other.astype(F32)])
            return lax.psum_scatter(full.reshape(-1, full.shape[-1]), "dp", scatter_dimension=0, tiled=True)

        sum_down = share(own_down, other_down)
        sum_proj = share(own_pair[:, :16], other_pair[:, :16])
        sum_up = share(own_pair[:, 16:], other_pair[:, 16:])
        sum_qkv = share(own_last[:, :, :1536], other_last[:, :, :1536])
        sum_out = share(own_last[:, :, 1536:], other_last[:, :, 1536:])
        small = jnp.concatenate([own_small, other_small.astype(F32)])
        vectors = jnp.concatenate([small[8 * k, :13] for k in range(4)], axis=1)
        sums = lax.psum_scatter(vectors, "dp", scatter_dimension=1, tiled=True)
        upbias = jnp.concatenate([small[2 * k, 13] for k in range(16)])
        sum_upbias = lax.psum_scatter(upbias, "dp", scatter_dimension=0, tiled=True)
    return (
        output,
        grad_embeds.reshape(entries, SLOTS, 512),
        sums[:8],
        sums[8],
        sums[9],
        sum_qkv,
        sum_out,
        sums[10],
        sums[11],
        sum_up,
        sum_upbias,
        sum_down,
        sums[12],
        sum_proj,
    )


def solution(mesh):
    placed = (
        P("dp", None, None),
        P("dp"),
        P("dp"),
        P(None, "dp"),
        P("dp"),
        P("dp"),
        P("dp", None),
        P("dp", None),
        P("dp"),
        P("dp"),
        P("dp", None),
        P("dp"),
        P("dp", None),
        P("dp"),
        P("dp", None),
        P("dp", None),
    )
    return jax.shard_map(
        on_device,
        mesh=mesh,
        in_specs=placed,
        out_specs=(
            P("dp", None),
            P("dp", None, None),
            P(None, "dp"),
            P("dp"),
            P("dp"),
            P("dp", None),
            P("dp", None),
            P("dp"),
            P("dp"),
            P("dp", None),
            P("dp"),
            P("dp", None),
            P("dp"),
            P("dp", None),
        ),
        check_vma=False,
    )
```

```python
import jax
import jax.numpy as jnp
from jax import lax
from jax.experimental import pallas as pl
from jax.experimental.pallas import tpu as pltpu
from jax.sharding import PartitionSpec as P

HEADS = 8
HEAD_DIM = 64
SLOTS = 8
SHARDS = 32
EB = 32
RB = EB * SLOTS
CH = 64
VMEM_LIMIT = 58 * 2**20
SCALE = HEAD_DIM ** (-0.5)
F32 = jnp.float32
LOW = jnp.bfloat16


def pairs(partner):
    return [(i, partner(i)) for i in range(32)]


CORE = pairs(lambda i: i ^ 1)
NEAR = pairs(lambda i: i ^ (2 if i % 2 == 0 else 4))
FAR = pairs(lambda i: i ^ (4 if i % 2 == 0 else 2))
ACROSS = pairs(lambda i: i ^ 6)
LAYER = {p: pairs(lambda i: i ^ (p << 3)) for p in (1, 2, 3)}


def send(value, to):
    return lax.ppermute(value, "dp", to)


def spread(value, *ways):
    return [send(value, way) for way in ways]


def tie(value, *after, every=False):
    tied = lax.optimization_barrier((value, *after))
    return tied if every else tied[0]


def side_by_side(parts, shape):
    total = None
    for row, column, part in parts:
        edges = [(row, shape[0] - row - part.shape[0], 0), (column, shape[1] - column - part.shape[1], 0)]
        padded = lax.pad(part, jnp.zeros((), part.dtype), edges)
        total = padded if total is None else total + padded
    return total


def side_by_side_lanes(parts):
    return jnp.concatenate(parts, axis=-1)


def widen(*values):
    total = values[0].astype(F32)
    for value in values[1:]:
        total = total + value.astype(F32)
    return total


class Sum:
    def __init__(self, own, low, high):
        self.own = own
        self.high = send(high, CORE)
        self.low = send(low, CORE)

    def first(self):
        part = widen(self.own[8:], self.high).astype(LOW)
        self.far = send(part, FAR)
        return part

    def second(self):
        part = widen(self.own[4:8], self.low[4:], self.far[4:]).astype(LOW)
        self.near = send(part, NEAR)
        return part

    def total(self, at):
        return widen(self.own[at], self.low[at], self.far[at], self.near[at])

    def third(self):
        part = self.total(slice(1, 4, 2)).astype(LOW)
        self.beside = send(part, LAYER[1])
        return part

    def fourth(self):
        part = widen(self.total(2), self.beside[1]).astype(LOW)
        self.beyond = send(part, LAYER[2])
        self.rest = tie(widen(self.total(0), self.beside[0]), part)
        return part

    def done(self):
        return widen(self.rest, self.beyond)


def shard_at(me, k, turned=False):
    if me is None:
        return k
    near = 2 + 2 * (me & 1)
    quads = [0, near, 6 - near, 6, 1, 7 - near, near + 1, 7]
    core, row, column = k // 16, k // 4 % 4, k % 4
    quad, layer = (4 * core + column, row) if turned else (4 * core + row, column)
    return me ^ quads[quad] ^ (layer << 3)


def dot(left, right):
    return jnp.dot(left, right, preferred_element_type=F32)


def dot_nt(left, right):
    return lax.dot_general(left, right, (((1,), (1,)), ((), ())), preferred_element_type=F32)


def dot_tn(left, right):
    return lax.dot_general(left, right, (((0,), (0,)), ((), ())), preferred_element_type=F32)


def iota(shape, axis):
    return lax.broadcasted_iota(jnp.int32, shape, axis)


def norm_parts(values):
    center = values - jnp.mean(values, axis=-1, keepdims=True)
    rate = lax.rsqrt(jnp.mean(center * center, axis=-1, keepdims=True) + 1e-05)
    return center * rate, rate


def norm_back(grad, unit, rate, gain):
    scaled = grad * gain
    return rate * (
        scaled
        - jnp.mean(scaled, axis=-1, keepdims=True)
        - unit * jnp.mean(scaled * unit, axis=-1, keepdims=True)
    )


def fold(values):
    rows, width = values.shape
    return jnp.sum(values.reshape(rows // 8, 8, width), axis=0)


def spread_heads(rows):
    tiled = jnp.concatenate([rows] * HEADS, axis=0)
    shape = (HEADS * EB, HEADS * HEAD_DIM)
    return jnp.where(iota(shape, 0) // EB == iota(shape, 1) // HEAD_DIM, tiled, jnp.zeros_like(tiled))


def pick_heads(full):
    parts = []
    for k in range(HEADS // 2):
        lanes = slice(128 * k, 128 * k + 128)
        even = full[2 * k * EB : (2 * k + 1) * EB, lanes]
        odd = full[(2 * k + 1) * EB : (2 * k + 2) * EB, lanes]
        parts.append(jnp.where(iota(even.shape, 1) < HEAD_DIM, even, odd))
    return jnp.concatenate(parts, axis=1)


def slots_first(ref, out, at):
    for k in range(4):
        out[at, 128 * k : 128 * k + 128] = ref[pl.ds(k * RB, EB, stride=SLOTS), :]


def put_first(ref, values):
    for k in range(4):
        ref[pl.ds(k * RB, EB, stride=SLOTS), :] = values[:, 128 * k : 128 * k + 128]


def put_tall(ref, start, values):
    for k in range(4):
        ref[pl.ds(k * RB + start, values.shape[0]), :] = values[:, 128 * k : 128 * k + 128]


def get_tall(ref, start, rows):
    return jnp.concatenate([ref[pl.ds(k * RB + start, rows), :] for k in range(4)], axis=1)


def block(i, rows):
    return pl.ds(pl.multiple_of(i * rows, rows), rows)


class Load:
    def __init__(self, source, buffer, sems, first, parts, box):
        self.buffer, self.parts, self.box = buffer, parts, box
        self.source, self.sems, self.first = source, sems, first
        for i in range(parts):
            self.copy(i).start()

    def copy(self, i):
        rows = self.buffer.shape[0] // self.parts
        at = block(i, rows) if self.parts > 1 else pl.ds(0, rows)
        if self.box is None:
            source = self.source.at[at]
        else:
            row, _rows, column, columns = self.box
            start = row + i * rows
            if not isinstance(start, int):
                start = pl.multiple_of(start, rows)
            source = self.source.at[pl.ds(start, rows), pl.ds(column, columns)]
        return pltpu.make_async_copy(source, self.buffer.at[at], self.sems.at[self.first + i])

    def part(self, i):
        self.copy(i).wait()

    def whole(self):
        for i in range(self.parts):
            self.copy(i).wait()
        return self.buffer


class Store:
    def __init__(self, target, buffer, sems, first, parts):
        self.buffer, self.parts = buffer, parts
        self.target, self.sems, self.first = target, sems, first

    def copy(self, i):
        rows = self.buffer.shape[0] // self.parts
        at = block(i, rows) if self.parts > 1 else pl.ds(0, rows)
        return pltpu.make_async_copy(self.buffer.at[at], self.target.at[at], self.sems.at[self.first + i])

    def part(self, i):
        self.copy(i).start()

    def send(self):
        for i in range(self.parts):
            self.copy(i).start()


def call(body, micros, me, near, loads, stores, scratch=(), after=()):
    far = pl.BlockSpec(memory_space=pltpu.HBM)
    counts = [len(near), len(loads), len(after), len(stores), len(loads), len(stores), len(scratch)]

    def kernel(me_ref, *refs):
        groups, at = [], 0
        for count in counts:
            groups.append(refs[at : at + count])
            at += count
        near_refs, sources, _unused, targets, in_buffers, out_buffers, rest = groups
        in_sems, out_sems, near_sem = refs[at:]
        first, reads = 0, []
        for (_array, parts, box), source, buffer in zip(loads, sources, in_buffers):
            reads.append(Load(source, buffer, in_sems, first, parts, box))
            first += parts
        first, writes = 0, []
        for (_shape, _type, parts), target, buffer in zip(stores, targets, out_buffers):
            writes.append(Store(target, buffer, out_sems, first, parts))
            first += parts
        body(None if me is None else me_ref[0], (near_refs, near_sem), reads, writes, rest)
        for write in writes:
            for i in range(write.parts):
                write.copy(i).wait()

    buffers = [(a.shape if box is None else (box[1], box[3]), a.dtype) for a, _parts, box in loads]
    buffers += [(s, t) for s, t, _parts in stores]
    return pl.pallas_call(
        kernel,
        out_shape=[jax.ShapeDtypeStruct(s, t) for s, t, _parts in stores],
        in_specs=[pl.BlockSpec(memory_space=pltpu.SMEM)]
        + [far] * (len(near) + len(loads))
        + [pl.BlockSpec(memory_space=pl.ANY)] * len(after),
        out_specs=[far] * len(stores),
        scratch_shapes=[pltpu.VMEM(s, t) for s, t in buffers + list(scratch)]
        + [
            pltpu.SemaphoreType.DMA((max(1, sum(parts for _array, parts, _box in loads)),)),
            pltpu.SemaphoreType.DMA((max(1, sum(parts for _shape, _type, parts in stores)),)),
            pltpu.SemaphoreType.DMA((4,)),
        ],
        compiler_params=pltpu.CompilerParams(vmem_limit_bytes=VMEM_LIMIT),
        cost_estimate=pl.CostEstimate(flops=int(micros * 1.1e9), bytes_accessed=1000, transcendentals=0),
    )(jnp.zeros((1,), jnp.int32) if me is None else me, *near, *[a for a, _parts, _box in loads], *after)


class Place:
    def __init__(self, me, pieces, target, sem, cut, turned=False):
        self.copies = []
        rows = target.shape[0] // SHARDS
        for i, piece in enumerate(pieces):
            for p in range(4):
                at = block(shard_at(me, 4 * i + p, turned), rows)
                copy = pltpu.make_async_copy(cut(piece.at[p]), target.at[at], sem)
                copy.start()
                self.copies.append(copy)

    def wait(self):
        for copy in self.copies:
            copy.wait()


def attend_kernel(me, near, reads, writes, scratch):
    marks, embeds = reads
    weights, vec, bias_up, base0, normed, normed0, query, keyval, probs, mixed = writes
    small, table, rows, tall, rows0, norm0 = scratch
    pieces, sem = near
    Place(me, pieces, weights.buffer, sem.at[0], lambda piece: piece).wait()
    small[...] = weights.buffer[:, 1536:].astype(F32).reshape(SHARDS, 16, 128)
    lane = iota((16, 128), 1)
    for k in range(4):
        tile = small[8 * k]
        for t in range(1, 8):
            tile = jnp.where(lane // 16 == t, pltpu.roll(small[8 * k + t], 16 * t, 1), tile)
        vec.buffer[:, 128 * k : 128 * k + 128] = tile
    lane = iota((16, 128), 1)
    for k in range(16):
        tile = jnp.where(lane < 64, small[2 * k], pltpu.roll(small[2 * k + 1], 64, 1))
        bias_up.buffer[:, 128 * k : 128 * k + 128] = jnp.broadcast_to(tile[13:14], (8, 128))
    for write in (weights, vec, bias_up):
        write.send()
    table[...] = jnp.zeros_like(table)
    table[0:8, :] = vec.buffer[0:8, :]
    gain, shift = vec.buffer[8:9, :], vec.buffer[9:10, :]
    marks.whole()
    blocks = embeds.buffer.shape[0] // RB

    def norm_pair(pair, _):
        embeds.part(pair)
        for half in range(2):
            b = 2 * pair + half
            rows[half] = dot(marks.buffer[block(b, RB), :], table[...].astype(LOW))
            for c in range(RB // CH):
                at = pl.ds(c * CH, CH)
                here = pl.ds(pl.multiple_of(b * RB + c * CH, CH), CH)
                base = embeds.buffer[here, :].astype(F32) + rows[half, at, :]
                put_tall(tall.at[half], c * CH, base)
                unit, _rate = norm_parts(base)
                value = unit * gain + shift
                put_tall(rows0.at[half], c * CH, value)
                normed.buffer[here, :] = value.astype(LOW)
            out = block(b, EB)
            slots_first(tall.at[half], base0.buffer, out)
            slots_first(rows0.at[half], norm0, out)
            keyval.buffer[block(b, RB), :] = dot(normed.buffer[block(b, RB), :], weights.buffer[:, 512:1536]).astype(LOW)
        normed.part(pair)
        keyval.part(pair)
        return 0

    lax.fori_loop(0, blocks // 2, norm_pair, 0)
    normed0.buffer[...] = norm0[...].astype(LOW)
    query.buffer[...] = dot(normed0.buffer[...], weights.buffer[:, :512]).astype(LOW)
    normed0.send()
    query.send()
    base0.send()
    shape = (RB, HEADS * EB)
    match = iota(shape, 0) // SLOTS == iota(shape, 1) % EB
    liver = jnp.where(iota((128, HEADS * EB), 0) == 8, 1.0, 0.0).astype(LOW)

    def attend_pair(pair, _):
        for half in range(2):
            b = 2 * pair + half
            at, out = block(b, RB), block(b, EB)
            scores = dot_nt(keyval.buffer[at, :512], spread_heads(query.buffer[out, :])) * SCALE
            live = dot(marks.buffer[at, :], liver) > 0.5
            scores = jnp.where(live, scores, -1000000000.0).reshape(EB, SLOTS, HEADS * EB)
            top = jnp.max(scores, axis=1, keepdims=True)
            power = jnp.exp(scores - top)
            part = (power / jnp.sum(power, axis=1, keepdims=True)).reshape(shape)
            low = jnp.where(match, part, 0.0).astype(LOW)
            probs.buffer[at, :] = low
            mixed.buffer[out, :] = pick_heads(dot_tn(low, keyval.buffer[at, 512:])).astype(LOW)
        probs.part(pair)
        return 0

    lax.fori_loop(0, blocks // 2, attend_pair, 0)
    mixed.send()


def ffn_kernel(me, near, reads, writes, scratch):
    cotangent, base0, mixed, vec, bias_up = reads
    output, dfirst, dmixed, sum_up, sum_gain, sum_shift, sum_pool, own, *halves = writes
    w_proj, w_up, w_down, w_out, first, norm_ffn, pre_low, dpool, hidden, slope, total = scratch
    pieces, sem = near
    out = Place(me, pieces[8:], w_out, sem.at[3], lambda piece: piece.at[pl.ds(64, 16)], turned=True)
    proj = Place(me, pieces[:8], w_proj, sem.at[0], lambda piece: piece.at[pl.ds(0, 16)])
    up = Place(me, pieces[:8], w_up, sem.at[1], lambda piece: piece.at[pl.ds(16, 16)])
    down = Place(me, pieces[8:], w_down, sem.at[2], lambda piece: piece.at[pl.ds(0, 64)], turned=True)

    def share(row, steps, target, base=0):
        for k in range(SHARDS):
            half, place = (own, k) if k < 16 else (halves[k // 8 - 2], k % 8)
            for step in range(steps):
                at = pl.ds(pl.multiple_of(base + (shard_at(me, k) * steps + step) * 16, 16), 16)
                half.buffer[place, row : row + 16, target(step)] = total[at, :].astype(LOW)

    for read in (base0, mixed, vec):
        read.whole()
    out.wait()
    first[...] = base0.buffer[...] + dot(mixed.buffer[...], w_out[...])
    for c in range(first.shape[0] // CH):
        at = pl.ds(c * CH, CH)
        unit, _rate = norm_parts(first[at, :])
        norm_ffn[at, :] = (unit * vec.buffer[10:11, :] + vec.buffer[11:12, :]).astype(LOW)
    cotangent.whole()
    proj.wait()
    grad = dot_nt(cotangent.buffer[...], w_proj[...])
    dpool[...] = grad
    sum_pool.buffer[...] = fold(grad)
    low = grad.astype(LOW)
    bias_up.whole()
    up.wait()
    for k in range(8):
        lanes = slice(256 * k, 256 * k + 256)
        pre = dot(norm_ffn[...], w_up[:, lanes])
        rows = pre.shape[0] // 4
        for c in range(4):
            at = slice(rows * c, rows * c + rows)
            value = pre[at] + bias_up.buffer[0:1, lanes]
            below = 0.5 * (1.0 + lax.erf(value * (0.5**0.5)))
            hidden[at, lanes] = (value * below).astype(LOW)
            slope[at, lanes] = below + value * (jnp.exp(-0.5 * value * value) * 0.3989422804014327)
        total[256 * k : 256 * k + 256, :] = dot_tn(hidden[:, lanes], low)
    share(32, 4, lambda step: slice(512 * step, 512 * step + 512))
    down.wait()
    for k in range(8):
        lanes = slice(256 * k, 256 * k + 256)
        dpre = slope[:, lanes] * dot_nt(low, w_down[lanes, :])
        sum_up.buffer[:, lanes] = fold(dpre)
        pre_low[:, lanes] = dpre.astype(LOW)
    dfirst.buffer[...] = dot_nt(pre_low[...], w_up[...])
    gains = jnp.zeros((8, 512), F32)
    shifts = jnp.zeros((8, 512), F32)
    for c in range(first.shape[0] // CH):
        at = slice(CH * c, CH * c + CH)
        grad = dfirst.buffer[at, :]
        unit, rate = norm_parts(first[at, :])
        gains += fold(grad * unit)
        shifts += fold(grad)
        dfirst.buffer[at, :] = norm_back(grad, unit, rate, vec.buffer[10:11, :]) + dpool[at, :]
    sum_gain.buffer[...] = gains
    sum_shift.buffer[...] = shifts
    dmixed.buffer[...] = dot_nt(dfirst.buffer[...].astype(LOW), w_out[...]).astype(LOW)
    for write in (dfirst, dmixed, sum_up, sum_gain, sum_shift, sum_pool):
        write.send()
    pooled = (first[...] + dot(hidden[...], w_down[...]) + vec.buffer[12:13, :]).astype(LOW)
    for k in range(4):
        lanes = slice(512 * k, 512 * k + 512)
        total[:512, :] = dot_tn(pooled, cotangent.buffer[:, lanes])
        share(0, 1, lambda _step: lanes)
        total[512:1024, :] = dot_tn(norm_ffn[...], pre_low[:, lanes])
        share(16, 1, lambda _step: lanes, 512)
        output.buffer[:, lanes] = dot(pooled, w_proj[:, lanes]).astype(LOW)
    for half in halves:
        half.send()
    own.send()
    output.send()


def attend_back_kernel(me, _near, reads, writes, scratch):
    dmixed, query, probs, keyval, weights = reads
    dkeyval, dquery, query_part = writes
    dmixed.whole()
    query.whole()

    def attend_pair(pair, _):
        probs.part(pair)
        keyval.part(pair)
        for half in range(2):
            b = 2 * pair + half
            at, out = block(b, RB), block(b, EB)
            low = probs.buffer[at, :]
            part = low.astype(F32)
            dmix = spread_heads(dmixed.buffer[out, :])
            grad = dot_nt(keyval.buffer[at, 512:], dmix)
            shape = (EB, SLOTS, HEADS * EB)
            whole = jnp.sum((part * grad).reshape(shape), axis=1, keepdims=True)
            dscores = (part.reshape(shape) * (grad.reshape(shape) - whole)).reshape(RB, HEADS * EB).astype(LOW)
            dkeyval.buffer[at, 512:] = dot(low, dmix).astype(LOW)
            dkeyval.buffer[at, :512] = (dot(dscores, spread_heads(query.buffer[out, :])) * SCALE).astype(LOW)
            dquery.buffer[out, :] = (pick_heads(dot_tn(dscores, keyval.buffer[at, :512])) * SCALE).astype(LOW)
        dkeyval.part(pair)
        return 0

    lax.fori_loop(0, keyval.buffer.shape[0] // RB // 2, attend_pair, 0)
    dquery.send()
    query_part.buffer[...] = dot_nt(dquery.buffer[...], weights.whole()[...])
    query_part.send()


def input_back_kernel(me, _near, reads, writes, scratch):
    vec, query_part, dfirst, marks, weights, dkeyval, embeds, gain_ffn, shift_ffn, pool, up, mixed, normed0, dquery, normed = reads
    grad_embeds, own, *halves = writes
    grad_qkv, grad_out, table, rows, work, lower, spread_query, spread_first, small, sums = scratch
    for read in (weights, query_part, dfirst, vec, marks):
        read.whole()
    table[...] = jnp.zeros_like(table)
    table[0:8, :] = vec.buffer[0:8, :].astype(LOW)
    sums[...] = jnp.zeros_like(sums)
    spread_query[...] = jnp.zeros_like(spread_query)
    spread_first[...] = jnp.zeros_like(spread_first)
    gain = vec.buffer[8:9, :]

    def norm_pair(pair, _):
        dkeyval.part(pair)
        embeds.part(pair)
        for half in range(2):
            b = 2 * pair + half
            at, out = block(b, RB), block(b, EB)
            put_first(spread_query.at[half], query_part.buffer[out, :])
            put_first(spread_first.at[half], dfirst.buffer[out, :])
            rows[half] = dot(marks.buffer[at, :], table[...])
            work[half] = dot_nt(dkeyval.buffer[at, :], weights.buffer[...])
            gains, shifts = jnp.zeros((8, 512), F32), jnp.zeros((8, 512), F32)
            for c in range(RB // CH):
                local = pl.ds(c * CH, CH)
                here = pl.ds(pl.multiple_of(b * RB + c * CH, CH), CH)
                grad = work[half, local, :] + get_tall(spread_query.at[half], c * CH, CH)
                unit, rate = norm_parts(embeds.buffer[here, :].astype(F32) + rows[half, local, :])
                gains += fold(grad * unit)
                shifts += fold(grad)
                value = norm_back(grad, unit, rate, gain) + get_tall(spread_first.at[half], c * CH, CH)
                high = value.astype(LOW)
                grad_embeds.buffer[here, :] = high
                lower[half, local, :] = (value - high.astype(F32)).astype(LOW)
            sums[half, 0:8, :] += gains
            sums[half, 8:16, :] += shifts
            mark = marks.buffer[at, :]
            sums[half, 16:144, :] += dot_tn(mark, grad_embeds.buffer[at, :]) + dot_tn(mark, lower[half])
        grad_embeds.part(pair)
        return 0

    lax.fori_loop(0, embeds.buffer.shape[0] // RB // 2, norm_pair, 0)
    grad_out[...] = dot_tn(mixed.whole()[...], dfirst.buffer[...].astype(LOW))
    grad_qkv[:, :512] = dot_tn(normed0.whole()[...], dquery.whole()[...])
    normed.whole()
    for k in range(4):
        lanes = slice(256 * k, 256 * k + 256)
        grad_qkv[:, 512 + 256 * k : 768 + 256 * k] = dot_tn(normed.buffer[...], dkeyval.buffer[:, lanes])
    sums[0] = sums[0] + sums[1]
    small[...] = jnp.zeros_like(small)
    small[0:8, :] = sums[0, 16:24, :]
    folded = (sums[0, 0:8, :], sums[0, 8:16, :], gain_ffn.whole()[...], shift_ffn.whole()[...], pool.whole()[...])
    for i, value in enumerate(folded):
        small[8 + i : 9 + i, :] = jnp.sum(value, axis=0, keepdims=True)
    up_row = jnp.sum(up.whole()[...], axis=0, keepdims=True)
    row = iota((16, 128), 0)
    for r in range(SHARDS):
        tile = small[:, 128 * (r // 8) : 128 * (r // 8) + 128]
        tile = jnp.where(row == 13, up_row[:, 128 * (r // 2) : 128 * (r // 2) + 128], tile)
        rows[0, 8 * r : 8 * r + 8, 0:128] = tile[0:8]
        rows[0, 8 * r : 8 * r + 8, 128:256] = tile[8:16]
    for k in range(SHARDS):
        half, place = (own, k) if k < 16 else (halves[k // 8 - 2], k % 8)
        at, near = block(shard_at(me, k), 16), block(shard_at(me, k), 8)
        half.buffer[place, :, :1536] = grad_qkv[at, :].astype(LOW)
        half.buffer[place, :, 1536:2048] = grad_out[at, :].astype(LOW)
        value = jnp.concatenate([rows[0, near, 0:128], rows[0, near, 128:256]])
        half.buffer[place, :, 2048:2176] = value.astype(LOW)
    for half in halves:
        half.send()
    own.send()


def on_device(
    embeds,
    piece_counts,
    group_ids,
    group_table,
    gain_attn,
    shift_attn,
    w_qkv,
    w_out,
    gain_ffn,
    shift_ffn,
    w_up,
    bias_up,
    w_down,
    bias_down,
    w_proj,
    cotangent,
):
    tuned = lax.axis_size("dp") == 32
    entries = embeds.shape[0]
    rows = entries * SLOTS
    flat = embeds.reshape(rows, 512)
    lane = jnp.arange(128, dtype=jnp.int32)
    slot = jnp.arange(SLOTS, dtype=jnp.int32)
    vectors = [gain_attn, shift_attn, gain_ffn, shift_ffn, bias_down]
    later = [embeds]
    if tuned:
        me = lax.axis_index("dp").astype(jnp.int32).reshape(1)
        parts = [(0, 0, w_qkv), (0, 1536, group_table), (13, 1536, bias_up[None, :])]
        parts += [(8 + i, 1536, vector[None, :]) for i, vector in enumerate(vectors)]
        shard = side_by_side(parts, (16, 1664))
        own = jnp.stack([shard, *spread(shard, LAYER[1], LAYER[2], LAYER[3])])
        third = side_by_side([(0, 0, w_down), (64, 0, w_out)], (80, 512))
        quad = [third, *spread(third, NEAR, FAR, ACROSS)]
        mine = [own, *spread(own, NEAR, FAR, ACROSS)]
        pieces = [mine + [send(part, CORE) for part in mine]]
        shard = side_by_side([(0, 0, w_proj), (16, 0, w_up)], (32, 2048))
        upper, lower = spread(shard, LAYER[2], LAYER[1])
        quad = jnp.stack([tie(third, own), *quad[1:]])
        own2 = jnp.stack([tie(shard, quad), lower, upper, send(tie(upper, own), LAYER[1])])
        pieces.append([own2, *spread(own2, NEAR, FAR, ACROSS)])
        lower, upper = spread(quad, LAYER[1], LAYER[2])
        upper = tie(upper, own2)
        pieces.append([quad, lower, upper, send(upper, LAYER[1])])
        later = [tie(own2, upper)]
        group_ids, piece_counts = tie(group_ids, piece_counts, own, every=True)[:2]
    else:
        me = None

        def whole(shard, axis=0):
            return lax.all_gather(shard, "dp", axis=axis, tiled=True)

        def cut(full):
            return [full[4 * i : 4 * i + 4] for i in range(8)]

        gathered = whole(jnp.concatenate([group_table, jnp.stack(vectors)]), 1)
        gathered = jnp.transpose(gathered.reshape(13, SHARDS, 16), (1, 0, 2))
        small = jnp.concatenate(
            [
                jnp.pad(gathered, ((0, 0), (0, 0), (0, 112))),
                jnp.pad(whole(bias_up).reshape(SHARDS, 1, 64), ((0, 0), (0, 2), (0, 64))),
            ],
            axis=1,
        )
        pieces = [
            cut(
                jnp.concatenate(
                    [whole(w_qkv).reshape(SHARDS, 16, 1536), small], axis=2
                )
            ),
            cut(
                jnp.concatenate(
                    [whole(w_proj).reshape(SHARDS, 16, 2048), whole(w_up).reshape(SHARDS, 16, 2048)], axis=1
                )
            ),
            cut(
                jnp.concatenate([whole(w_down).reshape(SHARDS, 64, 512), whole(w_out).reshape(SHARDS, 16, 512)], axis=1)
            ),
        ]
    marks = jnp.where(
        lane[None, None, :] < 8,
        group_ids[:, None, None] == lane[None, None, :],
        slot[None, :, None] < piece_counts[:, None, None],
    )
    marks = marks.astype(LOW).reshape(rows, 128)
    steps = rows // RB // 2
    low, wide = LOW, F32
    (qkv_all, vec, upbias, base0, normed, normed0, query, keyval, probs, mixed) = call(
        attend_kernel, 15,
        me,
        pieces[0],
        [(marks, 1, None), (flat, steps, None)],
        [
            ((512, 1664), low, 1), ((16, 512), wide, 1), ((8, 2048), wide, 1), ((entries, 512), wide, 1),
            ((rows, 512), low, steps), ((entries, 512), low, 1), ((entries, 512), low, 1), ((rows, 1024), low, steps),
            ((rows, HEADS * EB), low, steps), ((entries, 512), low, 1),
        ],
        scratch=[
            ((32, 16, 128), wide), ((128, 512), wide), ((2, RB, 512), wide), ((2, 4 * RB, 128), wide),
            ((2, 4 * RB, 128), wide), ((entries, 512), wide),
        ],
        after=later,
    )
    if tuned:
        mixed, *came = tie(mixed, *pieces[1], *pieces[2], every=True)
        came += [send(part, CORE) for part in came]
        pieces[1:] = [came[0:4] + came[8:12], came[4:8] + came[12:16]]
    (
        output, dfirst, dmixed, sum_up, sum_gain, sum_shift, sum_pool, own_pair, *other_pair
    ) = call(
        ffn_kernel,
        12,
        me,
        [*pieces[1], *pieces[2]],
        [
            (cotangent, 1, None), (base0, 1, None), (mixed, 1, None), (vec, 1, None), (upbias, 1, None),
        ],
        [
            ((entries, 2048), low, 1), ((entries, 512), wide, 1), ((entries, 512), low, 1), ((8, 2048), wide, 1),
            ((8, 512), wide, 1), ((8, 512), wide, 1), ((8, 512), wide, 1), ((16, 48, 2048), low, 1),
            ((8, 48, 2048), low, 1), ((8, 48, 2048), low, 1),
        ],
        [
            ((512, 2048), low), ((512, 2048), low), ((2048, 512), low), ((512, 512), low), ((entries, 512), wide),
            ((entries, 512), low), ((entries, 2048), low), ((entries, 512), wide), ((entries, 2048), low),
            ((entries, 2048), wide), ((2048, 512), wide),
        ],
    )
    if tuned:
        pair = Sum(own_pair, *other_pair)
    (dkeyval, dquery, query_part) = call(
        attend_back_kernel, 8,
        me,
        [],
        [
            (dmixed, 1, None), (query, 1, None), (probs, steps, None), (keyval, steps, None),
            (qkv_all, 1, (0, 512, 0, 512)),
        ],
        [((rows, 1024), low, steps), ((entries, 512), low, 1), ((entries, 512), wide, 1)],
    )
    part = own_pair
    if tuned:
        query_part, pair.high = tie(query_part, pair.high, every=True)
        part = pair.first()
    (grad_embeds, own_last, *other_last) = call(
        input_back_kernel,
        18,
        me,
        [],
        [
            (vec, 1, None), (query_part, 1, None), (dfirst, 1, None), (marks, 1, None), (qkv_all, 1, (0, 512, 512, 1024)),
            (dkeyval, steps, None), (flat, steps, None), (sum_gain, 1, None), (sum_shift, 1, None), (sum_pool, 1, None),
            (sum_up, 1, None), (mixed, 1, None), (normed0, 1, None), (dquery, 1, None), (normed, 1, None),
        ],
        [((rows, 512), low, steps), ((16, 16, 2176), low, 1), ((8, 16, 2176), low, 1), ((8, 16, 2176), low, 1)],
        [
            ((512, 1536), wide), ((512, 512), wide), ((128, 512), low), ((2, RB, 512), wide), ((2, RB, 512), wide),
            ((2, RB, 512), low), ((2, 4 * RB, 128), wide), ((2, 4 * RB, 128), wide), ((16, 512), wide),
            ((2, 144, 512), wide),
        ],
        after=[part],
    )
    if tuned:
        last = Sum(own_last, *other_last)
        part = last.first()
        pair.far = tie(pair.far, part)
        part = pair.second()
        last.far = tie(last.far, part)
        part = last.second()
        pair.near = tie(pair.near, part)
        part = pair.third()
        last.near = tie(last.near, part)
        part = last.third()
        pair.beside = tie(pair.beside, part)
        part = pair.fourth()
        last.beside = tie(last.beside, part)
        part = last.fourth()
        last.beyond = tie(last.beyond, part)
        sum_qkv, sum_out, last_small = [
            widen(last.rest[:, at], last.beyond[:, at])
            for at in (slice(0, 1536), slice(1536, 2048), slice(2048, 2176))
        ]
        pair.beyond = tie(pair.beyond, sum_qkv)
        pair = pair.done()
        sum_proj, sum_up = pair[:16], pair[16:32]
        sum_down = jnp.concatenate([pair[32:, 512 * j : 512 * j + 512] for j in range(4)])
        me = lax.axis_index("dp")
        sums = lax.dynamic_slice(last_small, (0, 16 * (me % 8)), (13, 16))
        sum_upbias = lax.dynamic_slice(last_small, (13, 64 * (me % 2)), (1, 64))[0]
    else:

        def share(full):
            return lax.psum_scatter(full.reshape(-1, full.shape[-1]), "dp", scatter_dimension=0, tiled=True)

        pair_all = jnp.concatenate([own_pair, *other_pair]).astype(F32)
        last_all = jnp.concatenate([own_last, *other_last]).astype(F32)
        sum_proj = share(pair_all[:, :16])
        sum_up = share(pair_all[:, 16:32])
        sum_down = share(pair_all[:, 32:].reshape(SHARDS, 16, 4, 512).transpose(0, 2, 1, 3))
        sum_qkv = share(last_all[:, :, :1536])
        sum_out = share(last_all[:, :, 1536:2048])
        small = last_all[:, :, 2048:]
        vectors = jnp.concatenate([small[8 * k, :13] for k in range(4)], axis=1)
        sums = lax.psum_scatter(vectors, "dp", scatter_dimension=1, tiled=True)
        upbias = jnp.concatenate([small[2 * k, 13] for k in range(16)])
        sum_upbias = lax.psum_scatter(upbias, "dp", scatter_dimension=0, tiled=True)
    return (
        output,
        grad_embeds.reshape(entries, SLOTS, 512),
        sums[:8],
        sums[8],
        sums[9],
        sum_qkv,
        sum_out,
        sums[10],
        sums[11],
        sum_up,
        sum_upbias,
        sum_down,
        sums[12],
        sum_proj,
    )


def solution(mesh):
    placed = (
        P("dp", None, None),
        P("dp"),
        P("dp"),
        P(None, "dp"),
        P("dp"),
        P("dp"),
        P("dp", None),
        P("dp", None),
        P("dp"),
        P("dp"),
        P("dp", None),
        P("dp"),
        P("dp", None),
        P("dp"),
        P("dp", None),
        P("dp", None),
    )
    return jax.shard_map(
        on_device,
        mesh=mesh,
        in_specs=placed,
        out_specs=(
            P("dp", None),
            P("dp", None, None),
            P(None, "dp"),
            P("dp"),
            P("dp"),
            P("dp", None),
            P("dp", None),
            P("dp"),
            P("dp"),
            P("dp", None),
            P("dp"),
            P("dp", None),
            P("dp"),
            P("dp", None),
        ),
        check_vma=False,
    )
```

```python
import jax
import jax.numpy as jnp
from jax import lax
from jax.experimental import pallas as pl
from jax.experimental.pallas import tpu as pltpu
from jax.sharding import PartitionSpec as P

HEADS = 8
HEAD_DIM = 64
SLOTS = 8
SHARDS = 32
EB = 32
RB = EB * SLOTS
CH = 64
VMEM_LIMIT = 58 * 2**20
SCALE = HEAD_DIM ** (-0.5)
F32 = jnp.float32
LOW = jnp.bfloat16


def pairs(partner):
    return [(i, partner(i)) for i in range(32)]


CORE = pairs(lambda i: i ^ 1)
NEAR = pairs(lambda i: i ^ (2 if i % 2 == 0 else 4))
FAR = pairs(lambda i: i ^ (4 if i % 2 == 0 else 2))
ACROSS = pairs(lambda i: i ^ 6)
LAYER = {p: pairs(lambda i: i ^ (p << 3)) for p in (1, 2, 3)}


def send(value, to):
    return lax.ppermute(value, "dp", to)


def spread(value, *ways):
    return [send(value, way) for way in ways]


def tie(value, *after, every=False):
    tied = lax.optimization_barrier((value, *after))
    return tied if every else tied[0]


def side_by_side(parts, shape):
    total = None
    for row, column, part in parts:
        edges = [(row, shape[0] - row - part.shape[0], 0), (column, shape[1] - column - part.shape[1], 0)]
        padded = lax.pad(part, jnp.zeros((), part.dtype), edges)
        total = padded if total is None else total + padded
    return total


def side_by_side_lanes(parts):
    return jnp.concatenate(parts, axis=-1)


def widen(*values):
    total = values[0].astype(F32)
    for value in values[1:]:
        total = total + value.astype(F32)
    return total


class Sum:
    def __init__(self, own, low, high):
        self.own = own
        self.high = send(high, CORE)
        self.low = send(low, CORE)

    def first(self):
        part = widen(self.own[8:], self.high).astype(LOW)
        self.far = send(part, FAR)
        return part

    def second(self):
        part = widen(self.own[4:8], self.low[4:], self.far[4:]).astype(LOW)
        self.near = send(part, NEAR)
        return part

    def total(self, at):
        return widen(self.own[at], self.low[at], self.far[at], self.near[at])

    def third(self):
        part = self.total(slice(1, 4, 2)).astype(LOW)
        self.beside = send(part, LAYER[1])
        return part

    def fourth(self):
        part = widen(self.total(2), self.beside[1]).astype(LOW)
        self.beyond = send(part, LAYER[2])
        self.rest = tie(widen(self.total(0), self.beside[0]), part)
        return part

    def done(self):
        return widen(self.rest, self.beyond)


def shard_at(me, k, turned=False):
    if me is None:
        return k
    near = 2 + 2 * (me & 1)
    quads = [0, near, 6 - near, 6, 1, 7 - near, near + 1, 7]
    core, row, column = k // 16, k // 4 % 4, k % 4
    quad, layer = (4 * core + column, row) if turned else (4 * core + row, column)
    return me ^ quads[quad] ^ (layer << 3)


def dot(left, right):
    return jnp.dot(left, right, preferred_element_type=F32)


def dot_nt(left, right):
    return lax.dot_general(left, right, (((1,), (1,)), ((), ())), preferred_element_type=F32)


def dot_tn(left, right):
    return lax.dot_general(left, right, (((0,), (0,)), ((), ())), preferred_element_type=F32)


def iota(shape, axis):
    return lax.broadcasted_iota(jnp.int32, shape, axis)


def norm_parts(values):
    center = values - jnp.mean(values, axis=-1, keepdims=True)
    rate = lax.rsqrt(jnp.mean(center * center, axis=-1, keepdims=True) + 1e-05)
    return center * rate, rate


def norm_back(grad, unit, rate, gain):
    scaled = grad * gain
    return rate * (
        scaled
        - jnp.mean(scaled, axis=-1, keepdims=True)
        - unit * jnp.mean(scaled * unit, axis=-1, keepdims=True)
    )


def fold(values):
    rows, width = values.shape
    return jnp.sum(values.reshape(rows // 8, 8, width), axis=0)


def spread_heads(rows):
    tiled = jnp.concatenate([rows] * HEADS, axis=0)
    shape = (HEADS * EB, HEADS * HEAD_DIM)
    return jnp.where(iota(shape, 0) // EB == iota(shape, 1) // HEAD_DIM, tiled, jnp.zeros_like(tiled))


def pick_heads(full):
    parts = []
    for k in range(HEADS // 2):
        lanes = slice(128 * k, 128 * k + 128)
        even = full[2 * k * EB : (2 * k + 1) * EB, lanes]
        odd = full[(2 * k + 1) * EB : (2 * k + 2) * EB, lanes]
        parts.append(jnp.where(iota(even.shape, 1) < HEAD_DIM, even, odd))
    return jnp.concatenate(parts, axis=1)


def slots_first(ref, out, at):
    for k in range(4):
        out[at, 128 * k : 128 * k + 128] = ref[pl.ds(k * RB, EB, stride=SLOTS), :]


def put_first(ref, values):
    for k in range(4):
        ref[pl.ds(k * RB, EB, stride=SLOTS), :] = values[:, 128 * k : 128 * k + 128]


def put_tall(ref, start, values):
    for k in range(4):
        ref[pl.ds(k * RB + start, values.shape[0]), :] = values[:, 128 * k : 128 * k + 128]


def get_tall(ref, start, rows):
    return jnp.concatenate([ref[pl.ds(k * RB + start, rows), :] for k in range(4)], axis=1)


def block(i, rows):
    return pl.ds(pl.multiple_of(i * rows, rows), rows)


class Load:
    def __init__(self, source, buffer, sems, first, parts, box):
        self.buffer, self.parts, self.box = buffer, parts, box
        self.source, self.sems, self.first = source, sems, first
        for i in range(parts):
            self.copy(i).start()

    def copy(self, i):
        rows = self.buffer.shape[0] // self.parts
        at = block(i, rows) if self.parts > 1 else pl.ds(0, rows)
        if self.box is None:
            source = self.source.at[at]
        else:
            row, _rows, column, columns = self.box
            start = row + i * rows
            if not isinstance(start, int):
                start = pl.multiple_of(start, rows)
            source = self.source.at[pl.ds(start, rows), pl.ds(column, columns)]
        return pltpu.make_async_copy(source, self.buffer.at[at], self.sems.at[self.first + i])

    def part(self, i):
        self.copy(i).wait()

    def whole(self):
        for i in range(self.parts):
            self.copy(i).wait()
        return self.buffer


class Store:
    def __init__(self, target, buffer, sems, first, parts):
        self.buffer, self.parts = buffer, parts
        self.target, self.sems, self.first = target, sems, first

    def copy(self, i):
        rows = self.buffer.shape[0] // self.parts
        at = block(i, rows) if self.parts > 1 else pl.ds(0, rows)
        return pltpu.make_async_copy(self.buffer.at[at], self.target.at[at], self.sems.at[self.first + i])

    def part(self, i):
        self.copy(i).start()

    def send(self):
        for i in range(self.parts):
            self.copy(i).start()


def call(body, micros, me, near, loads, stores, scratch=(), after=(), raw=()):
    far = pl.BlockSpec(memory_space=pltpu.HBM)
    counts = [len(near), len(loads), len(after), len(stores), len(raw), len(loads), len(stores), len(scratch)]

    def kernel(me_ref, *refs):
        groups, at = [], 0
        for count in counts:
            groups.append(refs[at : at + count])
            at += count
        near_refs, sources, _unused, targets, raw_refs, in_buffers, out_buffers, rest = groups
        in_sems, out_sems, near_sem = refs[at:]
        first, reads = 0, []
        for (_array, parts, box), source, buffer in zip(loads, sources, in_buffers):
            reads.append(Load(source, buffer, in_sems, first, parts, box))
            first += parts
        first, writes = 0, []
        for (_shape, _type, parts), target, buffer in zip(stores, targets, out_buffers):
            writes.append(Store(target, buffer, out_sems, first, parts))
            first += parts
        body(None if me is None else me_ref[0], (near_refs, near_sem, raw_refs), reads, writes, rest)
        for write in writes:
            for i in range(write.parts):
                write.copy(i).wait()

    buffers = [(a.shape if box is None else (box[1], box[3]), a.dtype) for a, _parts, box in loads]
    buffers += [(s, t) for s, t, _parts in stores]
    return pl.pallas_call(
        kernel,
        out_shape=[jax.ShapeDtypeStruct(s, t) for s, t, _parts in stores]
        + [jax.ShapeDtypeStruct(s, t) for s, t in raw],
        in_specs=[pl.BlockSpec(memory_space=pltpu.SMEM)]
        + [far] * (len(near) + len(loads))
        + [pl.BlockSpec(memory_space=pl.ANY)] * len(after),
        out_specs=[far] * (len(stores) + len(raw)),
        scratch_shapes=[pltpu.VMEM(s, t) for s, t in buffers + list(scratch)]
        + [
            pltpu.SemaphoreType.DMA((max(1, sum(parts for _array, parts, _box in loads)),)),
            pltpu.SemaphoreType.DMA((max(1, sum(parts for _shape, _type, parts in stores)),)),
            pltpu.SemaphoreType.DMA((7,)),
        ],
        compiler_params=pltpu.CompilerParams(vmem_limit_bytes=VMEM_LIMIT),
        cost_estimate=pl.CostEstimate(flops=int(micros * 1.1e9), bytes_accessed=1000, transcendentals=0),
    )(jnp.zeros((1,), jnp.int32) if me is None else me, *near, *[a for a, _parts, _box in loads], *after)


class Place:
    def __init__(self, me, pieces, target, sem, cut, turned=False):
        self.copies = []
        rows = target.shape[0] // SHARDS
        for i, piece in enumerate(pieces):
            for p in range(4):
                at = block(shard_at(me, 4 * i + p, turned), rows)
                copy = pltpu.make_async_copy(cut(piece.at[p]), target.at[at], sem)
                copy.start()
                self.copies.append(copy)

    def wait(self):
        for copy in self.copies:
            copy.wait()


def attend_kernel(me, near, reads, writes, scratch):
    marks, embeds = reads
    weights, vec, bias_up, base0, normed, normed0, query, keyval, probs, mixed = writes
    small, table, rows, tall, rows0, norm0 = scratch
    pieces, sem, _raw = near
    Place(me, pieces, weights.buffer, sem.at[0], lambda piece: piece).wait()
    small[...] = weights.buffer[:, 1536:].astype(F32).reshape(SHARDS, 16, 128)
    lane = iota((16, 128), 1)
    for k in range(4):
        tile = small[8 * k]
        for t in range(1, 8):
            tile = jnp.where(lane // 16 == t, pltpu.roll(small[8 * k + t], 16 * t, 1), tile)
        vec.buffer[:, 128 * k : 128 * k + 128] = tile
    lane = iota((16, 128), 1)
    for k in range(16):
        tile = jnp.where(lane < 64, small[2 * k], pltpu.roll(small[2 * k + 1], 64, 1))
        bias_up.buffer[:, 128 * k : 128 * k + 128] = jnp.broadcast_to(tile[13:14], (8, 128))
    for write in (weights, vec, bias_up):
        write.send()
    table[...] = jnp.zeros_like(table)
    table[0:8, :] = vec.buffer[0:8, :]
    gain, shift = vec.buffer[8:9, :], vec.buffer[9:10, :]
    marks.whole()
    blocks = embeds.buffer.shape[0] // RB

    def project(b):
        at = slice(b * RB, b * RB + RB)
        keyval.buffer[at, :] = dot(normed.buffer[at, :], weights.buffer[:, 512:1536]).astype(LOW)
        if b % 2 == 1:
            normed.part(b // 2)
            keyval.part(b // 2)

    for b in range(blocks):
        half = b % 2
        if half == 0:
            embeds.part(b // 2)
        rows[half] = dot(marks.buffer[b * RB : b * RB + RB, :], table[...].astype(LOW))
        if b > 0:
            project(b - 1)
        for c in range(RB // CH):
            at, here = slice(c * CH, c * CH + CH), slice(b * RB + c * CH, b * RB + c * CH + CH)
            base = embeds.buffer[here, :].astype(F32) + rows[half, at, :]
            put_tall(tall.at[half], c * CH, base)
            unit, _rate = norm_parts(base)
            value = unit * gain + shift
            put_tall(rows0.at[half], c * CH, value)
            normed.buffer[here, :] = value.astype(LOW)
        out = slice(b * EB, b * EB + EB)
        slots_first(tall.at[half], base0.buffer, out)
        slots_first(rows0.at[half], norm0, out)
    project(blocks - 1)
    normed0.buffer[...] = norm0[...].astype(LOW)
    query.buffer[...] = dot(normed0.buffer[...], weights.buffer[:, :512]).astype(LOW)
    normed0.send()
    query.send()
    base0.send()
    shape = (RB, HEADS * EB)
    match = iota(shape, 0) // SLOTS == iota(shape, 1) % EB
    liver = jnp.where(iota((128, HEADS * EB), 0) == 8, 1.0, 0.0).astype(LOW)

    for pair in range(blocks // 2):
        for half in range(2):
            b = 2 * pair + half
            at, out = slice(b * RB, b * RB + RB), slice(b * EB, b * EB + EB)
            scores = dot_nt(keyval.buffer[at, :512], spread_heads(query.buffer[out, :])) * SCALE
            live = dot(marks.buffer[at, :], liver) > 0.5
            scores = jnp.where(live, scores, -1000000000.0).reshape(EB, SLOTS, HEADS * EB)
            top = jnp.max(scores, axis=1, keepdims=True)
            power = jnp.exp(scores - top)
            part = (power * (1.0 / jnp.sum(power, axis=1, keepdims=True))).reshape(shape)
            low = jnp.where(match, part, 0.0).astype(LOW)
            probs.buffer[at, :] = low
            mixed.buffer[out, :] = pick_heads(dot_tn(low, keyval.buffer[at, 512:])).astype(LOW)
        probs.part(pair)

    mixed.send()


def ffn_kernel(me, near, reads, writes, scratch):
    cotangent, base0, mixed, vec, bias_up = reads
    output, dfirst, dmixed, sum_up, sum_gain, sum_shift, sum_pool = writes
    w_proj, w_up, w_down, w_out, first, norm_ffn, pre_low, dpool, hidden, slope, low_proj, low_up, low_down = scratch
    pieces, sem, halves = near
    out = Place(me, pieces[8:], w_out, sem.at[3], lambda piece: piece.at[pl.ds(64, 16)], turned=True)
    proj = Place(me, pieces[:8], w_proj, sem.at[0], lambda piece: piece.at[pl.ds(0, 16)])
    up = Place(me, pieces[:8], w_up, sem.at[1], lambda piece: piece.at[pl.ds(16, 16)])
    down = Place(me, pieces[8:], w_down, sem.at[2], lambda piece: piece.at[pl.ds(0, 64)], turned=True)

    copies = []

    def share(grad, row, slot):
        for k in range(SHARDS):
            half, place = (halves[0], k) if k < 16 else (halves[k // 8 - 1], k % 8)
            at = block(shard_at(me, k), 16)
            copy = pltpu.make_async_copy(grad.at[at], half.at[place, pl.ds(row, 16)], sem.at[slot])
            copy.start()
            copies.append(copy)

    for read in (base0, mixed, vec):
        read.whole()
    out.wait()
    first[...] = base0.buffer[...] + dot(mixed.buffer[...], w_out[...])
    for c in range(first.shape[0] // CH):
        at = pl.ds(c * CH, CH)
        unit, _rate = norm_parts(first[at, :])
        norm_ffn[at, :] = (unit * vec.buffer[10:11, :] + vec.buffer[11:12, :]).astype(LOW)
    cotangent.whole()
    proj.wait()
    grad = dot_nt(cotangent.buffer[...], w_proj[...])
    dpool[...] = grad
    sum_pool.buffer[...] = fold(grad)
    low = grad.astype(LOW)
    bias_up.whole()
    up.wait()
    for k in range(8):
        lanes = slice(256 * k, 256 * k + 256)
        pre = dot(norm_ffn[...], w_up[:, lanes])
        rows = pre.shape[0] // 4
        for c in range(4):
            at = slice(rows * c, rows * c + rows)
            value = pre[at] + bias_up.buffer[0:1, lanes]
            below = 0.5 * (1.0 + lax.erf(value * (0.5**0.5)))
            hidden[at, lanes] = (value * below).astype(LOW)
            slope[at, lanes] = below + value * (jnp.exp(-0.5 * value * value) * 0.3989422804014327)
        grad = dot_tn(hidden[:, lanes], low)
        for r in range(4):
            for j in range(4):
                part = grad[64 * r + 16 * j : 64 * r + 16 * j + 16, :]
                low_down[64 * k + 16 * r : 64 * k + 16 * r + 16, 512 * j : 512 * j + 512] = part.astype(LOW)
    share(low_down, 32, 6)
    down.wait()
    for k in range(8):
        lanes = slice(256 * k, 256 * k + 256)
        dpre = slope[:, lanes] * dot_nt(low, w_down[lanes, :])
        sum_up.buffer[:, lanes] = fold(dpre)
        pre_low[:, lanes] = dpre.astype(LOW)
    dfirst.buffer[...] = dot_nt(pre_low[...], w_up[...])
    gains = jnp.zeros((8, 512), F32)
    shifts = jnp.zeros((8, 512), F32)
    for c in range(first.shape[0] // CH):
        at = slice(CH * c, CH * c + CH)
        grad = dfirst.buffer[at, :]
        unit, rate = norm_parts(first[at, :])
        gains += fold(grad * unit)
        shifts += fold(grad)
        dfirst.buffer[at, :] = norm_back(grad, unit, rate, vec.buffer[10:11, :]) + dpool[at, :]
    sum_gain.buffer[...] = gains
    sum_shift.buffer[...] = shifts
    dmixed.buffer[...] = dot_nt(dfirst.buffer[...].astype(LOW), w_out[...]).astype(LOW)
    for k in range(4):
        lanes = slice(512 * k, 512 * k + 512)
        low_up[:, lanes] = dot_tn(norm_ffn[...], pre_low[:, lanes]).astype(LOW)
    share(low_up, 16, 4)
    for write in (dfirst, dmixed, sum_up, sum_gain, sum_shift, sum_pool):
        write.send()
    pooled = (first[...] + dot(hidden[...], w_down[...]) + vec.buffer[12:13, :]).astype(LOW)
    for k in range(4):
        lanes = slice(512 * k, 512 * k + 512)
        low_proj[:, lanes] = dot_tn(pooled, cotangent.buffer[:, lanes]).astype(LOW)
    share(low_proj, 0, 5)
    for k in range(4):
        lanes = slice(512 * k, 512 * k + 512)
        output.buffer[:, lanes] = dot(pooled, w_proj[:, lanes]).astype(LOW)
    output.send()
    for copy in copies:
        copy.wait()


def attend_back_kernel(me, _near, reads, writes, scratch):
    dmixed, query, probs, keyval, weights = reads
    dkeyval, dquery, query_part = writes
    dmixed.whole()
    query.whole()

    for pair in range(keyval.buffer.shape[0] // RB // 2):
        probs.part(pair)
        keyval.part(pair)
        for half in range(2):
            b = 2 * pair + half
            at, out = slice(b * RB, b * RB + RB), slice(b * EB, b * EB + EB)
            low = probs.buffer[at, :]
            part = low.astype(F32)
            dmix = spread_heads(dmixed.buffer[out, :])
            grad = dot_nt(keyval.buffer[at, 512:], dmix)
            shape = (EB, SLOTS, HEADS * EB)
            whole = jnp.sum((part * grad).reshape(shape), axis=1, keepdims=True)
            dscores = (part.reshape(shape) * (grad.reshape(shape) - whole)).reshape(RB, HEADS * EB).astype(LOW)
            dkeyval.buffer[at, 512:] = dot(low, dmix).astype(LOW)
            dkeyval.buffer[at, :512] = (dot(dscores, spread_heads(query.buffer[out, :])) * SCALE).astype(LOW)
            dquery.buffer[out, :] = (pick_heads(dot_tn(dscores, keyval.buffer[at, :512])) * SCALE).astype(LOW)
        dkeyval.part(pair)

    dquery.send()
    query_part.buffer[...] = dot_nt(dquery.buffer[...], weights.whole()[...])
    query_part.send()


def input_back_kernel(me, _near, reads, writes, scratch):
    vec, query_part, dfirst, marks, weights, dkeyval, embeds, gain_ffn, shift_ffn, pool, up, mixed, normed0, dquery, normed = reads
    grad_embeds, own, *halves = writes
    grad_qkv, grad_out, table, rows, work, lower, spread_query, spread_first, small, sums = scratch
    for read in (weights, query_part, dfirst, vec, marks):
        read.whole()
    table[...] = jnp.zeros_like(table)
    table[0:8, :] = vec.buffer[0:8, :].astype(LOW)
    sums[...] = jnp.zeros_like(sums)
    spread_query[...] = jnp.zeros_like(spread_query)
    spread_first[...] = jnp.zeros_like(spread_first)
    gain = vec.buffer[8:9, :]

    blocks = embeds.buffer.shape[0] // RB

    def project(b):
        at = slice(b * RB, b * RB + RB)
        if b % 2 == 0:
            dkeyval.part(b // 2)
            embeds.part(b // 2)
        rows[b % 2] = dot(marks.buffer[at, :], table[...])
        work[b % 2] = dot_nt(dkeyval.buffer[at, :], weights.buffer[...])

    def collect(b):
        at = slice(b * RB, b * RB + RB)
        mark = marks.buffer[at, :]
        sums[b % 2, 16:144, :] += dot_tn(mark, grad_embeds.buffer[at, :]) + dot_tn(mark, lower[b % 2])
        if b % 2 == 1:
            grad_embeds.part(b // 2)

    project(0)
    for b in range(blocks):
        half = b % 2
        put_first(spread_query.at[half], query_part.buffer[b * EB : b * EB + EB, :])
        put_first(spread_first.at[half], dfirst.buffer[b * EB : b * EB + EB, :])
        if b + 1 < blocks:
            project(b + 1)
        if b > 0:
            collect(b - 1)
        gains, shifts = jnp.zeros((8, 512), F32), jnp.zeros((8, 512), F32)
        for c in range(RB // CH):
            local, here = slice(c * CH, c * CH + CH), slice(b * RB + c * CH, b * RB + c * CH + CH)
            grad = work[half, local, :] + get_tall(spread_query.at[half], c * CH, CH)
            unit, rate = norm_parts(embeds.buffer[here, :].astype(F32) + rows[half, local, :])
            gains += fold(grad * unit)
            shifts += fold(grad)
            value = norm_back(grad, unit, rate, gain) + get_tall(spread_first.at[half], c * CH, CH)
            high = value.astype(LOW)
            grad_embeds.buffer[here, :] = high
            lower[half, local, :] = (value - high.astype(F32)).astype(LOW)
        sums[half, 0:8, :] += gains
        sums[half, 8:16, :] += shifts
    collect(blocks - 1)
    grad_out[...] = dot_tn(mixed.whole()[...], dfirst.buffer[...].astype(LOW))
    grad_qkv[:, :512] = dot_tn(normed0.whole()[...], dquery.whole()[...])
    normed.whole()
    for k in range(4):
        lanes = slice(256 * k, 256 * k + 256)
        grad_qkv[:, 512 + 256 * k : 768 + 256 * k] = dot_tn(normed.buffer[...], dkeyval.buffer[:, lanes])
    sums[0] = sums[0] + sums[1]
    small[...] = jnp.zeros_like(small)
    small[0:8, :] = sums[0, 16:24, :]
    folded = (sums[0, 0:8, :], sums[0, 8:16, :], gain_ffn.whole()[...], shift_ffn.whole()[...], pool.whole()[...])
    for i, value in enumerate(folded):
        small[8 + i : 9 + i, :] = jnp.sum(value, axis=0, keepdims=True)
    up_row = jnp.sum(up.whole()[...], axis=0, keepdims=True)
    row = iota((16, 128), 0)
    for r in range(SHARDS):
        tile = small[:, 128 * (r // 8) : 128 * (r // 8) + 128]
        tile = jnp.where(row == 13, up_row[:, 128 * (r // 2) : 128 * (r // 2) + 128], tile)
        rows[0, 8 * r : 8 * r + 8, 0:128] = tile[0:8]
        rows[0, 8 * r : 8 * r + 8, 128:256] = tile[8:16]
    for k in range(SHARDS):
        half, place = (own, k) if k < 16 else (halves[k // 8 - 2], k % 8)
        at, near = block(shard_at(me, k), 16), block(shard_at(me, k), 8)
        half.buffer[place, :, :1536] = grad_qkv[at, :].astype(LOW)
        half.buffer[place, :, 1536:2048] = grad_out[at, :].astype(LOW)
        value = jnp.concatenate([rows[0, near, 0:128], rows[0, near, 128:256]])
        half.buffer[place, :, 2048:2176] = value.astype(LOW)
    for half in halves:
        half.send()
    own.send()


def on_device(
    embeds,
    piece_counts,
    group_ids,
    group_table,
    gain_attn,
    shift_attn,
    w_qkv,
    w_out,
    gain_ffn,
    shift_ffn,
    w_up,
    bias_up,
    w_down,
    bias_down,
    w_proj,
    cotangent,
):
    tuned = lax.axis_size("dp") == 32
    entries = embeds.shape[0]
    rows = entries * SLOTS
    flat = embeds.reshape(rows, 512)
    lane = jnp.arange(128, dtype=jnp.int32)
    slot = jnp.arange(SLOTS, dtype=jnp.int32)
    vectors = [gain_attn, shift_attn, gain_ffn, shift_ffn, bias_down]
    later = [embeds]
    if tuned:
        me = lax.axis_index("dp").astype(jnp.int32).reshape(1)
        parts = [(0, 0, w_qkv), (0, 1536, group_table), (13, 1536, bias_up[None, :])]
        parts += [(8 + i, 1536, vector[None, :]) for i, vector in enumerate(vectors)]
        shard = side_by_side(parts, (16, 1664))
        own = jnp.stack([shard, *spread(shard, LAYER[1], LAYER[2], LAYER[3])])
        third = side_by_side([(0, 0, w_down), (64, 0, w_out)], (80, 512))
        quad = [third, *spread(third, NEAR, FAR, ACROSS)]
        mine = [own, *spread(own, NEAR, FAR, ACROSS)]
        pieces = [mine + [send(part, CORE) for part in mine]]
        shard = side_by_side([(0, 0, w_proj), (16, 0, w_up)], (32, 2048))
        upper, lower = spread(shard, LAYER[2], LAYER[1])
        quad = jnp.stack([tie(third, own), *quad[1:]])
        own2 = jnp.stack([tie(shard, quad), lower, upper, send(tie(upper, own), LAYER[1])])
        pieces.append([own2, *spread(own2, NEAR, FAR, ACROSS)])
        lower, upper = spread(quad, LAYER[1], LAYER[2])
        upper = tie(upper, own2)
        pieces.append([quad, lower, upper, send(upper, LAYER[1])])
        near2 = tie(pieces[1][1], upper)
        early = [send(own2, CORE), send(near2, CORE)]
        later = [tie(own2, near2)]
        group_ids, piece_counts = tie(group_ids, piece_counts, own, every=True)[:2]
    else:
        me = None

        def whole(shard, axis=0):
            return lax.all_gather(shard, "dp", axis=axis, tiled=True)

        def cut(full):
            return [full[4 * i : 4 * i + 4] for i in range(8)]

        gathered = whole(jnp.concatenate([group_table, jnp.stack(vectors)]), 1)
        gathered = jnp.transpose(gathered.reshape(13, SHARDS, 16), (1, 0, 2))
        small = jnp.concatenate(
            [
                jnp.pad(gathered, ((0, 0), (0, 0), (0, 112))),
                jnp.pad(whole(bias_up).reshape(SHARDS, 1, 64), ((0, 0), (0, 2), (0, 64))),
            ],
            axis=1,
        )
        pieces = [
            cut(
                jnp.concatenate(
                    [whole(w_qkv).reshape(SHARDS, 16, 1536), small], axis=2
                )
            ),
            cut(
                jnp.concatenate(
                    [whole(w_proj).reshape(SHARDS, 16, 2048), whole(w_up).reshape(SHARDS, 16, 2048)], axis=1
                )
            ),
            cut(
                jnp.concatenate([whole(w_down).reshape(SHARDS, 64, 512), whole(w_out).reshape(SHARDS, 16, 512)], axis=1)
            ),
        ]
    marks = jnp.where(
        lane[None, None, :] < 8,
        group_ids[:, None, None] == lane[None, None, :],
        slot[None, :, None] < piece_counts[:, None, None],
    )
    marks = marks.astype(LOW).reshape(rows, 128)
    steps = rows // RB // 2
    low, wide = LOW, F32
    (qkv_all, vec, upbias, base0, normed, normed0, query, keyval, probs, mixed) = call(
        attend_kernel, 15,
        me,
        pieces[0],
        [(marks, 1, None), (flat, steps, None)],
        [
            ((512, 1664), low, 1), ((16, 512), wide, 1), ((8, 2048), wide, 1), ((entries, 512), wide, 1),
            ((rows, 512), low, steps), ((entries, 512), low, 1), ((entries, 512), low, 1), ((rows, 1024), low, steps),
            ((rows, HEADS * EB), low, steps), ((entries, 512), low, 1),
        ],
        scratch=[
            ((32, 16, 128), wide), ((128, 512), wide), ((2, RB, 512), wide), ((2, 4 * RB, 128), wide),
            ((2, 4 * RB, 128), wide), ((entries, 512), wide),
        ],
        after=later,
    )
    if tuned:
        mixed, *came = tie(mixed, *pieces[1], *pieces[2], every=True)
        cores = [send(part, CORE) for part in came[2:]]
        pieces[1:] = [came[0:4] + early + cores[:2], came[4:8] + cores[2:]]
    (
        output, dfirst, dmixed, sum_up, sum_gain, sum_shift, sum_pool, own_pair, *other_pair
    ) = call(
        ffn_kernel,
        12,
        me,
        [*pieces[1], *pieces[2]],
        [
            (cotangent, 1, None), (base0, 1, None), (mixed, 1, None), (vec, 1, None), (upbias, 1, None),
        ],
        [
            ((entries, 2048), low, 1), ((entries, 512), wide, 1), ((entries, 512), low, 1), ((8, 2048), wide, 1),
            ((8, 512), wide, 1), ((8, 512), wide, 1), ((8, 512), wide, 1),
        ],
        [
            ((512, 2048), low), ((512, 2048), low), ((2048, 512), low), ((512, 512), low), ((entries, 512), wide),
            ((entries, 512), low), ((entries, 2048), low), ((entries, 512), wide), ((entries, 2048), low),
            ((entries, 2048), wide), ((512, 2048), low), ((512, 2048), low), ((512, 2048), low),
        ],
        raw=[((16, 48, 2048), low), ((8, 48, 2048), low), ((8, 48, 2048), low)],
    )
    if tuned:
        pair = Sum(own_pair, *other_pair)
    (dkeyval, dquery, query_part) = call(
        attend_back_kernel, 8,
        me,
        [],
        [
            (dmixed, 1, None), (query, 1, None), (probs, steps, None), (keyval, steps, None),
            (qkv_all, 1, (0, 512, 0, 512)),
        ],
        [((rows, 1024), low, steps), ((entries, 512), low, 1), ((entries, 512), wide, 1)],
    )
    part = own_pair
    if tuned:
        query_part, pair.high = tie(query_part, pair.high, every=True)
        part = pair.first()
    (grad_embeds, own_last, *other_last) = call(
        input_back_kernel,
        18,
        me,
        [],
        [
            (vec, 1, None), (query_part, 1, None), (dfirst, 1, None), (marks, 1, None), (qkv_all, 1, (0, 512, 512, 1024)),
            (dkeyval, steps, None), (flat, steps, None), (sum_gain, 1, None), (sum_shift, 1, None), (sum_pool, 1, None),
            (sum_up, 1, None), (mixed, 1, None), (normed0, 1, None), (dquery, 1, None), (normed, 1, None),
        ],
        [((rows, 512), low, steps), ((16, 16, 2176), low, 1), ((8, 16, 2176), low, 1), ((8, 16, 2176), low, 1)],
        [
            ((512, 1536), wide), ((512, 512), wide), ((128, 512), low), ((2, RB, 512), wide), ((2, RB, 512), wide),
            ((2, RB, 512), low), ((2, 4 * RB, 128), wide), ((2, 4 * RB, 128), wide), ((16, 512), wide),
            ((2, 144, 512), wide),
        ],
        after=[part],
    )
    if tuned:
        last = Sum(own_last, *other_last)
        part = last.first()
        pair.far = tie(pair.far, part)
        part = pair.second()
        last.far = tie(last.far, part)
        part = last.second()
        pair.near = tie(pair.near, part)
        part = pair.third()
        last.near = tie(last.near, part)
        part = last.third()
        pair.beside = tie(pair.beside, part)
        part = pair.fourth()
        last.beside = tie(last.beside, part)
        part = last.fourth()
        last.beyond = tie(last.beyond, part)
        sum_qkv, sum_out, last_small = [
            widen(last.rest[:, at], last.beyond[:, at])
            for at in (slice(0, 1536), slice(1536, 2048), slice(2048, 2176))
        ]
        pair.beyond = tie(pair.beyond, sum_qkv)
        pair = pair.done()
        sum_proj, sum_up = pair[:16], pair[16:32]
        sum_down = jnp.concatenate([pair[32:, 512 * j : 512 * j + 512] for j in range(4)])
        me = lax.axis_index("dp")
        sums = lax.dynamic_slice(last_small, (0, 16 * (me % 8)), (13, 16))
        sum_upbias = lax.dynamic_slice(last_small, (13, 64 * (me % 2)), (1, 64))[0]
    else:

        def share(full):
            return lax.psum_scatter(full.reshape(-1, full.shape[-1]), "dp", scatter_dimension=0, tiled=True)

        pair_all = jnp.concatenate([own_pair, *other_pair]).astype(F32)
        last_all = jnp.concatenate([own_last, *other_last]).astype(F32)
        sum_proj = share(pair_all[:, :16])
        sum_up = share(pair_all[:, 16:32])
        sum_down = share(pair_all[:, 32:].reshape(SHARDS, 16, 4, 512).transpose(0, 2, 1, 3))
        sum_qkv = share(last_all[:, :, :1536])
        sum_out = share(last_all[:, :, 1536:2048])
        small = last_all[:, :, 2048:]
        vectors = jnp.concatenate([small[8 * k, :13] for k in range(4)], axis=1)
        sums = lax.psum_scatter(vectors, "dp", scatter_dimension=1, tiled=True)
        upbias = jnp.concatenate([small[2 * k, 13] for k in range(16)])
        sum_upbias = lax.psum_scatter(upbias, "dp", scatter_dimension=0, tiled=True)
    return (
        output,
        grad_embeds.reshape(entries, SLOTS, 512),
        sums[:8],
        sums[8],
        sums[9],
        sum_qkv,
        sum_out,
        sums[10],
        sums[11],
        sum_up,
        sum_upbias,
        sum_down,
        sums[12],
        sum_proj,
    )


def solution(mesh):
    placed = (
        P("dp", None, None),
        P("dp"),
        P("dp"),
        P(None, "dp"),
        P("dp"),
        P("dp"),
        P("dp", None),
        P("dp", None),
        P("dp"),
        P("dp"),
        P("dp", None),
        P("dp"),
        P("dp", None),
        P("dp"),
        P("dp", None),
        P("dp", None),
    )
    return jax.shard_map(
        on_device,
        mesh=mesh,
        in_specs=placed,
        out_specs=(
            P("dp", None),
            P("dp", None, None),
            P(None, "dp"),
            P("dp"),
            P("dp"),
            P("dp", None),
            P("dp", None),
            P("dp"),
            P("dp"),
            P("dp", None),
            P("dp"),
            P("dp", None),
            P("dp"),
            P("dp", None),
        ),
        check_vma=False,
    )
```

```python
import jax
import jax.numpy as jnp
from jax import lax
from jax.experimental import pallas as pl
from jax.experimental.pallas import tpu as pltpu
from jax.sharding import PartitionSpec as P

HEADS = 8
HEAD_DIM = 64
SLOTS = 8
SHARDS = 32
EB = 32
RB = EB * SLOTS
CH = 64
VMEM_LIMIT = 58 * 2**20
SCALE = HEAD_DIM ** (-0.5)
F32 = jnp.float32
LOW = jnp.bfloat16


def pairs(partner):
    return [(i, partner(i)) for i in range(32)]


CORE = pairs(lambda i: i ^ 1)
NEAR = pairs(lambda i: i ^ (2 if i % 2 == 0 else 4))
FAR = pairs(lambda i: i ^ (4 if i % 2 == 0 else 2))
ACROSS = pairs(lambda i: i ^ 6)
LAYER = {p: pairs(lambda i: i ^ (p << 3)) for p in (1, 2, 3)}


def send(value, to):
    return lax.ppermute(value, "dp", to)


def spread(value, *ways):
    return [send(value, way) for way in ways]


def tie(value, *after, every=False):
    tied = lax.optimization_barrier((value, *after))
    return tied if every else tied[0]


def side_by_side(parts, shape):
    total = None
    for row, column, part in parts:
        edges = [(row, shape[0] - row - part.shape[0], 0), (column, shape[1] - column - part.shape[1], 0)]
        padded = lax.pad(part, jnp.zeros((), part.dtype), edges)
        total = padded if total is None else total + padded
    return total


def side_by_side_lanes(parts):
    return jnp.concatenate(parts, axis=-1)


def widen(*values):
    total = values[0].astype(F32)
    for value in values[1:]:
        total = total + value.astype(F32)
    return total


class Sum:
    def __init__(self, own, low, *high):
        self.own = own
        self.high = [send(part, CORE) for part in high]
        self.low = send(low, CORE)

    def first(self):
        size = 8 // len(self.high)
        parts = [widen(self.own[8 + size * i : 8 + size * i + size], part) for i, part in enumerate(self.high)]
        part = jnp.concatenate(parts).astype(LOW)
        self.far = send(part, FAR)
        return part

    def second(self):
        part = widen(self.own[4:8], self.low[4:], self.far[4:]).astype(LOW)
        self.near = send(part, NEAR)
        return part

    def total(self, at):
        return widen(self.own[at], self.low[at], self.far[at], self.near[at])

    def third(self):
        part = self.total(slice(1, 4, 2)).astype(LOW)
        self.beside = send(part, LAYER[1])
        return part

    def fourth(self):
        part = widen(self.total(2), self.beside[1]).astype(LOW)
        self.beyond = send(part, LAYER[2])
        self.rest = tie(widen(self.total(0), self.beside[0]), part)
        return part

    def done(self):
        return widen(self.rest, self.beyond)


class LayersFirst:
    def __init__(self, own, other):
        self.own = own
        self.core = send(other, CORE)

    def first(self):
        part = widen(self.own[1::2], self.core[1::2]).astype(LOW)
        self.beside = send(part, LAYER[1])
        return part

    def second(self):
        part = widen(self.own[2::4], self.core[2::4], self.beside[1::2]).astype(LOW)
        self.beyond = send(part, LAYER[2])
        return part

    def total(self, quad):
        at = slice(4 * quad, 4 * quad + 1)
        half = slice(2 * quad, 2 * quad + 1)
        return widen(self.own[at], self.core[at], self.beside[half], self.beyond[quad : quad + 1])

    def third(self):
        part = widen(self.own[8::4], self.core[8::4], self.beside[4::2], self.beyond[2:]).astype(LOW)
        self.far = send(part, FAR)
        return part

    def fourth(self):
        part = widen(self.total(1), self.far[1:]).astype(LOW)
        self.near = send(part, NEAR)
        return part

    def done(self):
        return widen(self.total(0), self.far[:1], self.near)[0]


def shard_at(me, k, turned=False):
    if me is None:
        return k
    near = 2 + 2 * (me & 1)
    quads = [0, near, 6 - near, 6, 1, 7 - near, near + 1, 7]
    core, row, column = k // 16, k // 4 % 4, k % 4
    quad, layer = (4 * core + column, row) if turned else (4 * core + row, column)
    return me ^ quads[quad] ^ (layer << 3)


def dot(left, right):
    return jnp.dot(left, right, preferred_element_type=F32)


def dot_nt(left, right):
    return lax.dot_general(left, right, (((1,), (1,)), ((), ())), preferred_element_type=F32)


def dot_tn(left, right):
    return lax.dot_general(left, right, (((0,), (0,)), ((), ())), preferred_element_type=F32)


def iota(shape, axis):
    return lax.broadcasted_iota(jnp.int32, shape, axis)


def norm_parts(values):
    center = values - jnp.mean(values, axis=-1, keepdims=True)
    rate = lax.rsqrt(jnp.mean(center * center, axis=-1, keepdims=True) + 1e-05)
    return center * rate, rate


def norm_back(grad, unit, rate, gain):
    scaled = grad * gain
    return rate * (
        scaled
        - jnp.mean(scaled, axis=-1, keepdims=True)
        - unit * jnp.mean(scaled * unit, axis=-1, keepdims=True)
    )


def fold(values):
    rows, width = values.shape
    return jnp.sum(values.reshape(rows // 8, 8, width), axis=0)


def spread_heads(rows):
    tiled = jnp.concatenate([rows] * HEADS, axis=0)
    shape = (HEADS * EB, HEADS * HEAD_DIM)
    return jnp.where(iota(shape, 0) // EB == iota(shape, 1) // HEAD_DIM, tiled, jnp.zeros_like(tiled))


def pick_heads(full):
    parts = []
    for k in range(HEADS // 2):
        lanes = slice(128 * k, 128 * k + 128)
        even = full[2 * k * EB : (2 * k + 1) * EB, lanes]
        odd = full[(2 * k + 1) * EB : (2 * k + 2) * EB, lanes]
        parts.append(jnp.where(iota(even.shape, 1) < HEAD_DIM, even, odd))
    return jnp.concatenate(parts, axis=1)


def slots_first(ref, out, at):
    for k in range(4):
        out[at, 128 * k : 128 * k + 128] = ref[pl.ds(k * RB, EB, stride=SLOTS), :]


def put_first(ref, values):
    for k in range(4):
        ref[pl.ds(k * RB, EB, stride=SLOTS), :] = values[:, 128 * k : 128 * k + 128]


def put_tall(ref, start, values):
    for k in range(4):
        ref[pl.ds(k * RB + start, values.shape[0]), :] = values[:, 128 * k : 128 * k + 128]


def get_tall(ref, start, rows):
    return jnp.concatenate([ref[pl.ds(k * RB + start, rows), :] for k in range(4)], axis=1)


def block(i, rows):
    return pl.ds(pl.multiple_of(i * rows, rows), rows)


class Load:
    def __init__(self, source, buffer, sems, first, parts, box):
        self.buffer, self.parts, self.box = buffer, parts, box
        self.source, self.sems, self.first = source, sems, first
        for i in range(parts):
            self.copy(i).start()

    def copy(self, i):
        rows = self.buffer.shape[0] // self.parts
        at = block(i, rows) if self.parts > 1 else pl.ds(0, rows)
        if self.box is None:
            source = self.source.at[at]
        else:
            row, _rows, column, columns = self.box
            start = row + i * rows
            if not isinstance(start, int):
                start = pl.multiple_of(start, rows)
            source = self.source.at[pl.ds(start, rows), pl.ds(column, columns)]
        return pltpu.make_async_copy(source, self.buffer.at[at], self.sems.at[self.first + i])

    def part(self, i):
        self.copy(i).wait()

    def whole(self):
        for i in range(self.parts):
            self.copy(i).wait()
        return self.buffer


class Store:
    def __init__(self, target, buffer, sems, first, parts):
        self.buffer, self.parts = buffer, parts
        self.target, self.sems, self.first = target, sems, first

    def copy(self, i):
        rows = self.buffer.shape[0] // self.parts
        at = block(i, rows) if self.parts > 1 else pl.ds(0, rows)
        return pltpu.make_async_copy(self.buffer.at[at], self.target.at[at], self.sems.at[self.first + i])

    def part(self, i):
        self.copy(i).start()

    def send(self):
        for i in range(self.parts):
            self.copy(i).start()


def call(body, micros, me, near, loads, stores, scratch=(), after=(), raw=()):
    far = pl.BlockSpec(memory_space=pltpu.HBM)
    counts = [len(near), len(loads), len(after), len(stores), len(raw), len(loads), len(stores), len(scratch)]

    def kernel(me_ref, *refs):
        groups, at = [], 0
        for count in counts:
            groups.append(refs[at : at + count])
            at += count
        near_refs, sources, _unused, targets, raw_refs, in_buffers, out_buffers, rest = groups
        in_sems, out_sems, near_sem = refs[at:]
        first, reads = 0, []
        for (_array, parts, box), source, buffer in zip(loads, sources, in_buffers):
            reads.append(Load(source, buffer, in_sems, first, parts, box))
            first += parts
        first, writes = 0, []
        for (_shape, _type, parts), target, buffer in zip(stores, targets, out_buffers):
            writes.append(Store(target, buffer, out_sems, first, parts))
            first += parts
        body(None if me is None else me_ref[0], (near_refs, near_sem, raw_refs), reads, writes, rest)
        for write in writes:
            for i in range(write.parts):
                write.copy(i).wait()

    buffers = [(a.shape if box is None else (box[1], box[3]), a.dtype) for a, _parts, box in loads]
    buffers += [(s, t) for s, t, _parts in stores]
    return pl.pallas_call(
        kernel,
        out_shape=[jax.ShapeDtypeStruct(s, t) for s, t, _parts in stores]
        + [jax.ShapeDtypeStruct(s, t) for s, t in raw],
        in_specs=[pl.BlockSpec(memory_space=pltpu.SMEM)]
        + [far] * (len(near) + len(loads))
        + [pl.BlockSpec(memory_space=pl.ANY)] * len(after),
        out_specs=[far] * (len(stores) + len(raw)),
        scratch_shapes=[pltpu.VMEM(s, t) for s, t in buffers + list(scratch)]
        + [
            pltpu.SemaphoreType.DMA((max(1, sum(parts for _array, parts, _box in loads)),)),
            pltpu.SemaphoreType.DMA((max(1, sum(parts for _shape, _type, parts in stores)),)),
            pltpu.SemaphoreType.DMA((7,)),
        ],
        compiler_params=pltpu.CompilerParams(vmem_limit_bytes=VMEM_LIMIT),
        cost_estimate=pl.CostEstimate(flops=int(micros * 1.1e9), bytes_accessed=1000, transcendentals=0),
    )(jnp.zeros((1,), jnp.int32) if me is None else me, *near, *[a for a, _parts, _box in loads], *after)


class Place:
    def __init__(self, me, pieces, target, sem, cut, turned=False):
        self.copies = []
        rows = target.shape[0] // SHARDS
        for i, piece in enumerate(pieces):
            for p in range(4):
                at = block(shard_at(me, 4 * i + p, turned), rows)
                copy = pltpu.make_async_copy(cut(piece.at[p]), target.at[at], sem)
                copy.start()
                self.copies.append(copy)

    def wait(self):
        for copy in self.copies:
            copy.wait()


def attend_kernel(me, near, reads, writes, scratch):
    marks, embeds = reads
    weights, vec, bias_up, base0, normed, normed0, query, keyval, probs, mixed = writes
    small, table, rows, tall, rows0, norm0 = scratch
    pieces, sem, _raw = near
    Place(me, pieces, weights.buffer, sem.at[0], lambda piece: piece).wait()
    small[...] = weights.buffer[:, 1536:].astype(F32).reshape(SHARDS, 16, 128)
    lane = iota((16, 128), 1)
    for k in range(4):
        tile = small[8 * k]
        for t in range(1, 8):
            tile = jnp.where(lane // 16 == t, pltpu.roll(small[8 * k + t], 16 * t, 1), tile)
        vec.buffer[:, 128 * k : 128 * k + 128] = tile
    lane = iota((16, 128), 1)
    for k in range(16):
        tile = jnp.where(lane < 64, small[2 * k], pltpu.roll(small[2 * k + 1], 64, 1))
        bias_up.buffer[:, 128 * k : 128 * k + 128] = jnp.broadcast_to(tile[13:14], (8, 128))
    for write in (weights, vec, bias_up):
        write.send()
    table[...] = jnp.zeros_like(table)
    table[0:8, :] = vec.buffer[0:8, :]
    gain, shift = vec.buffer[8:9, :], vec.buffer[9:10, :]
    marks.whole()
    blocks = embeds.buffer.shape[0] // RB

    def project(b):
        at = slice(b * RB, b * RB + RB)
        keyval.buffer[at, :] = dot(normed.buffer[at, :], weights.buffer[:, 512:1536]).astype(LOW)
        if b % 2 == 1:
            normed.part(b // 2)
            keyval.part(b // 2)

    for b in range(blocks):
        half = b % 2
        if half == 0:
            embeds.part(b // 2)
        rows[half] = dot(marks.buffer[b * RB : b * RB + RB, :], table[...].astype(LOW))
        if b > 0:
            project(b - 1)
        for c in range(RB // CH):
            at, here = slice(c * CH, c * CH + CH), slice(b * RB + c * CH, b * RB + c * CH + CH)
            base = embeds.buffer[here, :].astype(F32) + rows[half, at, :]
            put_tall(tall.at[half], c * CH, base)
            unit, _rate = norm_parts(base)
            value = unit * gain + shift
            put_tall(rows0.at[half], c * CH, value)
            normed.buffer[here, :] = value.astype(LOW)
        out = slice(b * EB, b * EB + EB)
        slots_first(tall.at[half], base0.buffer, out)
        slots_first(rows0.at[half], norm0, out)
    project(blocks - 1)
    normed0.buffer[...] = norm0[...].astype(LOW)
    query.buffer[...] = dot(normed0.buffer[...], weights.buffer[:, :512]).astype(LOW)
    normed0.send()
    query.send()
    base0.send()
    shape = (RB, HEADS * EB)
    match = iota(shape, 0) // SLOTS == iota(shape, 1) % EB
    liver = jnp.where(iota((128, HEADS * EB), 0) == 8, 1.0, 0.0).astype(LOW)

    for pair in range(blocks // 2):
        for half in range(2):
            b = 2 * pair + half
            at, out = slice(b * RB, b * RB + RB), slice(b * EB, b * EB + EB)
            scores = dot_nt(keyval.buffer[at, :512], spread_heads(query.buffer[out, :])) * SCALE
            live = dot(marks.buffer[at, :], liver) > 0.5
            scores = jnp.where(live, scores, -1000000000.0).reshape(EB, SLOTS, HEADS * EB)
            top = jnp.max(scores, axis=1, keepdims=True)
            power = jnp.exp(scores - top)
            part = (power * (1.0 / jnp.sum(power, axis=1, keepdims=True))).reshape(shape)
            low = jnp.where(match, part, 0.0).astype(LOW)
            probs.buffer[at, :] = low
            mixed.buffer[out, :] = pick_heads(dot_tn(low, keyval.buffer[at, 512:])).astype(LOW)
        probs.part(pair)

    mixed.send()


def ffn_kernel(me, near, reads, writes, scratch):
    cotangent, base0, mixed, vec, bias_up = reads
    output, dfirst, dmixed, sum_up, sum_gain, sum_shift, sum_pool = writes
    w_proj, w_up, w_down, w_out, first, norm_ffn, pre_low, dpool, hidden, slope, low_proj, low_up, low_down = scratch
    pieces, sem, halves = near
    out = Place(me, pieces[8:], w_out, sem.at[3], lambda piece: piece.at[pl.ds(64, 16)], turned=True)
    proj = Place(me, pieces[:8], w_proj, sem.at[0], lambda piece: piece.at[pl.ds(0, 16)])
    up = Place(me, pieces[:8], w_up, sem.at[1], lambda piece: piece.at[pl.ds(16, 16)])
    down = Place(me, pieces[8:], w_down, sem.at[2], lambda piece: piece.at[pl.ds(0, 64)], turned=True)

    copies = []

    def share(grad, row, slot):
        for k in range(SHARDS):
            if row is None:
                half, place, row_at = halves[3 + k // 16], k % 16, 0
            else:
                half, place = (halves[0], k) if k < 16 else (halves[k // 8 - 1], k % 8)
                row_at = row
            at = block(shard_at(me, k), 16)
            copy = pltpu.make_async_copy(grad.at[at], half.at[place, pl.ds(row_at, 16)], sem.at[slot])
            copy.start()
            copies.append(copy)

    for read in (base0, mixed, vec):
        read.whole()
    out.wait()
    first[...] = base0.buffer[...] + dot(mixed.buffer[...], w_out[...])
    for c in range(first.shape[0] // CH):
        at = pl.ds(c * CH, CH)
        unit, _rate = norm_parts(first[at, :])
        norm_ffn[at, :] = (unit * vec.buffer[10:11, :] + vec.buffer[11:12, :]).astype(LOW)
    cotangent.whole()
    proj.wait()
    grad = dot_nt(cotangent.buffer[...], w_proj[...])
    dpool[...] = grad
    sum_pool.buffer[...] = fold(grad)
    low = grad.astype(LOW)
    bias_up.whole()
    up.wait()
    for k in range(8):
        lanes = slice(256 * k, 256 * k + 256)
        pre = dot(norm_ffn[...], w_up[:, lanes])
        rows = pre.shape[0] // 4
        for c in range(4):
            at = slice(rows * c, rows * c + rows)
            value = pre[at] + bias_up.buffer[0:1, lanes]
            below = 0.5 * (1.0 + lax.erf(value * (0.5**0.5)))
            hidden[at, lanes] = (value * below).astype(LOW)
            slope[at, lanes] = below + value * (jnp.exp(-0.5 * value * value) * 0.3989422804014327)
        grad = dot_tn(hidden[:, lanes], low)
        for r in range(4):
            for j in range(4):
                part = grad[64 * r + 16 * j : 64 * r + 16 * j + 16, :]
                low_down[64 * k + 16 * r : 64 * k + 16 * r + 16, 512 * j : 512 * j + 512] = part.astype(LOW)
    share(low_down, None, 6)
    down.wait()
    for k in range(8):
        lanes = slice(256 * k, 256 * k + 256)
        dpre = slope[:, lanes] * dot_nt(low, w_down[lanes, :])
        sum_up.buffer[:, lanes] = fold(dpre)
        pre_low[:, lanes] = dpre.astype(LOW)
    dfirst.buffer[...] = dot_nt(pre_low[...], w_up[...])
    gains = jnp.zeros((8, 512), F32)
    shifts = jnp.zeros((8, 512), F32)
    for c in range(first.shape[0] // CH):
        at = slice(CH * c, CH * c + CH)
        grad = dfirst.buffer[at, :]
        unit, rate = norm_parts(first[at, :])
        gains += fold(grad * unit)
        shifts += fold(grad)
        dfirst.buffer[at, :] = norm_back(grad, unit, rate, vec.buffer[10:11, :]) + dpool[at, :]
    sum_gain.buffer[...] = gains
    sum_shift.buffer[...] = shifts
    dmixed.buffer[...] = dot_nt(dfirst.buffer[...].astype(LOW), w_out[...]).astype(LOW)
    for k in range(4):
        lanes = slice(512 * k, 512 * k + 512)
        low_up[:, lanes] = dot_tn(norm_ffn[...], pre_low[:, lanes]).astype(LOW)
    share(low_up, 16, 4)
    for write in (dfirst, dmixed, sum_up, sum_gain, sum_shift, sum_pool):
        write.send()
    pooled = (first[...] + dot(hidden[...], w_down[...]) + vec.buffer[12:13, :]).astype(LOW)
    for k in range(4):
        lanes = slice(512 * k, 512 * k + 512)
        low_proj[:, lanes] = dot_tn(pooled, cotangent.buffer[:, lanes]).astype(LOW)
    share(low_proj, 0, 5)
    for k in range(4):
        lanes = slice(512 * k, 512 * k + 512)
        output.buffer[:, lanes] = dot(pooled, w_proj[:, lanes]).astype(LOW)
    output.send()
    for copy in copies:
        copy.wait()


def attend_back_kernel(me, _near, reads, writes, scratch):
    dmixed, query, probs, keyval, weights = reads
    dkeyval, dquery, query_part = writes
    dmixed.whole()
    query.whole()

    for pair in range(keyval.buffer.shape[0] // RB // 2):
        probs.part(pair)
        keyval.part(pair)
        for half in range(2):
            b = 2 * pair + half
            at, out = slice(b * RB, b * RB + RB), slice(b * EB, b * EB + EB)
            low = probs.buffer[at, :]
            part = low.astype(F32)
            dmix = spread_heads(dmixed.buffer[out, :])
            grad = dot_nt(keyval.buffer[at, 512:], dmix)
            shape = (EB, SLOTS, HEADS * EB)
            whole = jnp.sum((part * grad).reshape(shape), axis=1, keepdims=True)
            dscores = (part.reshape(shape) * (grad.reshape(shape) - whole)).reshape(RB, HEADS * EB).astype(LOW)
            dkeyval.buffer[at, 512:] = dot(low, dmix).astype(LOW)
            dkeyval.buffer[at, :512] = (dot(dscores, spread_heads(query.buffer[out, :])) * SCALE).astype(LOW)
            dquery.buffer[out, :] = (pick_heads(dot_tn(dscores, keyval.buffer[at, :512])) * SCALE).astype(LOW)
        dkeyval.part(pair)

    dquery.send()
    query_part.buffer[...] = dot_nt(dquery.buffer[...], weights.whole()[...])
    query_part.send()


def input_back_kernel(me, _near, reads, writes, scratch):
    vec, query_part, dfirst, marks, weights, dkeyval, embeds, gain_ffn, shift_ffn, pool, up, mixed, normed0, dquery, normed = reads
    grad_embeds, own, *halves = writes
    grad_qkv, grad_out, table, rows, work, lower, spread_query, spread_first, small, sums = scratch
    for read in (weights, query_part, dfirst, vec, marks):
        read.whole()
    table[...] = jnp.zeros_like(table)
    table[0:8, :] = vec.buffer[0:8, :].astype(LOW)
    sums[...] = jnp.zeros_like(sums)
    spread_query[...] = jnp.zeros_like(spread_query)
    spread_first[...] = jnp.zeros_like(spread_first)
    gain = vec.buffer[8:9, :]

    blocks = embeds.buffer.shape[0] // RB

    def project(b):
        at = slice(b * RB, b * RB + RB)
        if b % 2 == 0:
            dkeyval.part(b // 2)
            embeds.part(b // 2)
        rows[b % 2] = dot(marks.buffer[at, :], table[...])
        work[b % 2] = dot_nt(dkeyval.buffer[at, :], weights.buffer[...])

    def collect(b):
        at = slice(b * RB, b * RB + RB)
        mark = marks.buffer[at, :]
        sums[b % 2, 16:144, :] += dot_tn(mark, grad_embeds.buffer[at, :]) + dot_tn(mark, lower[b % 2])
        if b % 2 == 1:
            grad_embeds.part(b // 2)

    project(0)
    for b in range(blocks):
        half = b % 2
        put_first(spread_query.at[half], query_part.buffer[b * EB : b * EB + EB, :])
        put_first(spread_first.at[half], dfirst.buffer[b * EB : b * EB + EB, :])
        if b + 1 < blocks:
            project(b + 1)
        if b > 0:
            collect(b - 1)
        gains, shifts = jnp.zeros((8, 512), F32), jnp.zeros((8, 512), F32)
        for c in range(RB // CH):
            local, here = slice(c * CH, c * CH + CH), slice(b * RB + c * CH, b * RB + c * CH + CH)
            grad = work[half, local, :] + get_tall(spread_query.at[half], c * CH, CH)
            unit, rate = norm_parts(embeds.buffer[here, :].astype(F32) + rows[half, local, :])
            gains += fold(grad * unit)
            shifts += fold(grad)
            value = norm_back(grad, unit, rate, gain) + get_tall(spread_first.at[half], c * CH, CH)
            high = value.astype(LOW)
            grad_embeds.buffer[here, :] = high
            lower[half, local, :] = (value - high.astype(F32)).astype(LOW)
        sums[half, 0:8, :] += gains
        sums[half, 8:16, :] += shifts
    collect(blocks - 1)
    grad_out[...] = dot_tn(mixed.whole()[...], dfirst.buffer[...].astype(LOW))
    grad_qkv[:, :512] = dot_tn(normed0.whole()[...], dquery.whole()[...])
    normed.whole()
    for k in range(4):
        lanes = slice(256 * k, 256 * k + 256)
        grad_qkv[:, 512 + 256 * k : 768 + 256 * k] = dot_tn(normed.buffer[...], dkeyval.buffer[:, lanes])
    sums[0] = sums[0] + sums[1]
    small[...] = jnp.zeros_like(small)
    small[0:8, :] = sums[0, 16:24, :]
    folded = (sums[0, 0:8, :], sums[0, 8:16, :], gain_ffn.whole()[...], shift_ffn.whole()[...], pool.whole()[...])
    for i, value in enumerate(folded):
        small[8 + i : 9 + i, :] = jnp.sum(value, axis=0, keepdims=True)
    up_row = jnp.sum(up.whole()[...], axis=0, keepdims=True)
    row = iota((16, 128), 0)
    for r in range(SHARDS):
        tile = small[:, 128 * (r // 8) : 128 * (r // 8) + 128]
        tile = jnp.where(row == 13, up_row[:, 128 * (r // 2) : 128 * (r // 2) + 128], tile)
        rows[0, 8 * r : 8 * r + 8, 0:128] = tile[0:8]
        rows[0, 8 * r : 8 * r + 8, 128:256] = tile[8:16]
    for k in range(SHARDS):
        half, place = (own, k) if k < 16 else (halves[0], k % 8) if k < 24 else (halves[k // 4 - 5], k % 4)
        at, near = block(shard_at(me, k), 16), block(shard_at(me, k), 8)
        half.buffer[place, :, :1536] = grad_qkv[at, :].astype(LOW)
        half.buffer[place, :, 1536:2048] = grad_out[at, :].astype(LOW)
        value = jnp.concatenate([rows[0, near, 0:128], rows[0, near, 128:256]])
        half.buffer[place, :, 2048:2176] = value.astype(LOW)
    for half in halves:
        half.send()
    own.send()


def on_device(
    embeds,
    piece_counts,
    group_ids,
    group_table,
    gain_attn,
    shift_attn,
    w_qkv,
    w_out,
    gain_ffn,
    shift_ffn,
    w_up,
    bias_up,
    w_down,
    bias_down,
    w_proj,
    cotangent,
):
    tuned = lax.axis_size("dp") == 32
    entries = embeds.shape[0]
    rows = entries * SLOTS
    flat = embeds.reshape(rows, 512)
    lane = jnp.arange(128, dtype=jnp.int32)
    slot = jnp.arange(SLOTS, dtype=jnp.int32)
    vectors = [gain_attn, shift_attn, gain_ffn, shift_ffn, bias_down]
    later = [embeds]
    if tuned:
        me = lax.axis_index("dp").astype(jnp.int32).reshape(1)
        parts = [(0, 0, w_qkv), (0, 1536, group_table), (13, 1536, bias_up[None, :])]
        parts += [(8 + i, 1536, vector[None, :]) for i, vector in enumerate(vectors)]
        shard = side_by_side(parts, (16, 1664))
        own = jnp.stack([shard, *spread(shard, LAYER[1], LAYER[2], LAYER[3])])
        third = side_by_side([(0, 0, w_down), (64, 0, w_out)], (80, 512))
        quad = [third, *spread(third, NEAR, FAR, ACROSS)]
        mine = [own, *spread(own, NEAR, FAR, ACROSS)]
        pieces = [mine + [send(part, CORE) for part in mine]]
        shard = side_by_side([(0, 0, w_proj), (16, 0, w_up)], (32, 2048))
        upper, lower = spread(shard, LAYER[2], LAYER[1])
        quad = jnp.stack([tie(third, own), *quad[1:]])
        own2 = jnp.stack([tie(shard, quad), lower, upper, send(tie(upper, own), LAYER[1])])
        pieces.append([own2, *spread(own2, NEAR, FAR, ACROSS)])
        lower, upper = spread(quad, LAYER[1], LAYER[2])
        upper = tie(upper, own2)
        pieces.append([quad, lower, upper, send(upper, LAYER[1])])
        near2 = tie(pieces[1][1], upper)
        early = [send(own2, CORE), send(near2, CORE)]
        later = [tie(own2, near2)]
        group_ids, piece_counts = tie(group_ids, piece_counts, own, every=True)[:2]
    else:
        me = None

        def whole(shard, axis=0):
            return lax.all_gather(shard, "dp", axis=axis, tiled=True)

        def cut(full):
            return [full[4 * i : 4 * i + 4] for i in range(8)]

        gathered = whole(jnp.concatenate([group_table, jnp.stack(vectors)]), 1)
        gathered = jnp.transpose(gathered.reshape(13, SHARDS, 16), (1, 0, 2))
        small = jnp.concatenate(
            [
                jnp.pad(gathered, ((0, 0), (0, 0), (0, 112))),
                jnp.pad(whole(bias_up).reshape(SHARDS, 1, 64), ((0, 0), (0, 2), (0, 64))),
            ],
            axis=1,
        )
        pieces = [
            cut(
                jnp.concatenate(
                    [whole(w_qkv).reshape(SHARDS, 16, 1536), small], axis=2
                )
            ),
            cut(
                jnp.concatenate(
                    [whole(w_proj).reshape(SHARDS, 16, 2048), whole(w_up).reshape(SHARDS, 16, 2048)], axis=1
                )
            ),
            cut(
                jnp.concatenate([whole(w_down).reshape(SHARDS, 64, 512), whole(w_out).reshape(SHARDS, 16, 512)], axis=1)
            ),
        ]
    marks = jnp.where(
        lane[None, None, :] < 8,
        group_ids[:, None, None] == lane[None, None, :],
        slot[None, :, None] < piece_counts[:, None, None],
    )
    marks = marks.astype(LOW).reshape(rows, 128)
    steps = rows // RB // 2
    low, wide = LOW, F32
    (qkv_all, vec, upbias, base0, normed, normed0, query, keyval, probs, mixed) = call(
        attend_kernel, 15,
        me,
        pieces[0],
        [(marks, 1, None), (flat, steps, None)],
        [
            ((512, 1664), low, 1), ((16, 512), wide, 1), ((8, 2048), wide, 1), ((entries, 512), wide, 1),
            ((rows, 512), low, steps), ((entries, 512), low, 1), ((entries, 512), low, 1), ((rows, 1024), low, steps),
            ((rows, HEADS * EB), low, steps), ((entries, 512), low, 1),
        ],
        scratch=[
            ((32, 16, 128), wide), ((128, 512), wide), ((2, RB, 512), wide), ((2, 4 * RB, 128), wide),
            ((2, 4 * RB, 128), wide), ((entries, 512), wide),
        ],
        after=later,
    )
    if tuned:
        mixed, *came = tie(mixed, *pieces[1], *pieces[2], every=True)
        cores = [send(part, CORE) for part in came[2:]]
        pieces[1:] = [came[0:4] + early + cores[:2], came[4:8] + cores[2:]]
    (
        output, dfirst, dmixed, sum_up, sum_gain, sum_shift, sum_pool, own_pair, low_pair, high_pair, *both_down
    ) = call(
        ffn_kernel,
        12,
        me,
        [*pieces[1], *pieces[2]],
        [
            (cotangent, 1, None), (base0, 1, None), (mixed, 1, None), (vec, 1, None), (upbias, 1, None),
        ],
        [
            ((entries, 2048), low, 1), ((entries, 512), wide, 1), ((entries, 512), low, 1), ((8, 2048), wide, 1),
            ((8, 512), wide, 1), ((8, 512), wide, 1), ((8, 512), wide, 1),
        ],
        [
            ((512, 2048), low), ((512, 2048), low), ((2048, 512), low), ((512, 512), low), ((entries, 512), wide),
            ((entries, 512), low), ((entries, 2048), low), ((entries, 512), wide), ((entries, 2048), low),
            ((entries, 2048), wide), ((512, 2048), low), ((512, 2048), low), ((512, 2048), low),
        ],
        raw=[((16, 32, 2048), low), *[((8, 32, 2048), low)] * 2, *[((16, 16, 2048), low)] * 2],
    )
    if tuned:
        pair = Sum(own_pair, low_pair, high_pair)
        down = LayersFirst(*both_down)
    (dkeyval, dquery, query_part) = call(
        attend_back_kernel, 8,
        me,
        [],
        [
            (dmixed, 1, None), (query, 1, None), (probs, steps, None), (keyval, steps, None),
            (qkv_all, 1, (0, 512, 0, 512)),
        ],
        [((rows, 1024), low, steps), ((entries, 512), low, 1), ((entries, 512), wide, 1)],
    )
    part = own_pair
    if tuned:
        query_part, pair.high[0], down.core = tie(query_part, pair.high[0], down.core, every=True)
        part = pair.first()
        down.core = tie(down.core, part)
        part = down.first()
    (grad_embeds, own_last, *other_last) = call(
        input_back_kernel,
        18,
        me,
        [],
        [
            (vec, 1, None), (query_part, 1, None), (dfirst, 1, None), (marks, 1, None), (qkv_all, 1, (0, 512, 512, 1024)),
            (dkeyval, steps, None), (flat, steps, None), (sum_gain, 1, None), (sum_shift, 1, None), (sum_pool, 1, None),
            (sum_up, 1, None), (mixed, 1, None), (normed0, 1, None), (dquery, 1, None), (normed, 1, None),
        ],
        [((rows, 512), low, steps), ((16, 16, 2176), low, 1), ((8, 16, 2176), low, 1), *[((4, 16, 2176), low, 1)] * 2],
        [
            ((512, 1536), wide), ((512, 512), wide), ((128, 512), low), ((2, RB, 512), wide), ((2, RB, 512), wide),
            ((2, RB, 512), low), ((2, 4 * RB, 128), wide), ((2, 4 * RB, 128), wide), ((16, 512), wide),
            ((2, 144, 512), wide),
        ],
        after=[part],
    )
    if tuned:
        last = Sum(own_last, *other_last)
        pair.far, down.beside, *last.high = tie(pair.far, down.beside, *last.high, every=True)
        part = last.first()
        pair.far, down.beside = tie(pair.far, down.beside, part, every=True)[:2]
        part = pair.second()
        down.beside = tie(down.beside, part)
        part = down.second()
        last.far = tie(last.far, part)
        part = last.second()
        pair.near = tie(pair.near, part)
        part = pair.third()
        down.beyond = tie(down.beyond, part)
        part = down.third()
        last.near = tie(last.near, part)
        part = last.third()
        pair.beside, down.far = tie(pair.beside, down.far, part, every=True)[:2]
        part = pair.fourth()
        down.far = tie(down.far, part)
        part = down.fourth()
        last.beside = tie(last.beside, part)
        part = last.fourth()
        down.near = tie(down.near, part)
        sum_down = down.done()
        pair.beyond = tie(pair.beyond, sum_down)
        pair = pair.done()
        last.beyond = tie(last.beyond, pair)
        sum_qkv, sum_out, last_small = [
            widen(last.rest[:, at], last.beyond[:, at])
            for at in (slice(0, 1536), slice(1536, 2048), slice(2048, 2176))
        ]
        sum_proj, sum_up = pair[:16], pair[16:]
        sum_down = jnp.concatenate([sum_down[:, 512 * j : 512 * j + 512] for j in range(4)])
        me = lax.axis_index("dp")
        sums = lax.dynamic_slice(last_small, (0, 16 * (me % 8)), (13, 16))
        sum_upbias = lax.dynamic_slice(last_small, (13, 64 * (me % 2)), (1, 64))[0]
    else:

        def share(full):
            return lax.psum_scatter(full.reshape(-1, full.shape[-1]), "dp", scatter_dimension=0, tiled=True)

        pair_all = jnp.concatenate([own_pair, low_pair, high_pair]).astype(F32)
        down_all = jnp.concatenate(both_down).astype(F32)
        last_all = jnp.concatenate([own_last, *other_last]).astype(F32)
        sum_proj = share(pair_all[:, :16])
        sum_up = share(pair_all[:, 16:])
        sum_down = share(down_all.reshape(SHARDS, 16, 4, 512).transpose(0, 2, 1, 3))
        sum_qkv = share(last_all[:, :, :1536])
        sum_out = share(last_all[:, :, 1536:2048])
        small = last_all[:, :, 2048:]
        vectors = jnp.concatenate([small[8 * k, :13] for k in range(4)], axis=1)
        sums = lax.psum_scatter(vectors, "dp", scatter_dimension=1, tiled=True)
        upbias = jnp.concatenate([small[2 * k, 13] for k in range(16)])
        sum_upbias = lax.psum_scatter(upbias, "dp", scatter_dimension=0, tiled=True)
    return (
        output,
        grad_embeds.reshape(entries, SLOTS, 512),
        sums[:8],
        sums[8],
        sums[9],
        sum_qkv,
        sum_out,
        sums[10],
        sums[11],
        sum_up,
        sum_upbias,
        sum_down,
        sums[12],
        sum_proj,
    )


def solution(mesh):
    placed = (
        P("dp", None, None),
        P("dp"),
        P("dp"),
        P(None, "dp"),
        P("dp"),
        P("dp"),
        P("dp", None),
        P("dp", None),
        P("dp"),
        P("dp"),
        P("dp", None),
        P("dp"),
        P("dp", None),
        P("dp"),
        P("dp", None),
        P("dp", None),
    )
    return jax.shard_map(
        on_device,
        mesh=mesh,
        in_specs=placed,
        out_specs=(
            P("dp", None),
            P("dp", None, None),
            P(None, "dp"),
            P("dp"),
            P("dp"),
            P("dp", None),
            P("dp", None),
            P("dp"),
            P("dp"),
            P("dp", None),
            P("dp"),
            P("dp", None),
            P("dp"),
            P("dp", None),
        ),
        check_vma=False,
    )
```

```python
import jax
import jax.numpy as jnp
from jax import lax
from jax.experimental import pallas as pl
from jax.experimental.pallas import tpu as pltpu
from jax.sharding import PartitionSpec as P

HEADS = 8
HEAD_DIM = 64
SLOTS = 8
SHARDS = 32
EB = 32
RB = EB * SLOTS
CH = 64
VMEM_LIMIT = 50 * 2**20
SCALE = HEAD_DIM ** (-0.5)
F32 = jnp.float32
LOW = jnp.bfloat16


def pairs(partner):
    return [(i, partner(i)) for i in range(32)]


CORE = pairs(lambda i: i ^ 1)
NEAR = pairs(lambda i: i ^ (2 if i % 2 == 0 else 4))
FAR = pairs(lambda i: i ^ (4 if i % 2 == 0 else 2))
ACROSS = pairs(lambda i: i ^ 6)
LAYER = {p: pairs(lambda i: i ^ (p << 3)) for p in (1, 2, 3)}


def send(value, to):
    return lax.ppermute(value, "dp", to)


def spread(value, *ways):
    return [send(value, way) for way in ways]


def tie(value, *after, every=False):
    tied = lax.optimization_barrier((value, *after))
    return tied if every else tied[0]


def side_by_side(parts, shape):
    total = None
    for row, column, part in parts:
        edges = [(row, shape[0] - row - part.shape[0], 0), (column, shape[1] - column - part.shape[1], 0)]
        padded = lax.pad(part, jnp.zeros((), part.dtype), edges)
        total = padded if total is None else total + padded
    return total


def side_by_side_lanes(parts):
    return jnp.concatenate(parts, axis=-1)


def widen(*values):
    total = values[0].astype(F32)
    for value in values[1:]:
        total = total + value.astype(F32)
    return total


class Sum:
    def __init__(self, own, low, *high):
        self.own = own
        self.high = [send(part, CORE) for part in high]
        self.low = send(low, CORE)

    def first(self):
        size = 8 // len(self.high)
        parts = [widen(self.own[8 + size * i : 8 + size * i + size], part) for i, part in enumerate(self.high)]
        part = jnp.concatenate(parts).astype(LOW)
        self.far = send(part, FAR)
        return part

    def second(self):
        part = widen(self.own[4:8], self.low[4:], self.far[4:]).astype(LOW)
        self.near = send(part, NEAR)
        return part

    def total(self, at):
        return widen(self.own[at], self.low[at], self.far[at], self.near[at])

    def third(self):
        part = self.total(slice(1, 4, 2)).astype(LOW)
        self.beside = send(part, LAYER[1])
        return part

    def fourth(self):
        part = widen(self.total(2), self.beside[1]).astype(LOW)
        self.beyond = send(part, LAYER[2])
        self.rest = tie(widen(self.total(0), self.beside[0]), part)
        return part

    def done(self):
        return widen(self.rest, self.beyond)


class LayersFirst:
    def __init__(self, own, other):
        self.own = own
        self.core = send(other, CORE)

    def first(self):
        part = widen(self.own[1::2], self.core[1::2]).astype(LOW)
        self.beside = send(part, LAYER[1])
        return part

    def second(self):
        part = widen(self.own[2::4], self.core[2::4], self.beside[1::2]).astype(LOW)
        self.beyond = send(part, LAYER[2])
        return part

    def total(self, quad):
        at = slice(4 * quad, 4 * quad + 1)
        half = slice(2 * quad, 2 * quad + 1)
        return widen(self.own[at], self.core[at], self.beside[half], self.beyond[quad : quad + 1])

    def third(self):
        part = widen(self.own[8::4], self.core[8::4], self.beside[4::2], self.beyond[2:]).astype(LOW)
        self.far = send(part, FAR)
        return part

    def fourth(self):
        part = widen(self.total(1), self.far[1:]).astype(LOW)
        self.near = send(part, NEAR)
        return part

    def done(self):
        return widen(self.total(0), self.far[:1], self.near)[0]


def shard_at(me, k, turned=False):
    if me is None:
        return k
    near = 2 + 2 * (me & 1)
    quads = [0, near, 6 - near, 6, 1, 7 - near, near + 1, 7]
    core, row, column = k // 16, k // 4 % 4, k % 4
    quad, layer = (4 * core + column, row) if turned else (4 * core + row, column)
    return me ^ quads[quad] ^ (layer << 3)


def dot(left, right):
    return jnp.dot(left, right, preferred_element_type=F32)


def dot_nt(left, right):
    return lax.dot_general(left, right, (((1,), (1,)), ((), ())), preferred_element_type=F32)


def dot_tn(left, right):
    return lax.dot_general(left, right, (((0,), (0,)), ((), ())), preferred_element_type=F32)


def iota(shape, axis):
    return lax.broadcasted_iota(jnp.int32, shape, axis)


def norm_parts(values):
    center = values - jnp.mean(values, axis=-1, keepdims=True)
    rate = lax.rsqrt(jnp.mean(center * center, axis=-1, keepdims=True) + 1e-05)
    return center * rate, rate


def norm_back(grad, unit, rate, gain):
    scaled = grad * gain
    return rate * (
        scaled
        - jnp.mean(scaled, axis=-1, keepdims=True)
        - unit * jnp.mean(scaled * unit, axis=-1, keepdims=True)
    )


def fold(values):
    rows, width = values.shape
    return jnp.sum(values.reshape(rows // 8, 8, width), axis=0)


def spread_heads(rows):
    tiled = jnp.concatenate([rows] * HEADS, axis=0)
    shape = (HEADS * EB, HEADS * HEAD_DIM)
    return jnp.where(iota(shape, 0) // EB == iota(shape, 1) // HEAD_DIM, tiled, jnp.zeros_like(tiled))


def pick_heads(full):
    parts = []
    for k in range(HEADS // 2):
        lanes = slice(128 * k, 128 * k + 128)
        even = full[2 * k * EB : (2 * k + 1) * EB, lanes]
        odd = full[(2 * k + 1) * EB : (2 * k + 2) * EB, lanes]
        parts.append(jnp.where(iota(even.shape, 1) < HEAD_DIM, even, odd))
    return jnp.concatenate(parts, axis=1)


def slots_first(ref, out, at):
    for k in range(4):
        out[at, 128 * k : 128 * k + 128] = ref[pl.ds(k * RB, EB, stride=SLOTS), :]


def put_first(ref, values):
    for k in range(4):
        ref[pl.ds(k * RB, EB, stride=SLOTS), :] = values[:, 128 * k : 128 * k + 128]


def put_tall(ref, start, values):
    for k in range(4):
        ref[pl.ds(k * RB + start, values.shape[0]), :] = values[:, 128 * k : 128 * k + 128]


def get_tall(ref, start, rows):
    return jnp.concatenate([ref[pl.ds(k * RB + start, rows), :] for k in range(4)], axis=1)


def block(i, rows):
    return pl.ds(pl.multiple_of(i * rows, rows), rows)


class Load:
    def __init__(self, source, buffer, sems, first, parts, box):
        self.buffer, self.parts, self.box = buffer, parts, box
        self.source, self.sems, self.first = source, sems, first
        for i in range(parts):
            self.copy(i).start()

    def copy(self, i):
        rows = self.buffer.shape[0] // self.parts
        at = block(i, rows) if self.parts > 1 else pl.ds(0, rows)
        if self.box is None:
            source = self.source.at[at]
        else:
            row, _rows, column, columns = self.box
            start = row + i * rows
            if not isinstance(start, int):
                start = pl.multiple_of(start, rows)
            source = self.source.at[pl.ds(start, rows), pl.ds(column, columns)]
        return pltpu.make_async_copy(source, self.buffer.at[at], self.sems.at[self.first + i])

    def part(self, i):
        self.copy(i).wait()

    def whole(self):
        for i in range(self.parts):
            self.copy(i).wait()
        return self.buffer


class Store:
    def __init__(self, target, buffer, sems, first, parts):
        self.buffer, self.parts = buffer, parts
        self.target, self.sems, self.first = target, sems, first

    def copy(self, i):
        rows = self.buffer.shape[0] // self.parts
        at = block(i, rows) if self.parts > 1 else pl.ds(0, rows)
        return pltpu.make_async_copy(self.buffer.at[at], self.target.at[at], self.sems.at[self.first + i])

    def part(self, i):
        self.copy(i).start()

    def send(self):
        for i in range(self.parts):
            self.copy(i).start()


def call(body, micros, me, near, loads, stores, scratch=(), after=(), raw=()):
    far = pl.BlockSpec(memory_space=pltpu.HBM)
    counts = [len(near), len(loads), len(after), len(stores), len(raw), len(loads), len(stores), len(scratch)]

    def kernel(me_ref, *refs):
        groups, at = [], 0
        for count in counts:
            groups.append(refs[at : at + count])
            at += count
        near_refs, sources, _unused, targets, raw_refs, in_buffers, out_buffers, rest = groups
        in_sems, out_sems, near_sem = refs[at:]
        first, reads = 0, []
        for (_array, parts, box), source, buffer in zip(loads, sources, in_buffers):
            reads.append(Load(source, buffer, in_sems, first, parts, box))
            first += parts
        first, writes = 0, []
        for (_shape, _type, parts), target, buffer in zip(stores, targets, out_buffers):
            writes.append(Store(target, buffer, out_sems, first, parts))
            first += parts
        body(None if me is None else me_ref[0], (near_refs, near_sem, raw_refs), reads, writes, rest)
        for write in writes:
            for i in range(write.parts):
                write.copy(i).wait()

    buffers = [(a.shape if box is None else (box[1], box[3]), a.dtype) for a, _parts, box in loads]
    buffers += [(s, t) for s, t, _parts in stores]
    return pl.pallas_call(
        kernel,
        out_shape=[jax.ShapeDtypeStruct(s, t) for s, t, _parts in stores]
        + [jax.ShapeDtypeStruct(s, t) for s, t in raw],
        in_specs=[pl.BlockSpec(memory_space=pltpu.SMEM)]
        + [far] * (len(near) + len(loads))
        + [pl.BlockSpec(memory_space=pl.ANY)] * len(after),
        out_specs=[far] * (len(stores) + len(raw)),
        scratch_shapes=[pltpu.VMEM(s, t) for s, t in buffers + list(scratch)]
        + [
            pltpu.SemaphoreType.DMA((max(1, sum(parts for _array, parts, _box in loads)),)),
            pltpu.SemaphoreType.DMA((max(1, sum(parts for _shape, _type, parts in stores)),)),
            pltpu.SemaphoreType.DMA((7,)),
        ],
        compiler_params=pltpu.CompilerParams(vmem_limit_bytes=VMEM_LIMIT),
        cost_estimate=pl.CostEstimate(flops=int(micros * 1.1e9), bytes_accessed=1000, transcendentals=0),
    )(jnp.zeros((1,), jnp.int32) if me is None else me, *near, *[a for a, _parts, _box in loads], *after)


class Place:
    def __init__(self, me, pieces, target, sem, cut, turned=False):
        self.copies = []
        rows = target.shape[0] // SHARDS
        for i, piece in enumerate(pieces):
            for p in range(4):
                at = block(shard_at(me, 4 * i + p, turned), rows)
                copy = pltpu.make_async_copy(cut(piece.at[p]), target.at[at], sem)
                copy.start()
                self.copies.append(copy)

    def wait(self):
        for copy in self.copies:
            copy.wait()


def attend_kernel(me, near, reads, writes, scratch):
    marks, embeds = reads
    weights, vec, bias_up, base0, normed, normed0, query, keyval, probs, mixed = writes
    small, table, rows, tall, rows0, norm0 = scratch
    pieces, sem, _raw = near
    Place(me, pieces, weights.buffer, sem.at[0], lambda piece: piece).wait()
    small[...] = weights.buffer[:, 1536:].astype(F32).reshape(SHARDS, 16, 128)
    lane = iota((16, 128), 1)
    for k in range(4):
        tile = small[8 * k]
        for t in range(1, 8):
            tile = jnp.where(lane // 16 == t, pltpu.roll(small[8 * k + t], 16 * t, 1), tile)
        vec.buffer[:, 128 * k : 128 * k + 128] = tile
    lane = iota((16, 128), 1)
    for k in range(16):
        tile = jnp.where(lane < 64, small[2 * k], pltpu.roll(small[2 * k + 1], 64, 1))
        bias_up.buffer[:, 128 * k : 128 * k + 128] = jnp.broadcast_to(tile[13:14], (8, 128))
    for write in (weights, vec, bias_up):
        write.send()
    table[...] = jnp.zeros_like(table)
    table[0:8, :] = vec.buffer[0:8, :]
    gain, shift = vec.buffer[8:9, :], vec.buffer[9:10, :]
    marks.whole()
    blocks = embeds.buffer.shape[0] // RB

    def project(b):
        at = slice(b * RB, b * RB + RB)
        keyval.buffer[at, :] = dot(normed.buffer[at, :], weights.buffer[:, 512:1536]).astype(LOW)
        if b % 2 == 1:
            normed.part(b // 2)
            keyval.part(b // 2)

    for b in range(blocks):
        half = b % 2
        if half == 0:
            embeds.part(b // 2)
        rows[half] = dot(marks.buffer[b * RB : b * RB + RB, :], table[...].astype(LOW))
        if b > 0:
            project(b - 1)
        for c in range(RB // CH):
            at, here = slice(c * CH, c * CH + CH), slice(b * RB + c * CH, b * RB + c * CH + CH)
            base = embeds.buffer[here, :].astype(F32) + rows[half, at, :]
            put_tall(tall.at[half], c * CH, base)
            unit, _rate = norm_parts(base)
            value = unit * gain + shift
            put_tall(rows0.at[half], c * CH, value)
            normed.buffer[here, :] = value.astype(LOW)
        out = slice(b * EB, b * EB + EB)
        slots_first(tall.at[half], base0.buffer, out)
        slots_first(rows0.at[half], norm0, out)
    project(blocks - 1)
    normed0.buffer[...] = norm0[...].astype(LOW)
    query.buffer[...] = dot(normed0.buffer[...], weights.buffer[:, :512]).astype(LOW)
    normed0.send()
    query.send()
    base0.send()
    shape = (RB, HEADS * EB)
    match = iota(shape, 0) // SLOTS == iota(shape, 1) % EB
    liver = jnp.where(iota((128, HEADS * EB), 0) == 8, 1.0, 0.0).astype(LOW)

    for pair in range(blocks // 2):
        for half in range(2):
            b = 2 * pair + half
            at, out = slice(b * RB, b * RB + RB), slice(b * EB, b * EB + EB)
            scores = dot_nt(keyval.buffer[at, :512], spread_heads(query.buffer[out, :])) * SCALE
            live = dot(marks.buffer[at, :], liver) > 0.5
            scores = jnp.where(live, scores, -1000000000.0).reshape(EB, SLOTS, HEADS * EB)
            top = jnp.max(scores, axis=1, keepdims=True)
            power = jnp.exp(scores - top)
            part = (power * (1.0 / jnp.sum(power, axis=1, keepdims=True))).reshape(shape)
            low = jnp.where(match, part, 0.0).astype(LOW)
            probs.buffer[at, :] = low
            mixed.buffer[out, :] = pick_heads(dot_tn(low, keyval.buffer[at, 512:])).astype(LOW)
        probs.part(pair)

    mixed.send()


def ffn_kernel(me, near, reads, writes, scratch):
    cotangent, base0, mixed, vec, bias_up = reads
    output, dfirst, dmixed, sum_up, sum_gain, sum_shift, sum_pool = writes
    w_proj, w_up, w_down, w_out, first, norm_ffn, pre_low, dpool, hidden, slope, low_proj, low_up, low_down = scratch
    pieces, sem, halves = near
    out = Place(me, pieces[8:], w_out, sem.at[3], lambda piece: piece.at[pl.ds(64, 16)], turned=True)
    proj = Place(me, pieces[:8], w_proj, sem.at[0], lambda piece: piece.at[pl.ds(0, 16)])
    up = Place(me, pieces[:8], w_up, sem.at[1], lambda piece: piece.at[pl.ds(16, 16)])
    down = Place(me, pieces[8:], w_down, sem.at[2], lambda piece: piece.at[pl.ds(0, 64)], turned=True)

    copies = []

    def share(grad, row, slot):
        for k in range(SHARDS):
            if row is None:
                half, place, row_at = halves[3 + k // 16], k % 16, 0
            else:
                half, place = (halves[0], k) if k < 16 else (halves[k // 8 - 1], k % 8)
                row_at = row
            at = block(shard_at(me, k), 16)
            copy = pltpu.make_async_copy(grad.at[at], half.at[place, pl.ds(row_at, 16)], sem.at[slot])
            copy.start()
            copies.append(copy)

    for read in (base0, mixed, vec):
        read.whole()
    out.wait()
    first[...] = base0.buffer[...] + dot(mixed.buffer[...], w_out[...])
    for c in range(first.shape[0] // CH):
        at = pl.ds(c * CH, CH)
        unit, _rate = norm_parts(first[at, :])
        norm_ffn[at, :] = (unit * vec.buffer[10:11, :] + vec.buffer[11:12, :]).astype(LOW)
    cotangent.whole()
    proj.wait()
    grad = dot_nt(cotangent.buffer[...], w_proj[...])
    dpool[...] = grad
    sum_pool.buffer[...] = fold(grad)
    low = grad.astype(LOW)
    bias_up.whole()
    up.wait()
    for k in range(8):
        lanes = slice(256 * k, 256 * k + 256)
        pre = dot(norm_ffn[...], w_up[:, lanes])
        rows = pre.shape[0] // 4
        for c in range(4):
            at = slice(rows * c, rows * c + rows)
            value = pre[at] + bias_up.buffer[0:1, lanes]
            below = 0.5 * (1.0 + lax.erf(value * (0.5**0.5)))
            hidden[at, lanes] = (value * below).astype(LOW)
            slope[at, lanes] = below + value * (jnp.exp(-0.5 * value * value) * 0.3989422804014327)
        grad = dot_tn(hidden[:, lanes], low)
        for r in range(4):
            for j in range(4):
                part = grad[64 * r + 16 * j : 64 * r + 16 * j + 16, :]
                low_down[64 * k + 16 * r : 64 * k + 16 * r + 16, 512 * j : 512 * j + 512] = part.astype(LOW)
    share(low_down, None, 6)
    down.wait()
    for k in range(8):
        lanes = slice(256 * k, 256 * k + 256)
        dpre = slope[:, lanes] * dot_nt(low, w_down[lanes, :])
        sum_up.buffer[:, lanes] = fold(dpre)
        pre_low[:, lanes] = dpre.astype(LOW)
    dfirst.buffer[...] = dot_nt(pre_low[...], w_up[...])
    gains = jnp.zeros((8, 512), F32)
    shifts = jnp.zeros((8, 512), F32)
    for c in range(first.shape[0] // CH):
        at = slice(CH * c, CH * c + CH)
        grad = dfirst.buffer[at, :]
        unit, rate = norm_parts(first[at, :])
        gains += fold(grad * unit)
        shifts += fold(grad)
        dfirst.buffer[at, :] = norm_back(grad, unit, rate, vec.buffer[10:11, :]) + dpool[at, :]
    sum_gain.buffer[...] = gains
    sum_shift.buffer[...] = shifts
    dmixed.buffer[...] = dot_nt(dfirst.buffer[...].astype(LOW), w_out[...]).astype(LOW)
    for k in range(4):
        lanes = slice(512 * k, 512 * k + 512)
        low_up[:, lanes] = dot_tn(norm_ffn[...], pre_low[:, lanes]).astype(LOW)
    share(low_up, 16, 4)
    for write in (dfirst, dmixed, sum_up, sum_gain, sum_shift, sum_pool):
        write.send()
    pooled = (first[...] + dot(hidden[...], w_down[...]) + vec.buffer[12:13, :]).astype(LOW)
    for k in range(4):
        lanes = slice(512 * k, 512 * k + 512)
        low_proj[:, lanes] = dot_tn(pooled, cotangent.buffer[:, lanes]).astype(LOW)
    share(low_proj, 0, 5)
    for k in range(4):
        lanes = slice(512 * k, 512 * k + 512)
        output.buffer[:, lanes] = dot(pooled, w_proj[:, lanes]).astype(LOW)
    output.send()
    for copy in copies:
        copy.wait()


def attend_back_kernel(me, _near, reads, writes, scratch):
    dmixed, query, probs, keyval, weights = reads
    dkeyval, dquery, query_part = writes
    dmixed.whole()
    query.whole()

    for pair in range(keyval.buffer.shape[0] // RB // 2):
        probs.part(pair)
        keyval.part(pair)
        for half in range(2):
            b = 2 * pair + half
            at, out = slice(b * RB, b * RB + RB), slice(b * EB, b * EB + EB)
            low = probs.buffer[at, :]
            part = low.astype(F32)
            dmix = spread_heads(dmixed.buffer[out, :])
            grad = dot_nt(keyval.buffer[at, 512:], dmix)
            shape = (EB, SLOTS, HEADS * EB)
            whole = jnp.sum((part * grad).reshape(shape), axis=1, keepdims=True)
            dscores = (part.reshape(shape) * (grad.reshape(shape) - whole)).reshape(RB, HEADS * EB).astype(LOW)
            dkeyval.buffer[at, 512:] = dot(low, dmix).astype(LOW)
            dkeyval.buffer[at, :512] = (dot(dscores, spread_heads(query.buffer[out, :])) * SCALE).astype(LOW)
            dquery.buffer[out, :] = (pick_heads(dot_tn(dscores, keyval.buffer[at, :512])) * SCALE).astype(LOW)
        dkeyval.part(pair)

    dquery.send()
    query_part.buffer[...] = dot_nt(dquery.buffer[...], weights.whole()[...])
    query_part.send()


def input_back_kernel(me, _near, reads, writes, scratch):
    vec, query_part, dfirst, marks, weights, dkeyval, embeds, gain_ffn, shift_ffn, pool, up, mixed, normed0, dquery, normed = reads
    grad_embeds, own, *halves = writes
    grad_qkv, grad_out, table, rows, work, lower, spread_query, spread_first, small, sums = scratch
    for read in (weights, query_part, dfirst, vec, marks):
        read.whole()
    table[...] = jnp.zeros_like(table)
    table[0:8, :] = vec.buffer[0:8, :].astype(LOW)
    sums[...] = jnp.zeros_like(sums)
    spread_query[...] = jnp.zeros_like(spread_query)
    spread_first[...] = jnp.zeros_like(spread_first)
    gain = vec.buffer[8:9, :]

    blocks = embeds.buffer.shape[0] // RB

    def project(b):
        at = slice(b * RB, b * RB + RB)
        if b % 2 == 0:
            dkeyval.part(b // 2)
            embeds.part(b // 2)
        rows[b % 2] = dot(marks.buffer[at, :], table[...])
        work[b % 2] = dot_nt(dkeyval.buffer[at, :], weights.buffer[...])

    def collect(b):
        at = slice(b * RB, b * RB + RB)
        mark = marks.buffer[at, :]
        sums[b % 2, 16:144, :] += dot_tn(mark, grad_embeds.buffer[at, :]) + dot_tn(mark, lower[b % 2])
        if b % 2 == 1:
            grad_embeds.part(b // 2)

    project(0)
    for b in range(blocks):
        half = b % 2
        put_first(spread_query.at[half], query_part.buffer[b * EB : b * EB + EB, :])
        put_first(spread_first.at[half], dfirst.buffer[b * EB : b * EB + EB, :])
        if b + 1 < blocks:
            project(b + 1)
        if b > 0:
            collect(b - 1)
        gains, shifts = jnp.zeros((8, 512), F32), jnp.zeros((8, 512), F32)
        for c in range(RB // CH):
            local, here = slice(c * CH, c * CH + CH), slice(b * RB + c * CH, b * RB + c * CH + CH)
            grad = work[half, local, :] + get_tall(spread_query.at[half], c * CH, CH)
            unit, rate = norm_parts(embeds.buffer[here, :].astype(F32) + rows[half, local, :])
            gains += fold(grad * unit)
            shifts += fold(grad)
            value = norm_back(grad, unit, rate, gain) + get_tall(spread_first.at[half], c * CH, CH)
            high = value.astype(LOW)
            grad_embeds.buffer[here, :] = high
            lower[half, local, :] = (value - high.astype(F32)).astype(LOW)
        sums[half, 0:8, :] += gains
        sums[half, 8:16, :] += shifts
    collect(blocks - 1)
    grad_out[...] = dot_tn(mixed.whole()[...], dfirst.buffer[...].astype(LOW))
    grad_qkv[:, :512] = dot_tn(normed0.whole()[...], dquery.whole()[...])
    normed.whole()
    for k in range(4):
        lanes = slice(256 * k, 256 * k + 256)
        grad_qkv[:, 512 + 256 * k : 768 + 256 * k] = dot_tn(normed.buffer[...], dkeyval.buffer[:, lanes])
    sums[0] = sums[0] + sums[1]
    small[...] = jnp.zeros_like(small)
    small[0:8, :] = sums[0, 16:24, :]
    folded = (sums[0, 0:8, :], sums[0, 8:16, :], gain_ffn.whole()[...], shift_ffn.whole()[...], pool.whole()[...])
    for i, value in enumerate(folded):
        small[8 + i : 9 + i, :] = jnp.sum(value, axis=0, keepdims=True)
    up_row = jnp.sum(up.whole()[...], axis=0, keepdims=True)
    row = iota((16, 128), 0)
    for r in range(SHARDS):
        tile = small[:, 128 * (r // 8) : 128 * (r // 8) + 128]
        tile = jnp.where(row == 13, up_row[:, 128 * (r // 2) : 128 * (r // 2) + 128], tile)
        rows[0, 8 * r : 8 * r + 8, 0:128] = tile[0:8]
        rows[0, 8 * r : 8 * r + 8, 128:256] = tile[8:16]
    for k in range(SHARDS):
        half, place = (own, k) if k < 16 else (halves[0], k % 8) if k < 24 else (halves[k // 4 - 5], k % 4)
        at, near = block(shard_at(me, k), 16), block(shard_at(me, k), 8)
        half.buffer[place, :, :1536] = grad_qkv[at, :].astype(LOW)
        half.buffer[place, :, 1536:2048] = grad_out[at, :].astype(LOW)
        value = jnp.concatenate([rows[0, near, 0:128], rows[0, near, 128:256]])
        half.buffer[place, :, 2048:2176] = value.astype(LOW)
    for half in halves:
        half.send()
    own.send()


def on_device(
    embeds,
    piece_counts,
    group_ids,
    group_table,
    gain_attn,
    shift_attn,
    w_qkv,
    w_out,
    gain_ffn,
    shift_ffn,
    w_up,
    bias_up,
    w_down,
    bias_down,
    w_proj,
    cotangent,
):
    tuned = lax.axis_size("dp") == 32
    entries = embeds.shape[0]
    rows = entries * SLOTS
    flat = embeds.reshape(rows, 512)
    lane = jnp.arange(128, dtype=jnp.int32)
    slot = jnp.arange(SLOTS, dtype=jnp.int32)
    vectors = [gain_attn, shift_attn, gain_ffn, shift_ffn, bias_down]
    later = [embeds]
    if tuned:
        me = lax.axis_index("dp").astype(jnp.int32).reshape(1)
        parts = [(0, 0, w_qkv), (0, 1536, group_table), (13, 1536, bias_up[None, :])]
        parts += [(8 + i, 1536, vector[None, :]) for i, vector in enumerate(vectors)]
        shard = side_by_side(parts, (16, 1664))
        own = jnp.stack([shard, *spread(shard, LAYER[1], LAYER[2], LAYER[3])])
        third = side_by_side([(0, 0, w_down), (64, 0, w_out)], (80, 512))
        quad = [third, *spread(third, NEAR, FAR, ACROSS)]
        mine = [own, *spread(own, NEAR, FAR, ACROSS)]
        pieces = [mine + [send(part, CORE) for part in mine]]
        shard = side_by_side([(0, 0, w_proj), (16, 0, w_up)], (32, 2048))
        upper, lower = spread(shard, LAYER[2], LAYER[1])
        quad = jnp.stack([tie(third, own), *quad[1:]])
        own2 = jnp.stack([tie(shard, quad), lower, upper, send(tie(upper, own), LAYER[1])])
        pieces.append([own2, *spread(own2, NEAR, FAR)])
        lower, upper = spread(quad, LAYER[1], LAYER[2])
        upper = tie(upper, own2)
        pieces.append([quad, lower, upper, send(upper, LAYER[1])])
        near2 = tie(pieces[1][1], upper)
        pieces[1].append(send(near2, FAR))
        later = [tie(own2, near2)]
        group_ids, piece_counts = tie(group_ids, piece_counts, own, every=True)[:2]
    else:
        me = None

        def whole(shard, axis=0):
            return lax.all_gather(shard, "dp", axis=axis, tiled=True)

        def cut(full):
            return [full[4 * i : 4 * i + 4] for i in range(8)]

        gathered = whole(jnp.concatenate([group_table, jnp.stack(vectors)]), 1)
        gathered = jnp.transpose(gathered.reshape(13, SHARDS, 16), (1, 0, 2))
        small = jnp.concatenate(
            [
                jnp.pad(gathered, ((0, 0), (0, 0), (0, 112))),
                jnp.pad(whole(bias_up).reshape(SHARDS, 1, 64), ((0, 0), (0, 2), (0, 64))),
            ],
            axis=1,
        )
        pieces = [
            cut(
                jnp.concatenate(
                    [whole(w_qkv).reshape(SHARDS, 16, 1536), small], axis=2
                )
            ),
            cut(
                jnp.concatenate(
                    [whole(w_proj).reshape(SHARDS, 16, 2048), whole(w_up).reshape(SHARDS, 16, 2048)], axis=1
                )
            ),
            cut(
                jnp.concatenate([whole(w_down).reshape(SHARDS, 64, 512), whole(w_out).reshape(SHARDS, 16, 512)], axis=1)
            ),
        ]
    marks = jnp.where(
        lane[None, None, :] < 8,
        group_ids[:, None, None] == lane[None, None, :],
        slot[None, :, None] < piece_counts[:, None, None],
    )
    marks = marks.astype(LOW).reshape(rows, 128)
    steps = rows // RB // 2
    low, wide = LOW, F32
    (qkv_all, vec, upbias, base0, normed, normed0, query, keyval, probs, mixed) = call(
        attend_kernel, 15,
        me,
        pieces[0],
        [(marks, 1, None), (flat, steps, None)],
        [
            ((512, 1664), low, 1), ((16, 512), wide, 1), ((8, 2048), wide, 1), ((entries, 512), wide, 1),
            ((rows, 512), low, steps), ((entries, 512), low, 1), ((entries, 512), low, 1), ((rows, 1024), low, steps),
            ((rows, HEADS * EB), low, steps), ((entries, 512), low, 1),
        ],
        scratch=[
            ((32, 16, 128), wide), ((128, 512), wide), ((2, RB, 512), wide), ((2, 4 * RB, 128), wide),
            ((2, 4 * RB, 128), wide), ((entries, 512), wide),
        ],
        after=later,
    )
    if tuned:
        mixed, *came = tie(mixed, *pieces[1], *pieces[2], every=True)
        cores = [send(part, CORE) for part in came]
        pieces[1:] = [came[0:4] + cores[:4], came[4:8] + cores[4:]]
    (
        output, dfirst, dmixed, sum_up, sum_gain, sum_shift, sum_pool, own_pair, low_pair, high_pair, *both_down
    ) = call(
        ffn_kernel,
        12,
        me,
        [*pieces[1], *pieces[2]],
        [
            (cotangent, 1, None), (base0, 1, None), (mixed, 1, None), (vec, 1, None), (upbias, 1, None),
        ],
        [
            ((entries, 2048), low, 1), ((entries, 512), wide, 1), ((entries, 512), low, 1), ((8, 2048), wide, 1),
            ((8, 512), wide, 1), ((8, 512), wide, 1), ((8, 512), wide, 1),
        ],
        [
            ((512, 2048), low), ((512, 2048), low), ((2048, 512), low), ((512, 512), low), ((entries, 512), wide),
            ((entries, 512), low), ((entries, 2048), low), ((entries, 512), wide), ((entries, 2048), low),
            ((entries, 2048), wide), ((512, 2048), low), ((512, 2048), low), ((512, 2048), low),
        ],
        raw=[((16, 32, 2048), low), *[((8, 32, 2048), low)] * 2, *[((16, 16, 2048), low)] * 2],
    )
    if tuned:
        pair = Sum(own_pair, low_pair, high_pair)
        down = LayersFirst(*both_down)
    (dkeyval, dquery, query_part) = call(
        attend_back_kernel, 8,
        me,
        [],
        [
            (dmixed, 1, None), (query, 1, None), (probs, steps, None), (keyval, steps, None),
            (qkv_all, 1, (0, 512, 0, 512)),
        ],
        [((rows, 1024), low, steps), ((entries, 512), low, 1), ((entries, 512), wide, 1)],
    )
    part = own_pair
    if tuned:
        query_part, pair.high[0], down.core = tie(query_part, pair.high[0], down.core, every=True)
        part = pair.first()
        down.core = tie(down.core, part)
        part = down.first()
    (grad_embeds, own_last, *other_last) = call(
        input_back_kernel,
        18,
        me,
        [],
        [
            (vec, 1, None), (query_part, 1, None), (dfirst, 1, None), (marks, 1, None), (qkv_all, 1, (0, 512, 512, 1024)),
            (dkeyval, steps, None), (flat, steps, None), (sum_gain, 1, None), (sum_shift, 1, None), (sum_pool, 1, None),
            (sum_up, 1, None), (mixed, 1, None), (normed0, 1, None), (dquery, 1, None), (normed, 1, None),
        ],
        [((rows, 512), low, steps), ((16, 16, 2176), low, 1), ((8, 16, 2176), low, 1), *[((4, 16, 2176), low, 1)] * 2],
        [
            ((512, 1536), wide), ((512, 512), wide), ((128, 512), low), ((2, RB, 512), wide), ((2, RB, 512), wide),
            ((2, RB, 512), low), ((2, 4 * RB, 128), wide), ((2, 4 * RB, 128), wide), ((16, 512), wide),
            ((2, 144, 512), wide),
        ],
        after=[part],
    )
    if tuned:
        last = Sum(own_last, *other_last)
        pair.far, down.beside, *last.high = tie(pair.far, down.beside, *last.high, every=True)
        part = last.first()
        pair.far, down.beside = tie(pair.far, down.beside, part, every=True)[:2]
        part = pair.second()
        down.beside = tie(down.beside, part)
        part = down.second()
        last.far = tie(last.far, part)
        part = last.second()
        pair.near = tie(pair.near, part)
        part = pair.third()
        down.beyond = tie(down.beyond, part)
        part = down.third()
        last.near = tie(last.near, part)
        part = last.third()
        pair.beside, down.far = tie(pair.beside, down.far, part, every=True)[:2]
        part = pair.fourth()
        down.far = tie(down.far, part)
        part = down.fourth()
        last.beside = tie(last.beside, part)
        part = last.fourth()
        down.near = tie(down.near, part)
        sum_down = down.done()
        pair.beyond = tie(pair.beyond, sum_down)
        pair = pair.done()
        last.beyond = tie(last.beyond, pair)
        sum_qkv, sum_out, last_small = [
            widen(last.rest[:, at], last.beyond[:, at])
            for at in (slice(0, 1536), slice(1536, 2048), slice(2048, 2176))
        ]
        sum_proj, sum_up = pair[:16], pair[16:]
        sum_down = jnp.concatenate([sum_down[:, 512 * j : 512 * j + 512] for j in range(4)])
        me = lax.axis_index("dp")
        sums = lax.dynamic_slice(last_small, (0, 16 * (me % 8)), (13, 16))
        sum_upbias = lax.dynamic_slice(last_small, (13, 64 * (me % 2)), (1, 64))[0]
    else:

        def share(full):
            return lax.psum_scatter(full.reshape(-1, full.shape[-1]), "dp", scatter_dimension=0, tiled=True)

        pair_all = jnp.concatenate([own_pair, low_pair, high_pair]).astype(F32)
        down_all = jnp.concatenate(both_down).astype(F32)
        last_all = jnp.concatenate([own_last, *other_last]).astype(F32)
        sum_proj = share(pair_all[:, :16])
        sum_up = share(pair_all[:, 16:])
        sum_down = share(down_all.reshape(SHARDS, 16, 4, 512).transpose(0, 2, 1, 3))
        sum_qkv = share(last_all[:, :, :1536])
        sum_out = share(last_all[:, :, 1536:2048])
        small = last_all[:, :, 2048:]
        vectors = jnp.concatenate([small[8 * k, :13] for k in range(4)], axis=1)
        sums = lax.psum_scatter(vectors, "dp", scatter_dimension=1, tiled=True)
        upbias = jnp.concatenate([small[2 * k, 13] for k in range(16)])
        sum_upbias = lax.psum_scatter(upbias, "dp", scatter_dimension=0, tiled=True)
    return (
        output,
        grad_embeds.reshape(entries, SLOTS, 512),
        sums[:8],
        sums[8],
        sums[9],
        sum_qkv,
        sum_out,
        sums[10],
        sums[11],
        sum_up,
        sum_upbias,
        sum_down,
        sums[12],
        sum_proj,
    )


def solution(mesh):
    placed = (
        P("dp", None, None),
        P("dp"),
        P("dp"),
        P(None, "dp"),
        P("dp"),
        P("dp"),
        P("dp", None),
        P("dp", None),
        P("dp"),
        P("dp"),
        P("dp", None),
        P("dp"),
        P("dp", None),
        P("dp"),
        P("dp", None),
        P("dp", None),
    )
    return jax.shard_map(
        on_device,
        mesh=mesh,
        in_specs=placed,
        out_specs=(
            P("dp", None),
            P("dp", None, None),
            P(None, "dp"),
            P("dp"),
            P("dp"),
            P("dp", None),
            P("dp", None),
            P("dp"),
            P("dp"),
            P("dp", None),
            P("dp"),
            P("dp", None),
            P("dp"),
            P("dp", None),
        ),
        check_vma=False,
    )
```
